32 devices in a mesh: clip: 16 (over z, y, x), tm: 2 (over core).
Axes of the slice: x: 2, y: 2, z: 4, core: 2. Of those that a mesh axis runs over, the one named last changes fastest.
Arguments:
- audio_feats: bfloat16 [64, 512, 256], P('clip', 'tm'), may hold values from -6 to 6
- lip_feats: bfloat16 [64, 512, 256], P('clip', 'tm'), may hold values from -6 to 6
- lengths: int32 [64], P('clip'), may hold values from 256 to 512
- labels: int32 [64], P('clip'), may hold values from -15 to 15
- w_audio_conv: bfloat16 [3, 256, 512], replicated, may hold values from -0.21875 to 0.21875
- w_audio_proj: bfloat16 [512, 512], replicated, may hold values from -0.25 to 0.25
- w_lip_conv: bfloat16 [3, 256, 512], replicated, may hold values from -0.21875 to 0.21875
- w_lip_proj: bfloat16 [512, 512], replicated, may hold values from -0.25 to 0.25
Outputs:
- loss: float32 [], replicated
- grad_audio_conv: float32 [3, 256, 512], replicated
- grad_audio_proj: float32 [512, 512], replicated
- grad_lip_conv: float32 [3, 256, 512], replicated
- grad_lip_proj: float32 [512, 512], replicated
The draws below stay inside these ranges and needn't reach their ends.
All inputs are finite; a program needn't handle non-finite values.
Results may differ from the reference program's by a relative error of at most 0.0075.
Values may be sent and summed in bfloat16 or wider, within the bound.
No kernel may reach another device: no remote copies, remote signals or barrier semaphores. Data moves between devices by JAX's collectives and lax.ppermute only.
A program may use at most 64 MiB of HBM per device.

```python
import jax
import jax.numpy as jnp
from jax import lax

C_IN = 256
E = 512
SPAN = 15
CLIPS = 64
FRAMES = 512


def set_ends(array, stream_key, smallest, high):
    spot = [jax.random.randint(jax.random.fold_in(stream_key, axis), (), 0, length) for axis, length in enumerate(array.shape)]
    longest = array.shape.index(max(array.shape))
    next_to = spot[:longest] + [(spot[longest] + 1) % array.shape[longest]] + spot[longest + 1:]
    return array.at[tuple(spot)].set(smallest).at[tuple(next_to)].set(high)


def steps_of(stream_key, dims, split, smallest, top_value):
    level, own = 1.0, jax.random.fold_in(stream_key, 6)
    for dim, shards_of in split:
        heights = jnp.exp(jax.random.uniform(jax.random.fold_in(own, dim), (shards_of,), jnp.float32, smallest / len(split), top_value / len(split)))
        level = level * jnp.repeat(heights, dims[dim] // shards_of).reshape([-1 if axis == dim else 1 for axis in range(len(dims))])
    return level


def bell_draw(stream_key, dims, spread, most, cuts=(), kind=jnp.bfloat16):
    values = spread * jax.random.normal(stream_key, dims, jnp.float32)
    if cuts:
        values = values * steps_of(stream_key, dims, cuts, -0.22, 0.18)
    return jnp.clip(values, -most, most).astype(kind)


def setup_inputs(seed: int = 0) -> dict:
    splits = jax.random.split(jax.random.key(seed), 9)
    return {
        "audio_feats": bell_draw(splits[0], (CLIPS, FRAMES, C_IN), 1.0, 6.0, ((0, 16), (1, 2))),
        "lip_feats": bell_draw(splits[1], (CLIPS, FRAMES, C_IN), 1.0, 6.0, ((0, 16), (1, 2))),
        "lengths": set_ends(jax.random.randint(splits[2], (CLIPS,), FRAMES // 2, FRAMES + 1), jax.random.fold_in(splits[2], 1), FRAMES // 2, FRAMES).astype(jnp.int32),
        "labels": set_ends(jax.random.randint(splits[3], (CLIPS,), 0 - SPAN, SPAN + 1), jax.random.fold_in(splits[3], 1), 0 - SPAN, SPAN).astype(jnp.int32),
        "w_audio_conv": bell_draw(splits[4], (3, C_IN, E), (3 * C_IN) ** -0.5, 0.21875),
        "w_audio_proj": bell_draw(splits[5], (E, E), E ** -0.5, 0.25),
        "w_lip_conv": bell_draw(splits[6], (3, C_IN, E), (3 * C_IN) ** -0.5, 0.21875),
        "w_lip_proj": bell_draw(splits[7], (E, E), E ** -0.5, 0.25),
    }


logit_sharpening_divisor = 10.0
loss_scale = 1024.0
epsilon = 1e-06

def silu_slope(values):
    sigma = jax.nn.sigmoid(values)
    return sigma * (1.0 + values * (1.0 - sigma))

def encoder(inputs, w_conv, w_proj):
    frame_total = inputs.shape[0]
    padded = jnp.pad(inputs, ((1, 1), (0, 0)))
    columns = jnp.concatenate([padded[0:frame_total], padded[1:frame_total + 1], padded[2:frame_total + 2]], axis=1)
    before = jnp.dot(columns, w_conv.reshape(3 * C_IN, E), preferred_element_type=jnp.float32)
    hidden = jax.nn.silu(before).astype(jnp.bfloat16)
    embedded = jnp.dot(hidden, w_proj, preferred_element_type=jnp.float32).astype(jnp.bfloat16)
    return (columns, before, hidden, embedded)

def inverse_norm(embedded):
    values = embedded.astype(jnp.float32)
    return lax.rsqrt(lax.optimization_barrier(jnp.sum(values * values, axis=-1)) + epsilon)

def encoder_grads(columns, before, hidden, grad_emb, w_proj):
    grad_proj = jnp.dot(hidden.T, grad_emb, preferred_element_type=jnp.float32)
    grad_hidden = jnp.dot(grad_emb, w_proj.T, preferred_element_type=jnp.float32)
    grad_before = (grad_hidden * silu_slope(before)).astype(jnp.bfloat16)
    grad_conv = jnp.dot(columns.T, grad_before, preferred_element_type=jnp.float32).reshape(3, C_IN, E)
    return (grad_conv, grad_proj)

def reference(audio_feats, lip_feats, lengths, labels, w_audio_conv, w_audio_proj, w_lip_conv, w_lip_proj):
    offsets = 2 * SPAN + 1
    count = jnp.sum((lengths - jnp.abs(labels)).astype(jnp.float32))
    shifts = jnp.arange(offsets, dtype=jnp.int32) - SPAN
    frame_ids = jnp.arange(FRAMES, dtype=jnp.int32)

    def per_clip(carry, items):
        audio, lip, length, label = items
        cols_a, pre_a, hid_a, emb_a = encoder(audio, w_audio_conv, w_audio_proj)
        cols_v, pre_v, hid_v, emb_v = encoder(lip, w_lip_conv, w_lip_proj)
        emb_a_pad = jnp.pad(emb_a, ((SPAN, SPAN), (0, 0)))
        inv_a_pad = inverse_norm(emb_a_pad)
        reciprocal_visual_length = inverse_norm(emb_v)
        audio_vals = emb_a_pad.astype(jnp.float32)
        lip_vals = emb_v.astype(jnp.float32)
        lagged_inner_terms = jnp.stack([lax.optimization_barrier(jnp.sum(lip_vals * audio_vals[offset:offset + FRAMES], axis=-1)) for offset in range(offsets)], axis=1)
        reciprocal_lag_strip = jnp.stack([inv_a_pad[offset:offset + FRAMES] for offset in range(offsets)], axis=1)
        positions = frame_ids[:, None] + shifts[None, :]
        inside = frame_ids < length
        valid = inside[:, None] & (positions >= 0) & (positions < length)
        counted = inside & (frame_ids + label >= 0) & (frame_ids + label < length)
        correct_lag_position = (shifts == label).astype(jnp.float32)
        lag_similarity_logits = logit_sharpening_divisor * lagged_inner_terms * reciprocal_visual_length[:, None] * reciprocal_lag_strip
        exponentiated_logits = jnp.where(valid, jnp.exp(lag_similarity_logits), 0.0)
        partition_sums = jnp.where(inside, lax.optimization_barrier(jnp.sum(exponentiated_logits, axis=1)), 1.0)
        picked = lax.optimization_barrier(jnp.sum(lag_similarity_logits * correct_lag_position[None, :], axis=1))
        frame_loss = jnp.where(counted, jnp.log(partition_sums) - picked, 0.0)
        normalized_probabilities = jnp.where(counted, loss_scale / count, 0.0)
        logit_derivative = logit_sharpening_divisor * normalized_probabilities[:, None] * (exponentiated_logits / partition_sums[:, None] - correct_lag_position[None, :])
        grad_dots = (logit_derivative * reciprocal_visual_length[:, None] * reciprocal_lag_strip).astype(jnp.bfloat16)
        grad_inv_v = lax.optimization_barrier(jnp.sum(logit_derivative * lagged_inner_terms * reciprocal_lag_strip, axis=1))
        audio_term = logit_derivative * lagged_inner_terms * reciprocal_visual_length[:, None]
        dot_vals = grad_dots.astype(jnp.float32)
        lip_sum = jnp.zeros((FRAMES, E), jnp.float32)
        audio_sum = jnp.zeros((FRAMES + 2 * SPAN, E), jnp.float32)
        inv_sum = jnp.zeros((FRAMES + 2 * SPAN,), jnp.float32)
        for offset in range(offsets):
            lip_sum = lip_sum + dot_vals[:, offset, None] * audio_vals[offset:offset + FRAMES]
            audio_sum = audio_sum.at[offset:offset + FRAMES].add(dot_vals[:, offset, None] * lip_vals)
            inv_sum = inv_sum.at[offset:offset + FRAMES].add(audio_term[:, offset])
        grad_lip = (lip_sum - (reciprocal_visual_length * reciprocal_visual_length * reciprocal_visual_length * grad_inv_v)[:, None] * lip_vals).astype(jnp.bfloat16)
        audio_sum = audio_sum - (inv_a_pad * inv_a_pad * inv_a_pad * inv_sum)[:, None] * audio_vals
        grad_audio = audio_sum[SPAN:SPAN + FRAMES].astype(jnp.bfloat16)
        gca, gpa = encoder_grads(cols_a, pre_a, hid_a, grad_audio, w_audio_proj)
        gcv, gpv = encoder_grads(cols_v, pre_v, hid_v, grad_lip, w_lip_proj)
        acc_ac, acc_ap, acc_vc, acc_vp, acc_loss = carry
        return ((acc_ac + gca, acc_ap + gpa, acc_vc + gcv, acc_vp + gpv, acc_loss + jnp.sum(frame_loss)), None)
    start = (jnp.zeros((3, C_IN, E), jnp.float32), jnp.zeros((E, E), jnp.float32), jnp.zeros((3, C_IN, E), jnp.float32), jnp.zeros((E, E), jnp.float32), jnp.zeros((), jnp.float32))
    totals_out, unused = lax.scan(per_clip, start, (audio_feats, lip_feats, lengths, labels))
    grad_ac, grad_ap, grad_vc, grad_vp, loss_sum = totals_out
    return (loss_sum / count, grad_ac, grad_ap, grad_vc, grad_vp)
```

```python
import functools

import jax
import jax.numpy as jnp
from jax import lax
from jax.experimental import pallas as pl
from jax.experimental.pallas import tpu as pltpu
from jax.sharding import PartitionSpec as P

SPAN = 15
PAD = 16
TILE = 128
WIN = TILE + 2 * PAD
HALO = 64
LANES = 128
DIGITS = 48
FRACTION = 20

logit_sharpening_divisor = 10.0
loss_scale = 1024.0
epsilon = 1e-06

BF16 = jnp.bfloat16
F32 = jnp.float32


def dot(a, b, dims):
    return lax.dot_general(a, b, (dims, ((), ())), preferred_element_type=F32)


NN = ((1,), (0,))
NT = ((1,), (1,))
TN = ((0,), (0,))


def digit_weights(shape):
    lane = lax.broadcasted_iota(jnp.int32, shape, len(shape) - 1)
    return lane, jnp.exp2((lane - FRACTION).astype(F32))


def digits_of(value):
    lane, weight = digit_weights((1, LANES))
    size = jnp.abs(value)
    bits = jnp.floor(size / weight) - 2.0 * jnp.floor(size / (2.0 * weight))
    return jnp.where(lane < DIGITS, jnp.where(value < 0, -bits, bits), 0.0)


def value_of(digits):
    lane, weight = digit_weights(digits.shape)
    return jnp.sum(jnp.where(lane < DIGITS, digits * weight, 0.0))


def forward(feats, m, w_conv, w_proj, cols, slope, hid, clips, frames, block, put):
    chan = feats.shape[-1]
    for c in range(clips):
        x = feats[m, c].astype(F32)
        row = lax.broadcasted_iota(jnp.int32, x.shape, 0)
        base = c * frames
        cols[m, base : base + frames, 0:chan] = jnp.where(row == 0, 0.0, pltpu.roll(x, 1, 0)).astype(BF16)
        cols[m, base : base + frames, chan : 2 * chan] = feats[m, c]
        cols[m, base : base + frames, 2 * chan : 3 * chan] = jnp.where(
            row == frames - 1, 0.0, pltpu.roll(x, frames - 1, 0)
        ).astype(BF16)

    def step(i, _):
        rows = pl.ds(pl.multiple_of(i * block, block), block)
        pre = dot(cols[m, rows, :], w_conv[...], NN)
        sigma = jax.nn.sigmoid(pre)
        hidden = (pre * sigma).astype(BF16)
        hid[m, rows, :] = hidden
        slope[m, rows, :] = sigma * (1.0 + pre * (1.0 - sigma))
        emb = dot(hidden, w_proj[...], NN).astype(BF16)
        values = emb.astype(F32)
        inv = lax.rsqrt(jnp.sum(values * values, axis=1, keepdims=True) + epsilon)
        put(i, emb, jnp.broadcast_to(inv, (block, LANES)))
        return 0

    lax.fori_loop(0, clips * frames // block, step, 0)


def backward(m, w_proj, cols, slope, hid, gemb, gpre, total, block, rows_total):
    def step(i, _):
        rows = pl.ds(pl.multiple_of(i * block, block), block)
        grad = dot(gemb[m, rows, :], w_proj[...], NT) * slope[m, rows, :]
        gpre[m, rows, :] = grad.astype(BF16)
        return 0

    lax.fori_loop(0, rows_total // block, step, 0)
    conv_rows = cols.shape[-1]

    def conv_step(i, _):
        at = pl.multiple_of(i * 256, 256)
        total[pl.ds(at, 256), :] = dot(cols[m, :, pl.ds(at, 256)], gpre[m], TN)
        return 0

    lax.fori_loop(0, conv_rows // 256, conv_step, 0)

    def proj_step(i, _):
        at = pl.multiple_of(i * 256, 256)
        total[pl.ds(conv_rows + at, 256), :] = dot(hid[m, :, pl.ds(at, 256)], gemb[m], TN)
        return 0

    lax.fori_loop(0, hid.shape[-1] // 256, proj_step, 0)


def hand_over(total, keep, send, m, half):
    width = total.shape[1] // 2
    for j in range(width // LANES):
        mine = pl.ds(pl.multiple_of(half * width + j * LANES, LANES), LANES)
        other = pl.ds(pl.multiple_of((1 - half) * width + j * LANES, LANES), LANES)
        keep[m, j] = total[:, mine]
        send[m, j] = total[:, other].astype(BF16)


def kernel(
    frames, clips, halo, lengths, labels, feats, wac, wap, wvc, wvp, keep, send, stats,
    cols, slope, hid, gemb, gpre, total, emb_a, emb_v, inv_a, inv_v, gacc, giacc,
):
    me = lax.axis_index("tm")
    half = lax.rem(me, 2)
    rows_total = clips * frames
    start = me * (frames - 2 * halo) - halo if halo else 0
    first_clip = 0 if halo else me * clips
    block = 256 if frames % 256 == 0 else TILE
    per_clip = frames // block

    for c in range(clips):
        for lo in (0, PAD + frames):
            emb_a[c, lo : lo + PAD, :] = jnp.zeros((PAD, emb_a.shape[2]), BF16)
            inv_a[c, lo : lo + PAD, :] = jnp.zeros((PAD, LANES), F32)

    def put_a(i, emb, inv):
        c = i // per_clip
        at = pl.multiple_of(PAD + lax.rem(i, per_clip) * block, PAD)
        emb_a[c, pl.ds(at, block), :] = emb
        inv_a[c, pl.ds(at, block), :] = inv

    def put_v(i, emb, inv):
        at = pl.multiple_of(i * block, block)
        emb_v[pl.ds(at, block), :] = emb
        inv_v[pl.ds(at, block), :] = inv

    forward(feats, 1, wvc, wvp, cols, slope, hid, clips, frames, block, put_v)
    forward(feats, 0, wac, wap, cols, slope, hid, clips, frames, block, put_a)

    gacc[...] = jnp.zeros(gacc.shape, F32)
    giacc[...] = jnp.zeros(giacc.shape, F32)
    tiles = frames // TILE
    row = lax.broadcasted_iota(jnp.int32, (TILE, WIN), 0)
    col = lax.broadcasted_iota(jnp.int32, (TILE, WIN), 1)
    shift = col - row - PAD
    in_band = (shift >= -SPAN) & (shift <= SPAN)
    row_1 = lax.broadcasted_iota(jnp.int32, (TILE, 1), 0)

    def tile_step(i, loss):
        c = i // tiles
        first = pl.multiple_of(lax.rem(i, tiles) * TILE, TILE)
        length = lengths[first_clip + c]
        label = labels[first_clip + c]
        here = pl.ds(pl.multiple_of(i * TILE, TILE), TILE)
        window = pl.ds(first, WIN)
        ev = emb_v[here, :]
        wa = emb_a[c, window, :]
        iv = inv_v[here, 0:1]
        ia = inv_a[c, window, :].T
        dots = dot(ev, wa, NT)
        scores = logit_sharpening_divisor * dots * iv * ia
        t = start + first + row_1
        u = start + first - PAD + col
        inside = t < length
        valid = in_band & inside & (u >= 0) & (u < length)
        target = t + label
        counted = inside & (target >= 0) & (target < length)
        hit = shift == label
        weights = jnp.where(valid, jnp.exp(scores), 0.0)
        sums = jnp.where(inside, jnp.sum(weights, axis=1, keepdims=True), 1.0)
        picked = jnp.sum(jnp.where(hit, scores, 0.0), axis=1, keepdims=True)
        own = (first + row_1 >= halo) & (first + row_1 < frames - halo)
        loss = loss + jnp.sum(jnp.where(counted & own, jnp.log(sums) - picked, 0.0))
        scale = jnp.where(counted, logit_sharpening_divisor * loss_scale, 0.0)
        grad = scale * (weights / sums - jnp.where(hit, 1.0, 0.0))
        gd = (grad * iv * ia).astype(BF16)
        by_dots = grad * dots
        giv = jnp.sum(by_dots * ia, axis=1, keepdims=True)
        gia = jnp.sum((by_dots * iv).T, axis=1, keepdims=True)
        glip = dot(gd, wa, NN) - (iv * iv * iv * giv) * ev.astype(F32)
        gemb[1, here, :] = jnp.where(own, glip, 0.0).astype(BF16)
        gacc[c, window, :] += dot(gd, ev, TN)
        giacc[c, window, :] += jnp.broadcast_to(gia, (WIN, LANES))
        return loss

    loss = lax.fori_loop(0, clips * tiles, tile_step, jnp.zeros((), F32))

    def audio_step(i, _):
        c = i // per_clip
        at = pl.ds(pl.multiple_of(PAD + lax.rem(i, per_clip) * block, PAD), block)
        inv = inv_a[c, at, 0:1]
        grad = gacc[c, at, :] - (inv * inv * inv * giacc[c, at, 0:1]) * emb_a[c, at, :].astype(F32)
        if halo:
            at_row = lax.rem(i, per_clip) * block + lax.broadcasted_iota(jnp.int32, (block, 1), 0)
            grad = jnp.where((at_row >= halo) & (at_row < frames - halo), grad, 0.0)
        gemb[0, pl.ds(pl.multiple_of(i * block, block), block), :] = grad.astype(BF16)
        return 0

    lax.fori_loop(0, rows_total // block, audio_step, 0)

    count = jnp.zeros((), F32)
    for c in range(clips):
        count = count + (lengths[first_clip + c] - jnp.abs(labels[first_clip + c])).astype(F32)
    if halo:
        count = jnp.where(me == 0, count, 0.0)
    stats[...] = jnp.zeros(stats.shape, BF16)
    stats[0:1, :] = digits_of(loss).astype(BF16)
    stats[16:17, :] = digits_of(count).astype(BF16)

    backward(1, wvp, cols, slope, hid, gemb, gpre, total, block, rows_total)
    hand_over(total, keep, send, 1, half)
    backward(0, wap, cols, slope, hid, gemb, gpre, total, block, rows_total)
    hand_over(total, keep, send, 0, half)


def local_grads(halo, lengths, labels, feats, wac, wap, wvc, wvp):
    _, clips, frames, chan = feats.shape
    width = wap.shape[0]
    rows = clips * frames
    taps = wac.shape[0]
    grad_rows = taps * chan + width
    wac = wac.reshape(taps * chan, width)
    wvc = wvc.reshape(taps * chan, width)
    blocks = width // 2 // LANES
    smem = pl.BlockSpec(memory_space=pltpu.SMEM)
    vmem = pl.BlockSpec(memory_space=pltpu.VMEM)
    return pl.pallas_call(
        functools.partial(kernel, frames, clips, halo),
        out_shape=(
            jax.ShapeDtypeStruct((2, blocks, grad_rows, LANES), F32),
            jax.ShapeDtypeStruct((2, blocks, grad_rows, LANES), BF16),
            jax.ShapeDtypeStruct((32, LANES), BF16),
        ),
        in_specs=[smem, smem] + [vmem] * 5,
        out_specs=(vmem, vmem, vmem),
        scratch_shapes=[
            pltpu.VMEM((2, rows, taps * chan), BF16),
            pltpu.VMEM((2, rows, width), F32),
            pltpu.VMEM((2, rows, width), BF16),
            pltpu.VMEM((2, rows, width), BF16),
            pltpu.VMEM((2, rows, width), BF16),
            pltpu.VMEM((grad_rows, width), F32),
            pltpu.VMEM((clips, frames + 2 * PAD, width), BF16),
            pltpu.VMEM((rows, width), BF16),
            pltpu.VMEM((clips, frames + 2 * PAD, LANES), F32),
            pltpu.VMEM((rows, LANES), F32),
            pltpu.VMEM((clips, frames + 2 * PAD, width), F32),
            pltpu.VMEM((clips, frames + 2 * PAD, LANES), F32),
        ],
        compiler_params=pltpu.CompilerParams(vmem_limit_bytes=60 * 1024 * 1024),
    )(lengths, labels, feats, wac, wap, wvc, wvp)


def swap(value, axis, bit):
    return lax.ppermute(value, axis, [(i, i ^ bit) for i in range(lax.axis_size(axis))])


def pick(value, index):
    return lax.dynamic_index_in_dim(value, index, 0, keepdims=False)


def halve(value, axis, bit, tile=None):
    me = (lax.axis_index(axis) // bit) % 2
    parts = value.reshape(2, -1, LANES)
    out = pick(parts, 1 - me).astype(BF16)
    if tile is not None:
        out = jnp.concatenate([out, tile])
    got = swap(out, axis, bit)
    rows = parts.shape[1]
    mine = pick(parts, me).astype(F32) + got[:rows].astype(F32)
    return mine if tile is None else (mine, (tile.astype(F32) + got[rows:].astype(F32)).astype(BF16))


def double(value, axis, bit):
    me = (lax.axis_index(axis) // bit) % 2
    got = swap(value, axis, bit)
    return jnp.stack([jnp.where(me == 0, value, got), jnp.where(me == 0, got, value)]).reshape(-1, LANES)


def quarter(parts, axis, bit, tile):
    me = (lax.axis_index(axis) // bit) % 4
    rows = parts.shape[1]
    mine = pick(parts, me).astype(F32)
    whole = tile.astype(F32)
    for k in (1, 2, 3):
        got = swap(jnp.concatenate([pick(parts, me ^ k).astype(BF16), tile]), axis, k * bit).astype(F32)
        mine = mine + got[:rows]
        whole = whole + got[rows:]
    return mine, whole


def quadruple(value, axis, bit):
    me = (lax.axis_index(axis) // bit) % 4
    got = [value] + [swap(value, axis, k * bit) for k in (1, 2, 3)]
    out = []
    for j in range(4):
        k = me ^ j
        out.append(jnp.where(k == 0, got[0], jnp.where(k == 1, got[1], jnp.where(k == 2, got[2], got[3]))))
    return jnp.stack(out)


def bits_of(axis):
    size, bits = lax.axis_size(axis), []
    bit = 1
    while bit < size:
        bits.append(bit)
        bit *= 2
    return bits


def reduce_all(keep, send, stats):
    shape = keep.shape
    tm_bits, clip_bits = bits_of("tm"), bits_of("clip")
    got = swap(jnp.concatenate([send.reshape(-1, LANES), stats]), "tm", 1)
    rows = shape[0] * shape[1] * shape[2]
    total = keep.reshape(rows, LANES) + got[:rows].astype(F32)
    tile = (stats.astype(F32) + got[rows:].astype(F32)).astype(BF16)
    first, second = total.reshape(2, -1, LANES)
    for bit in tm_bits[1:]:
        first, tile = halve(first, "tm", bit, tile)
        second = halve(second, "tm", bit)
    singles, last = clip_bits[:-2], clip_bits[-2]
    order_1 = singles
    order_2 = singles[1::-1] + singles[2:]
    for bit_1, bit_2 in zip(order_1, order_2):
        first, tile = halve(first, "clip", bit_1, tile)
        second = halve(second, "clip", bit_2)
    parts = jnp.concatenate([first.reshape(4, -1, LANES), second.reshape(4, -1, LANES)], axis=1)
    mine, tile = quarter(parts, "clip", last, tile)
    parts = quadruple(mine.astype(BF16), "clip", last)
    n = parts.shape[1] // 2
    first, second = parts[:, :n].reshape(-1, LANES), parts[:, n:].reshape(-1, LANES)
    for bit_1, bit_2 in zip(order_1[::-1], order_2[::-1]):
        first = double(first, "clip", bit_1)
        second = double(second, "clip", bit_2)
    for bit in tm_bits[:0:-1]:
        first = double(first, "tm", bit)
        second = double(second, "tm", bit)
    whole = double(jnp.concatenate([first, second]), "tm", 1)
    halves = whole.reshape(2, shape[0], shape[1], shape[2], LANES)
    return halves, tile


def shards(
    audio_feats, lip_feats, lengths, labels, w_audio_conv, w_audio_proj, w_lip_conv, w_lip_proj
):
    both = jnp.stack([audio_feats, lip_feats])
    peers = lax.axis_size("tm")
    halo = 0
    if peers == 2 and both.shape[1] % 2 == 0:
        me = lax.axis_index("tm")
        parts = both.reshape(2, 2, both.shape[1] // 2, *both.shape[2:])
        mine = lax.dynamic_index_in_dim(parts, me, 1, keepdims=False)
        got = swap(lax.dynamic_index_in_dim(parts, 1 - me, 1, keepdims=False), "tm", 1)
        feats = jnp.concatenate(
            [jnp.where(me == 0, mine, got), jnp.where(me == 0, got, mine)], axis=2
        )
    else:
        halo = HALO
        after = [(i, i + 1) for i in range(peers - 1)]
        before = [(i + 1, i) for i in range(peers - 1)]
        feats = jnp.concatenate(
            [
                lax.ppermute(both[:, :, -HALO:], "tm", after),
                both,
                lax.ppermute(both[:, :, :HALO], "tm", before),
            ],
            axis=2,
        )
    keep, send, stats = local_grads(
        halo, lengths, labels, feats, w_audio_conv, w_audio_proj, w_lip_conv, w_lip_proj
    )
    halves, tile = reduce_all(keep, send, stats)
    loss_sum, count = value_of(tile[0:1].astype(F32)), value_of(tile[16:17].astype(F32))
    scale = 1.0 / count
    taps, chan, width = w_audio_conv.shape
    full = halves.transpose(1, 3, 0, 2, 4).reshape(2, -1, width).astype(F32) * scale
    conv = full[:, : taps * chan].reshape(2, taps, chan, width)
    proj = full[:, taps * chan :]
    return (loss_sum * scale, conv[0], proj[0], conv[1], proj[1])


def solution(mesh):
    placed = (
        P("clip", "tm", None),
        P("clip", "tm", None),
        P("clip"),
        P("clip"),
        P(),
        P(),
        P(),
        P(),
    )
    return jax.shard_map(
        shards, mesh=mesh, in_specs=placed, out_specs=(P(), P(), P(), P(), P()), check_vma=False
    )
```

```python
import functools

import jax
import jax.numpy as jnp
from jax import lax
from jax.experimental import pallas as pl
from jax.experimental.pallas import tpu as pltpu
from jax.sharding import PartitionSpec as P

SPAN = 15
PAD = 16
TILE = 128
WIN = TILE + 2 * PAD
HALO = 64
LANES = 128
DIGITS = 48
FRACTION = 20

logit_sharpening_divisor = 10.0
loss_scale = 1024.0
epsilon = 1e-06

BF16 = jnp.bfloat16
F32 = jnp.float32


def dot(a, b, dims):
    return lax.dot_general(a, b, (dims, ((), ())), preferred_element_type=F32)


NN = ((1,), (0,))
NT = ((1,), (1,))
TN = ((0,), (0,))


def digit_weights(shape):
    lane = lax.broadcasted_iota(jnp.int32, shape, len(shape) - 1)
    return lane, jnp.exp2((lane - FRACTION).astype(F32))


def digits_of(value):
    lane, weight = digit_weights((1, LANES))
    size = jnp.abs(value)
    bits = jnp.floor(size / weight) - 2.0 * jnp.floor(size / (2.0 * weight))
    return jnp.where(lane < DIGITS, jnp.where(value < 0, -bits, bits), 0.0)


def value_of(digits):
    lane, weight = digit_weights(digits.shape)
    return jnp.sum(jnp.where(lane < DIGITS, digits * weight, 0.0))


def forward(feats, m, w_conv, w_proj, cols, slope, hid, clips, frames, block, put):
    chan = feats.shape[-1]
    for c in range(clips):
        x = feats[m, c].astype(F32)
        row = lax.broadcasted_iota(jnp.int32, x.shape, 0)
        base = c * frames
        cols[m, base : base + frames, 0:chan] = jnp.where(row == 0, 0.0, pltpu.roll(x, 1, 0)).astype(BF16)
        cols[m, base : base + frames, chan : 2 * chan] = feats[m, c]
        cols[m, base : base + frames, 2 * chan : 3 * chan] = jnp.where(
            row == frames - 1, 0.0, pltpu.roll(x, frames - 1, 0)
        ).astype(BF16)

    def step(i, _):
        rows = pl.ds(pl.multiple_of(i * block, block), block)
        pre = dot(cols[m, rows, :], w_conv[...], NN)
        sigma = 0.5 * jnp.tanh(0.5 * pre) + 0.5
        hidden = (pre * sigma).astype(BF16)
        hid[m, rows, :] = hidden
        slope[m, rows, :] = sigma * (1.0 + pre * (1.0 - sigma))
        emb = dot(hidden, w_proj[...], NN).astype(BF16)
        values = emb.astype(F32)
        inv = lax.rsqrt(jnp.sum(values * values, axis=1, keepdims=True) + epsilon)
        put(i, emb, jnp.broadcast_to(inv, (block, LANES)))
        return 0

    lax.fori_loop(0, clips * frames // block, step, 0, unroll=True)


def backward(m, w_proj, cols, slope, hid, gemb, gpre, total, block, rows_total):
    def step(i, _):
        rows = pl.ds(pl.multiple_of(i * block, block), block)
        grad = dot(gemb[m, rows, :], w_proj[...], NT) * slope[m, rows, :]
        gpre[m, rows, :] = grad.astype(BF16)
        return 0

    lax.fori_loop(0, rows_total // block, step, 0, unroll=True)
    conv_rows = cols.shape[-1]

    def conv_step(i, _):
        at = pl.multiple_of(i * 256, 256)
        total[pl.ds(at, 256), :] = dot(cols[m, :, pl.ds(at, 256)], gpre[m], TN)
        return 0

    lax.fori_loop(0, conv_rows // 256, conv_step, 0)

    def proj_step(i, _):
        at = pl.multiple_of(i * 256, 256)
        total[pl.ds(conv_rows + at, 256), :] = dot(hid[m, :, pl.ds(at, 256)], gemb[m], TN)
        return 0

    lax.fori_loop(0, hid.shape[-1] // 256, proj_step, 0)


def hand_over(total, keep, send, m, half):
    width = total.shape[1] // 2
    for j in range(width // LANES):
        mine = pl.ds(pl.multiple_of(half * width + j * LANES, LANES), LANES)
        other = pl.ds(pl.multiple_of((1 - half) * width + j * LANES, LANES), LANES)
        at = (m * (width // LANES) + j) * total.shape[0]
        keep[at : at + total.shape[0], :] = total[:, mine]
        send[at : at + total.shape[0], :] = total[:, other].astype(BF16)


def kernel(
    frames, clips, halo, lengths, labels, feats, wac, wap, wvc, wvp, keep, send,
    cols, slope, hid, gemb, gpre, total, emb_a, emb_v, inv_a, inv_v, gacc, giacc,
):
    me = lax.axis_index("tm")
    half = lax.rem(me, 2)
    rows_total = clips * frames
    start = me * (frames - 2 * halo) - halo if halo else 0
    first_clip = 0 if halo else me * clips
    block = 256 if frames % 256 == 0 else TILE
    per_clip = frames // block

    for c in range(clips):
        for lo in (0, PAD + frames):
            emb_a[c, lo : lo + PAD, :] = jnp.zeros((PAD, emb_a.shape[2]), BF16)
            inv_a[c, lo : lo + PAD, :] = jnp.zeros((PAD, LANES), F32)

    def put_a(i, emb, inv):
        c = i // per_clip
        at = pl.multiple_of(PAD + lax.rem(i, per_clip) * block, PAD)
        emb_a[c, pl.ds(at, block), :] = emb
        inv_a[c, pl.ds(at, block), :] = inv

    def put_v(i, emb, inv):
        at = pl.multiple_of(i * block, block)
        emb_v[pl.ds(at, block), :] = emb
        inv_v[pl.ds(at, block), :] = inv

    forward(feats, 1, wvc, wvp, cols, slope, hid, clips, frames, block, put_v)
    forward(feats, 0, wac, wap, cols, slope, hid, clips, frames, block, put_a)

    gacc[...] = jnp.zeros(gacc.shape, F32)
    giacc[...] = jnp.zeros(giacc.shape, F32)
    tiles = frames // TILE
    row = lax.broadcasted_iota(jnp.int32, (TILE, WIN), 0)
    col = lax.broadcasted_iota(jnp.int32, (TILE, WIN), 1)
    shift = col - row - PAD
    in_band = (shift >= -SPAN) & (shift <= SPAN)
    row_1 = lax.broadcasted_iota(jnp.int32, (TILE, 1), 0)

    def tile_step(i, loss):
        c = i // tiles
        first = pl.multiple_of(lax.rem(i, tiles) * TILE, TILE)
        length = lengths[first_clip + c]
        label = labels[first_clip + c]
        here = pl.ds(pl.multiple_of(i * TILE, TILE), TILE)
        window = pl.ds(first, WIN)
        ev = emb_v[here, :]
        wa = emb_a[c, window, :]
        iv = inv_v[here, 0:1]
        ia = inv_a[c, window, :].T
        dots = dot(ev, wa, NT)
        scores = logit_sharpening_divisor * dots * iv * ia
        t = start + first + row_1
        u = start + first - PAD + col
        inside = t < length
        valid = in_band & inside & (u >= 0) & (u < length)
        target = t + label
        counted = inside & (target >= 0) & (target < length)
        hit = shift == label
        weights = jnp.where(valid, jnp.exp(scores), 0.0)
        sums = jnp.where(inside, jnp.sum(weights, axis=1, keepdims=True), 1.0)
        picked = jnp.sum(jnp.where(hit, scores, 0.0), axis=1, keepdims=True)
        own = (first + row_1 >= halo) & (first + row_1 < frames - halo)
        loss = loss + jnp.sum(jnp.where(counted & own, jnp.log(sums) - picked, 0.0))
        scale = jnp.where(counted, logit_sharpening_divisor * loss_scale, 0.0)
        grad = scale * (weights / sums - jnp.where(hit, 1.0, 0.0))
        gd = (grad * iv * ia).astype(BF16)
        by_dots = grad * dots
        giv = jnp.sum(by_dots * ia, axis=1, keepdims=True)
        gia = jnp.sum((by_dots * iv).T, axis=1, keepdims=True)
        glip = dot(gd, wa, NN) - (iv * iv * iv * giv) * ev.astype(F32)
        gemb[1, here, :] = jnp.where(own, glip, 0.0).astype(BF16)
        gacc[c, window, :] += dot(gd, ev, TN)
        giacc[c, window, :] += jnp.broadcast_to(gia, (WIN, LANES))
        return loss

    loss = lax.fori_loop(0, clips * tiles, tile_step, jnp.zeros((), F32), unroll=clips * tiles <= 8)

    def audio_step(i, _):
        c = i // per_clip
        at = pl.ds(pl.multiple_of(PAD + lax.rem(i, per_clip) * block, PAD), block)
        inv = inv_a[c, at, 0:1]
        grad = gacc[c, at, :] - (inv * inv * inv * giacc[c, at, 0:1]) * emb_a[c, at, :].astype(F32)
        if halo:
            at_row = lax.rem(i, per_clip) * block + lax.broadcasted_iota(jnp.int32, (block, 1), 0)
            grad = jnp.where((at_row >= halo) & (at_row < frames - halo), grad, 0.0)
        gemb[0, pl.ds(pl.multiple_of(i * block, block), block), :] = grad.astype(BF16)
        return 0

    lax.fori_loop(0, rows_total // block, audio_step, 0)

    count = jnp.zeros((), F32)
    for c in range(clips):
        count = count + (lengths[first_clip + c] - jnp.abs(labels[first_clip + c])).astype(F32)
    if halo:
        count = jnp.where(me == 0, count, 0.0)
    send_rows = send.shape[0] - 2 * PAD
    send[send_rows : send_rows + PAD, :] = jnp.broadcast_to(digits_of(loss), (PAD, LANES)).astype(BF16)
    send[send_rows + PAD :, :] = jnp.broadcast_to(digits_of(count), (PAD, LANES)).astype(BF16)

    backward(1, wvp, cols, slope, hid, gemb, gpre, total, block, rows_total)
    hand_over(total, keep, send, 1, half)
    backward(0, wap, cols, slope, hid, gemb, gpre, total, block, rows_total)
    hand_over(total, keep, send, 0, half)


def local_grads(halo, lengths, labels, feats, wac, wap, wvc, wvp):
    _, clips, frames, chan = feats.shape
    width = wap.shape[0]
    rows = clips * frames
    taps = wac.shape[0]
    grad_rows = taps * chan + width
    wac = wac.reshape(taps * chan, width)
    wvc = wvc.reshape(taps * chan, width)
    blocks = width // 2 // LANES
    smem = pl.BlockSpec(memory_space=pltpu.SMEM)
    vmem = pl.BlockSpec(memory_space=pltpu.VMEM)
    return pl.pallas_call(
        functools.partial(kernel, frames, clips, halo),
        out_shape=(
            jax.ShapeDtypeStruct((2 * blocks * grad_rows, LANES), F32),
            jax.ShapeDtypeStruct((2 * blocks * grad_rows + 2 * PAD, LANES), BF16),
        ),
        in_specs=[smem, smem] + [vmem] * 5,
        out_specs=(vmem, vmem),
        scratch_shapes=[
            pltpu.VMEM((2, rows, taps * chan), BF16),
            pltpu.VMEM((2, rows, width), F32),
            pltpu.VMEM((2, rows, width), BF16),
            pltpu.VMEM((2, rows, width), BF16),
            pltpu.VMEM((2, rows, width), BF16),
            pltpu.VMEM((grad_rows, width), F32),
            pltpu.VMEM((clips, frames + 2 * PAD, width), BF16),
            pltpu.VMEM((rows, width), BF16),
            pltpu.VMEM((clips, frames + 2 * PAD, LANES), F32),
            pltpu.VMEM((rows, LANES), F32),
            pltpu.VMEM((clips, frames + 2 * PAD, width), F32),
            pltpu.VMEM((clips, frames + 2 * PAD, LANES), F32),
        ],
        compiler_params=pltpu.CompilerParams(vmem_limit_bytes=60 * 1024 * 1024),
    )(lengths, labels, feats, wac, wap, wvc, wvp)


def swap(value, axis, bit):
    return lax.ppermute(value, axis, [(i, i ^ bit) for i in range(lax.axis_size(axis))])


def pick(value, index):
    return lax.dynamic_index_in_dim(value, index, 0, keepdims=False)


def halve(value, axis, bit, tile=None):
    me = (lax.axis_index(axis) // bit) % 2
    parts = value.reshape(2, -1, LANES)
    out = pick(parts, 1 - me).astype(BF16)
    if tile is not None:
        out = jnp.concatenate([out, tile])
    got = swap(out, axis, bit)
    rows = parts.shape[1]
    mine = pick(parts, me).astype(F32) + got[:rows].astype(F32)
    return mine if tile is None else (mine, (tile.astype(F32) + got[rows:].astype(F32)).astype(BF16))


def double(value, axis, bit):
    me = (lax.axis_index(axis) // bit) % 2
    got = swap(value, axis, bit)
    return jnp.stack([jnp.where(me == 0, value, got), jnp.where(me == 0, got, value)]).reshape(-1, LANES)


def quarter(parts, axis, bit, tile):
    me = (lax.axis_index(axis) // bit) % 4
    rows = parts.shape[1]
    mine = pick(parts, me).astype(F32)
    whole = tile.astype(F32)
    for k in (1, 2, 3):
        got = swap(jnp.concatenate([pick(parts, me ^ k).astype(BF16), tile]), axis, k * bit).astype(F32)
        mine = mine + got[:rows]
        whole = whole + got[rows:]
    return mine, whole


def quadruple(value, axis, bit):
    me = (lax.axis_index(axis) // bit) % 4
    got = [value] + [swap(value, axis, k * bit) for k in (1, 2, 3)]
    out = []
    for j in range(4):
        k = me ^ j
        out.append(jnp.where(k == 0, got[0], jnp.where(k == 1, got[1], jnp.where(k == 2, got[2], got[3]))))
    return jnp.stack(out)


def bits_of(axis):
    size, bits = lax.axis_size(axis), []
    bit = 1
    while bit < size:
        bits.append(bit)
        bit *= 2
    return bits


def reduce_all(keep, send):
    tm_bits, clip_bits = bits_of("tm"), bits_of("clip")
    got = swap(send, "tm", 1)
    rows = keep.shape[0]
    total = keep + got[:rows].astype(F32)
    tile = (send[rows:].astype(F32) + got[rows:].astype(F32)).astype(BF16)
    first, second = total.reshape(2, -1, LANES)
    for bit in tm_bits[1:]:
        first, tile = halve(first, "tm", bit, tile)
        second = halve(second, "tm", bit)
    singles, last = clip_bits[:-2], clip_bits[-2]
    order_1 = singles
    order_2 = singles[1::-1] + singles[2:]
    for bit_1, bit_2 in zip(order_1, order_2):
        first, tile = halve(first, "clip", bit_1, tile)
        second = halve(second, "clip", bit_2)
    parts = jnp.concatenate([first.reshape(4, -1, LANES), second.reshape(4, -1, LANES)], axis=1)
    mine, tile = quarter(parts, "clip", last, tile)
    parts = quadruple(mine.astype(BF16), "clip", last)
    n = parts.shape[1] // 2
    first, second = parts[:, :n].reshape(-1, LANES), parts[:, n:].reshape(-1, LANES)
    for bit_1, bit_2 in zip(order_1[::-1], order_2[::-1]):
        first = double(first, "clip", bit_1)
        second = double(second, "clip", bit_2)
    for bit in tm_bits[:0:-1]:
        first = double(first, "tm", bit)
        second = double(second, "tm", bit)
    mine = jnp.concatenate([first, second])
    return mine, swap(mine, "tm", 1), tile


def finish_kernel(mine_c, got_c, mine_p, got_p, tile, loss, ac, ap, vc, vp):
    half = lax.rem(lax.axis_index("tm"), 2)
    digits = tile[...].astype(F32)
    count = value_of(digits[PAD : PAD + 1])
    scale = 1.0 / count
    loss[...] = jnp.broadcast_to(value_of(digits[0:1]) / count, loss.shape)
    for mine, got, outs in ((mine_c, got_c, (ac, vc)), (mine_p, got_p, (ap, vp))):
        for m, out in enumerate(outs):
            blocks = mine.shape[1]
            for j in range(blocks):
                at = pl.multiple_of((half * blocks + j) * LANES, LANES)
                out[:, pl.ds(at, LANES)] = mine[m, j].astype(F32) * scale
                at = pl.multiple_of(((1 - half) * blocks + j) * LANES, LANES)
                out[:, pl.ds(at, LANES)] = got[m, j].astype(F32) * scale


def finish(mine, got, tile, conv_rows, width):
    blocks = width // 2 // LANES
    rows = conv_rows + width
    mine = mine.reshape(2, blocks, rows, LANES)
    got = got.reshape(2, blocks, rows, LANES)
    steps = 4
    conv, proj = conv_rows // steps, width // steps
    skip = conv_rows // proj
    conv_spec = pl.BlockSpec((2, blocks, conv, LANES), lambda i: (0, 0, i, 0))
    proj_spec = pl.BlockSpec((2, blocks, proj, LANES), lambda i: (0, 0, skip + i, 0))
    conv_out = pl.BlockSpec((conv, width), lambda i: (i, 0))
    proj_out = pl.BlockSpec((proj, width), lambda i: (i, 0))
    one = pl.BlockSpec((8, LANES), lambda i: (0, 0))
    return pl.pallas_call(
        finish_kernel,
        grid=(steps,),
        out_shape=(
            jax.ShapeDtypeStruct((8, LANES), F32),
            jax.ShapeDtypeStruct((conv_rows, width), F32),
            jax.ShapeDtypeStruct((width, width), F32),
            jax.ShapeDtypeStruct((conv_rows, width), F32),
            jax.ShapeDtypeStruct((width, width), F32),
        ),
        in_specs=[conv_spec, conv_spec, proj_spec, proj_spec, pl.BlockSpec((2 * PAD, LANES), lambda i: (0, 0))],
        out_specs=(one, conv_out, proj_out, conv_out, proj_out),
        compiler_params=pltpu.CompilerParams(vmem_limit_bytes=32 * 1024 * 1024),
    )(mine, got, mine, got, tile)


def shards(
    audio_feats, lip_feats, lengths, labels, w_audio_conv, w_audio_proj, w_lip_conv, w_lip_proj
):
    both = jnp.stack([audio_feats, lip_feats])
    peers = lax.axis_size("tm")
    halo = 0
    if peers == 2 and both.shape[1] % 2 == 0:
        me = lax.axis_index("tm")
        parts = both.reshape(2, 2, both.shape[1] // 2, *both.shape[2:])
        mine = lax.dynamic_index_in_dim(parts, me, 1, keepdims=False)
        got = swap(lax.dynamic_index_in_dim(parts, 1 - me, 1, keepdims=False), "tm", 1)
        feats = jnp.concatenate(
            [jnp.where(me == 0, mine, got), jnp.where(me == 0, got, mine)], axis=2
        )
    else:
        halo = HALO
        after = [(i, i + 1) for i in range(peers - 1)]
        before = [(i + 1, i) for i in range(peers - 1)]
        feats = jnp.concatenate(
            [
                lax.ppermute(both[:, :, -HALO:], "tm", after),
                both,
                lax.ppermute(both[:, :, :HALO], "tm", before),
            ],
            axis=2,
        )
    keep, send = local_grads(
        halo, lengths, labels, feats, w_audio_conv, w_audio_proj, w_lip_conv, w_lip_proj
    )
    mine, got, tile = reduce_all(keep, send)
    taps, chan, width = w_audio_conv.shape
    loss, ac, ap, vc, vp = finish(mine, got, tile.astype(BF16), taps * chan, width)
    return (loss[0, 0], ac.reshape(w_audio_conv.shape), ap, vc.reshape(w_lip_conv.shape), vp)


def solution(mesh):
    placed = (
        P("clip", "tm", None),
        P("clip", "tm", None),
        P("clip"),
        P("clip"),
        P(),
        P(),
        P(),
        P(),
    )
    return jax.shard_map(
        shards, mesh=mesh, in_specs=placed, out_specs=(P(), P(), P(), P(), P()), check_vma=False
    )
```

```python
import functools

import jax
import jax.numpy as jnp
from jax import lax
from jax.experimental import pallas as pl
from jax.experimental.pallas import tpu as pltpu
from jax.sharding import PartitionSpec as P

SPAN = 15
PAD = 16
TILE = 128
WIN = TILE + 2 * PAD
HALO = 64
LANES = 128
DIGITS = 48
FRACTION = 20

logit_sharpening_divisor = 10.0
loss_scale = 1024.0
epsilon = 1e-06

BF16 = jnp.bfloat16
F32 = jnp.float32


def dot(a, b, dims):
    return lax.dot_general(a, b, (dims, ((), ())), preferred_element_type=F32)


NN = ((1,), (0,))
NT = ((1,), (1,))
TN = ((0,), (0,))


def digit_weights(shape):
    lane = lax.broadcasted_iota(jnp.int32, shape, len(shape) - 1)
    return lane, jnp.exp2((lane - FRACTION).astype(F32))


def digits_of(value):
    lane, weight = digit_weights((1, LANES))
    size = jnp.abs(value)
    bits = jnp.floor(size / weight) - 2.0 * jnp.floor(size / (2.0 * weight))
    return jnp.where(lane < DIGITS, jnp.where(value < 0, -bits, bits), 0.0)


def value_of(digits):
    lane, weight = digit_weights(digits.shape)
    return jnp.sum(jnp.where(lane < DIGITS, digits * weight, 0.0))


def forward(feats, m, w_conv, w_proj, cols, slope, hid, clips, frames, block, put):
    chan = feats.shape[-1]
    for c in range(clips):
        x = feats[m, c].astype(F32)
        row = lax.broadcasted_iota(jnp.int32, x.shape, 0)
        base = c * frames
        cols[m, base : base + frames, 0:chan] = jnp.where(row == 0, 0.0, pltpu.roll(x, 1, 0)).astype(BF16)
        cols[m, base : base + frames, chan : 2 * chan] = feats[m, c]
        cols[m, base : base + frames, 2 * chan : 3 * chan] = jnp.where(
            row == frames - 1, 0.0, pltpu.roll(x, frames - 1, 0)
        ).astype(BF16)

    def step(i, _):
        rows = pl.ds(pl.multiple_of(i * block, block), block)
        pre = dot(cols[m, rows, :], w_conv[...], NN)
        sigma = 0.5 * jnp.tanh(0.5 * pre) + 0.5
        hidden = (pre * sigma).astype(BF16)
        hid[m, rows, :] = hidden
        slope[m, rows, :] = sigma * (1.0 + pre * (1.0 - sigma))
        emb = dot(hidden, w_proj[...], NN).astype(BF16)
        values = emb.astype(F32)
        inv = lax.rsqrt(jnp.sum(values * values, axis=1, keepdims=True) + epsilon)
        put(i, emb, jnp.broadcast_to(inv, (block, LANES)))
        return 0

    lax.fori_loop(0, clips * frames // block, step, 0, unroll=True)


def backward(m, w_proj, cols, slope, hid, gemb, gpre, total, block, rows_total):
    def step(i, _):
        rows = pl.ds(pl.multiple_of(i * block, block), block)
        grad = dot(gemb[m, rows, :], w_proj[...], NT) * slope[m, rows, :]
        gpre[m, rows, :] = grad.astype(BF16)
        return 0

    lax.fori_loop(0, rows_total // block, step, 0, unroll=True)
    conv_rows = cols.shape[-1]

    def conv_step(i, _):
        at = pl.multiple_of(i * 256, 256)
        total[pl.ds(at, 256), :] = dot(cols[m, :, pl.ds(at, 256)], gpre[m], TN)
        return 0

    lax.fori_loop(0, conv_rows // 256, conv_step, 0)

    def proj_step(i, _):
        at = pl.multiple_of(i * 256, 256)
        total[pl.ds(conv_rows + at, 256), :] = dot(hid[m, :, pl.ds(at, 256)], gemb[m], TN)
        return 0

    lax.fori_loop(0, hid.shape[-1] // 256, proj_step, 0)


def hand_over(total, keep, send, m, half):
    width = total.shape[1] // 2
    for j in range(width // LANES):
        mine = pl.ds(pl.multiple_of(half * width + j * LANES, LANES), LANES)
        other = pl.ds(pl.multiple_of((1 - half) * width + j * LANES, LANES), LANES)
        at = (m * (width // LANES) + j) * total.shape[0]
        keep[at : at + total.shape[0], :] = total[:, mine]
        send[at : at + total.shape[0], :] = total[:, other].astype(BF16)


def kernel(
    frames, clips, halo, lengths, labels, own_a, own_v, got, wac, wap, wvc, wvp, keep, send,
    cols, slope, hid, gemb, gpre, total, emb_a, emb_v, inv_a, inv_v, gacc, giacc, feats,
):
    me = lax.axis_index("tm")
    half = lax.rem(me, 2)
    rows_total = clips * frames
    start = me * (frames - 2 * halo) - halo if halo else 0
    first_clip = 0 if halo else me * clips
    block = 256 if frames % 256 == 0 else TILE
    per_clip = frames // block

    if halo:
        feats[0] = own_a[...]
        feats[1] = own_v[...]
    else:
        seg = own_a.shape[1]
        mine = pl.ds(pl.multiple_of(me * seg, seg), seg)
        other = pl.ds(pl.multiple_of((1 - me) * seg, seg), seg)
        for c in range(clips):
            feats[0, c, mine, :] = own_a[first_clip + c]
            feats[1, c, mine, :] = own_v[first_clip + c]
            feats[0, c, other, :] = got[0, c]
            feats[1, c, other, :] = got[1, c]

    for c in range(clips):
        for lo in (0, PAD + frames):
            emb_a[c, lo : lo + PAD, :] = jnp.zeros((PAD, emb_a.shape[2]), BF16)
            inv_a[c, lo : lo + PAD, :] = jnp.zeros((PAD, LANES), F32)

    def put_a(i, emb, inv):
        c = i // per_clip
        at = pl.multiple_of(PAD + lax.rem(i, per_clip) * block, PAD)
        emb_a[c, pl.ds(at, block), :] = emb
        inv_a[c, pl.ds(at, block), :] = inv

    def put_v(i, emb, inv):
        at = pl.multiple_of(i * block, block)
        emb_v[pl.ds(at, block), :] = emb
        inv_v[pl.ds(at, block), :] = inv

    forward(feats, 1, wvc, wvp, cols, slope, hid, clips, frames, block, put_v)
    forward(feats, 0, wac, wap, cols, slope, hid, clips, frames, block, put_a)

    gacc[...] = jnp.zeros(gacc.shape, F32)
    giacc[...] = jnp.zeros(giacc.shape, F32)
    tiles = frames // TILE
    row = lax.broadcasted_iota(jnp.int32, (TILE, WIN), 0)
    col = lax.broadcasted_iota(jnp.int32, (TILE, WIN), 1)
    shift = col - row - PAD
    in_band = (shift >= -SPAN) & (shift <= SPAN)
    row_1 = lax.broadcasted_iota(jnp.int32, (TILE, 1), 0)

    def tile_step(i, loss):
        c = i // tiles
        first = pl.multiple_of(lax.rem(i, tiles) * TILE, TILE)
        length = lengths[first_clip + c]
        label = labels[first_clip + c]
        here = pl.ds(pl.multiple_of(i * TILE, TILE), TILE)
        window = pl.ds(first, WIN)
        ev = emb_v[here, :]
        wa = emb_a[c, window, :]
        iv = inv_v[here, 0:1]
        ia = inv_a[c, window, :].T
        dots = dot(ev, wa, NT)
        scores = logit_sharpening_divisor * dots * iv * ia
        t = start + first + row_1
        u = start + first - PAD + col
        inside = t < length
        valid = in_band & inside & (u >= 0) & (u < length)
        target = t + label
        counted = inside & (target >= 0) & (target < length)
        hit = shift == label
        weights = jnp.where(valid, jnp.exp(scores), 0.0)
        sums = jnp.where(inside, jnp.sum(weights, axis=1, keepdims=True), 1.0)
        picked = jnp.sum(jnp.where(hit, scores, 0.0), axis=1, keepdims=True)
        own = (first + row_1 >= halo) & (first + row_1 < frames - halo)
        loss = loss + jnp.sum(jnp.where(counted & own, jnp.log(sums) - picked, 0.0))
        scale = jnp.where(counted, logit_sharpening_divisor * loss_scale, 0.0)
        grad = scale * (weights / sums - jnp.where(hit, 1.0, 0.0))
        gd = (grad * iv * ia).astype(BF16)
        by_dots = grad * dots
        giv = jnp.sum(by_dots * ia, axis=1, keepdims=True)
        gia = jnp.sum((by_dots * iv).T, axis=1, keepdims=True)
        glip = dot(gd, wa, NN) - (iv * iv * iv * giv) * ev.astype(F32)
        gemb[1, here, :] = jnp.where(own, glip, 0.0).astype(BF16)
        gacc[c, window, :] += dot(gd, ev, TN)
        giacc[c, window, :] += jnp.broadcast_to(gia, (WIN, LANES))
        return loss

    loss = lax.fori_loop(0, clips * tiles, tile_step, jnp.zeros((), F32), unroll=clips * tiles <= 8)

    def audio_step(i, _):
        c = i // per_clip
        at = pl.ds(pl.multiple_of(PAD + lax.rem(i, per_clip) * block, PAD), block)
        inv = inv_a[c, at, 0:1]
        grad = gacc[c, at, :] - (inv * inv * inv * giacc[c, at, 0:1]) * emb_a[c, at, :].astype(F32)
        if halo:
            at_row = lax.rem(i, per_clip) * block + lax.broadcasted_iota(jnp.int32, (block, 1), 0)
            grad = jnp.where((at_row >= halo) & (at_row < frames - halo), grad, 0.0)
        gemb[0, pl.ds(pl.multiple_of(i * block, block), block), :] = grad.astype(BF16)
        return 0

    lax.fori_loop(0, rows_total // block, audio_step, 0)

    count = jnp.zeros((), F32)
    for c in range(clips):
        count = count + (lengths[first_clip + c] - jnp.abs(labels[first_clip + c])).astype(F32)
    if halo:
        count = jnp.where(me == 0, count, 0.0)
    send_rows = send.shape[0] - 2 * PAD
    send[send_rows : send_rows + PAD, :] = jnp.broadcast_to(digits_of(loss), (PAD, LANES)).astype(BF16)
    send[send_rows + PAD :, :] = jnp.broadcast_to(digits_of(count), (PAD, LANES)).astype(BF16)

    backward(1, wvp, cols, slope, hid, gemb, gpre, total, block, rows_total)
    hand_over(total, keep, send, 1, half)
    backward(0, wap, cols, slope, hid, gemb, gpre, total, block, rows_total)
    hand_over(total, keep, send, 0, half)


def local_grads(halo, lengths, labels, own_a, own_v, got, wac, wap, wvc, wvp):
    clips, frames, chan = own_a.shape
    if not halo:
        clips, frames = clips // 2, frames * 2
    width = wap.shape[0]
    rows = clips * frames
    taps = wac.shape[0]
    grad_rows = taps * chan + width
    wac = wac.reshape(taps * chan, width)
    wvc = wvc.reshape(taps * chan, width)
    blocks = width // 2 // LANES
    smem = pl.BlockSpec(memory_space=pltpu.SMEM)
    vmem = pl.BlockSpec(memory_space=pltpu.VMEM)
    return pl.pallas_call(
        functools.partial(kernel, frames, clips, halo),
        out_shape=(
            jax.ShapeDtypeStruct((2 * blocks * grad_rows, LANES), F32),
            jax.ShapeDtypeStruct((2 * blocks * grad_rows + 2 * PAD, LANES), BF16),
        ),
        in_specs=[smem, smem] + [vmem] * 7,
        out_specs=(vmem, vmem),
        scratch_shapes=[
            pltpu.VMEM((2, rows, taps * chan), BF16),
            pltpu.VMEM((2, rows, width), F32),
            pltpu.VMEM((2, rows, width), BF16),
            pltpu.VMEM((2, rows, width), BF16),
            pltpu.VMEM((2, rows, width), BF16),
            pltpu.VMEM((grad_rows, width), F32),
            pltpu.VMEM((clips, frames + 2 * PAD, width), BF16),
            pltpu.VMEM((rows, width), BF16),
            pltpu.VMEM((clips, frames + 2 * PAD, LANES), F32),
            pltpu.VMEM((rows, LANES), F32),
            pltpu.VMEM((clips, frames + 2 * PAD, width), F32),
            pltpu.VMEM((clips, frames + 2 * PAD, LANES), F32),
            pltpu.VMEM((2, clips, frames, chan), BF16),
        ],
        compiler_params=pltpu.CompilerParams(vmem_limit_bytes=60 * 1024 * 1024),
    )(lengths, labels, own_a, own_v, got, wac, wap, wvc, wvp)


def swap(value, axis, bit):
    return lax.ppermute(value, axis, [(i, i ^ bit) for i in range(lax.axis_size(axis))])


def swap_by_core(value, bits):
    peers = lax.axis_size("tm")
    pairs = []
    for clip in range(lax.axis_size("clip")):
        for tm in range(peers):
            pairs.append((clip * peers + tm, (clip ^ bits[tm % 2]) * peers + tm))
    return lax.ppermute(value, ("clip", "tm"), pairs)


def pick(value, index):
    return lax.dynamic_index_in_dim(value, index, 0, keepdims=False)


def halve(value, axis, bit, tile):
    me = (lax.axis_index(axis) // bit) % 2
    parts = value.reshape(2, -1, LANES)
    got = swap(jnp.concatenate([pick(parts, 1 - me).astype(BF16), tile]), axis, bit).astype(F32)
    rows = parts.shape[1]
    return pick(parts, me).astype(F32) + got[:rows], (tile.astype(F32) + got[rows:]).astype(BF16)


def double(value, axis, bit):
    me = (lax.axis_index(axis) // bit) % 2
    got = swap(value, axis, bit)
    return jnp.stack([jnp.where(me == 0, value, got), jnp.where(me == 0, got, value)]).reshape(-1, LANES)


def place_of(bits):
    clip, odd = lax.axis_index("clip"), lax.axis_index("tm") % 2
    return jnp.where(odd == 0, (clip // bits[0]) % 4, (clip // bits[1]) % 4)


def quarter(parts, bits, tile):
    me = place_of(bits)
    rows = parts.shape[1]
    mine = pick(parts, me).astype(F32)
    whole = tile.astype(F32)
    for k in (1, 2, 3):
        out = jnp.concatenate([pick(parts, me ^ k).astype(BF16), tile])
        got = swap_by_core(out, (k * bits[0], k * bits[1])).astype(F32)
        mine = mine + got[:rows]
        whole = whole + got[rows:]
    return mine, whole.astype(BF16)


def quadruple(value, bits):
    me = place_of(bits)
    got = [value] + [swap_by_core(value, (k * bits[0], k * bits[1])) for k in (1, 2, 3)]
    out = []
    for j in range(4):
        k = me ^ j
        out.append(jnp.where(k == 0, got[0], jnp.where(k == 1, got[1], jnp.where(k == 2, got[2], got[3]))))
    return jnp.stack(out).reshape(-1, LANES)


def bits_of(axis):
    size, bits = lax.axis_size(axis), []
    bit = 1
    while bit < size:
        bits.append(bit)
        bit *= 2
    return bits


def reduce_all(keep, send):
    got = swap(send, "tm", 1)
    rows = keep.shape[0]
    total = keep + got[:rows].astype(F32)
    tile = (send[rows:].astype(F32) + got[rows:].astype(F32)).astype(BF16)
    rest = [("tm", bit) for bit in bits_of("tm")[1:]] + [("clip", bit) for bit in bits_of("clip")[4:]]
    for axis, bit in rest:
        total, tile = halve(total, axis, bit, tile)
    total, tile = quarter(total.reshape(4, -1, LANES), (1, 4), tile)
    total, tile = quarter(total.reshape(4, -1, LANES), (4, 1), tile)
    mine = quadruple(total.astype(BF16), (4, 1))
    mine = quadruple(mine, (1, 4))
    for axis, bit in rest[::-1]:
        mine = double(mine, axis, bit)
    return mine, swap(mine, "tm", 1), tile


def finish_kernel(mine_c, got_c, mine_p, got_p, tile, loss, ac, ap, vc, vp):
    half = lax.rem(lax.axis_index("tm"), 2)
    digits = tile[...].astype(F32)
    count = value_of(digits[PAD : PAD + 1])
    scale = 1.0 / count
    loss[...] = jnp.broadcast_to(value_of(digits[0:1]) / count, loss.shape)
    for mine, got, outs in ((mine_c, got_c, (ac, vc)), (mine_p, got_p, (ap, vp))):
        for m, out in enumerate(outs):
            blocks = mine.shape[1]
            for j in range(blocks):
                at = pl.multiple_of((half * blocks + j) * LANES, LANES)
                out[:, pl.ds(at, LANES)] = mine[m, j].astype(F32) * scale
                at = pl.multiple_of(((1 - half) * blocks + j) * LANES, LANES)
                out[:, pl.ds(at, LANES)] = got[m, j].astype(F32) * scale


def finish(mine, got, tile, conv_rows, width):
    blocks = width // 2 // LANES
    rows = conv_rows + width
    mine = mine.reshape(2, blocks, rows, LANES)
    got = got.reshape(2, blocks, rows, LANES)
    steps = 4
    conv, proj = conv_rows // steps, width // steps
    skip = conv_rows // proj
    conv_spec = pl.BlockSpec((2, blocks, conv, LANES), lambda i: (0, 0, i, 0))
    proj_spec = pl.BlockSpec((2, blocks, proj, LANES), lambda i: (0, 0, skip + i, 0))
    conv_out = pl.BlockSpec((conv, width), lambda i: (i, 0))
    proj_out = pl.BlockSpec((proj, width), lambda i: (i, 0))
    one = pl.BlockSpec((8, LANES), lambda i: (0, 0))
    return pl.pallas_call(
        finish_kernel,
        grid=(steps,),
        out_shape=(
            jax.ShapeDtypeStruct((8, LANES), F32),
            jax.ShapeDtypeStruct((conv_rows, width), F32),
            jax.ShapeDtypeStruct((width, width), F32),
            jax.ShapeDtypeStruct((conv_rows, width), F32),
            jax.ShapeDtypeStruct((width, width), F32),
        ),
        in_specs=[conv_spec, conv_spec, proj_spec, proj_spec, pl.BlockSpec((2 * PAD, LANES), lambda i: (0, 0))],
        out_specs=(one, conv_out, proj_out, conv_out, proj_out),
        compiler_params=pltpu.CompilerParams(vmem_limit_bytes=32 * 1024 * 1024),
    )(mine, got, mine, got, tile)


def shards(
    audio_feats, lip_feats, lengths, labels, w_audio_conv, w_audio_proj, w_lip_conv, w_lip_proj
):
    peers = lax.axis_size("tm")
    clips, frames, chan = audio_feats.shape
    halo = 0
    if peers == 2 and clips % 2 == 0:
        others = (1 - lax.axis_index("tm")) * (clips // 2)
        out = jnp.stack([lax.dynamic_slice_in_dim(x, others, clips // 2) for x in (audio_feats, lip_feats)])
        got = swap(out, "tm", 1)
    else:
        halo = HALO
        after = [(i, i + 1) for i in range(peers - 1)]
        before = [(i + 1, i) for i in range(peers - 1)]
        both = jnp.stack([audio_feats, lip_feats])
        audio_feats, lip_feats = jnp.concatenate(
            [
                lax.ppermute(both[:, :, -HALO:], "tm", after),
                both,
                lax.ppermute(both[:, :, :HALO], "tm", before),
            ],
            axis=2,
        )
        got = lengths.astype(BF16)
    keep, send = local_grads(
        halo, lengths, labels, audio_feats, lip_feats, got, w_audio_conv, w_audio_proj, w_lip_conv, w_lip_proj
    )
    mine, got, tile = reduce_all(keep, send)
    taps, chan, width = w_audio_conv.shape
    loss, ac, ap, vc, vp = finish(mine, got, tile, taps * chan, width)
    return (loss[0, 0], ac.reshape(w_audio_conv.shape), ap, vc.reshape(w_lip_conv.shape), vp)


def solution(mesh):
    placed = (
        P("clip", "tm", None),
        P("clip", "tm", None),
        P("clip"),
        P("clip"),
        P(),
        P(),
        P(),
        P(),
    )
    return jax.shard_map(
        shards, mesh=mesh, in_specs=placed, out_specs=(P(), P(), P(), P(), P()), check_vma=False
    )
```

```python
import functools

import jax
import jax.numpy as jnp
from jax import lax
from jax.experimental import pallas as pl
from jax.experimental.pallas import tpu as pltpu
from jax.sharding import PartitionSpec as P

SPAN = 15
PAD = 16
TILE = 128
WIN = TILE + 2 * PAD
HALO = 64
LANES = 128
DIGITS = 48
FRACTION = 20

logit_sharpening_divisor = 10.0
loss_scale = 1024.0
epsilon = 1e-06

BF16 = jnp.bfloat16
F32 = jnp.float32


def dot(a, b, dims):
    return lax.dot_general(a, b, (dims, ((), ())), preferred_element_type=F32)


NN = ((1,), (0,))
NT = ((1,), (1,))
TN = ((0,), (0,))


def digit_weights(shape):
    lane = lax.broadcasted_iota(jnp.int32, shape, len(shape) - 1)
    return lane, jnp.exp2((lane - FRACTION).astype(F32))


def digits_of(value):
    lane, weight = digit_weights((1, LANES))
    size = jnp.abs(value)
    bits = jnp.floor(size / weight) - 2.0 * jnp.floor(size / (2.0 * weight))
    return jnp.where(lane < DIGITS, jnp.where(value < 0, -bits, bits), 0.0)


def value_of(digits):
    lane, weight = digit_weights(digits.shape)
    return jnp.sum(jnp.where(lane < DIGITS, digits * weight, 0.0))


def forward(feats, m, copies, w_conv, w_proj, cols, slope, hid, clips, frames, block, put):
    chan = feats.shape[-1]
    for copy in copies[0]:
        copy.wait()
    for c in range(clips):
        x = feats[m, c].astype(F32)
        row = lax.broadcasted_iota(jnp.int32, x.shape, 0)
        base = c * frames
        cols[m, base : base + frames, 0:chan] = jnp.where(row == 0, 0.0, pltpu.roll(x, 1, 0)).astype(BF16)
        cols[m, base : base + frames, chan : 2 * chan] = feats[m, c]
        cols[m, base : base + frames, 2 * chan : 3 * chan] = jnp.where(
            row == frames - 1, 0.0, pltpu.roll(x, frames - 1, 0)
        ).astype(BF16)

    for copy in copies[1]:
        copy.wait()

    def step(i, _):
        rows = pl.ds(pl.multiple_of(i * block, block), block)
        pre = dot(cols[m, rows, :], w_conv[...], NN)
        sigma = 0.5 * jnp.tanh(0.5 * pre) + 0.5
        hidden = (pre * sigma).astype(BF16)
        hid[m, rows, :] = hidden
        slope[m, rows, :] = sigma * (1.0 + pre * (1.0 - sigma))
        emb = dot(hidden, w_proj[...], NN).astype(BF16)
        values = emb.astype(F32)
        inv = lax.rsqrt(jnp.sum(values * values, axis=1, keepdims=True) + epsilon)
        put(i, emb, jnp.broadcast_to(inv, (block, LANES)))
        return 0

    lax.fori_loop(0, clips * frames // block, step, 0, unroll=True)


def backward(m, w_proj, cols, slope, hid, gemb, gpre, total, block, rows_total):
    def step(i, _):
        rows = pl.ds(pl.multiple_of(i * block, block), block)
        grad = dot(gemb[m, rows, :], w_proj[...], NT) * slope[m, rows, :]
        gpre[m, rows, :] = grad.astype(BF16)
        return 0

    lax.fori_loop(0, rows_total // block, step, 0, unroll=True)
    conv_rows = cols.shape[-1]

    def conv_step(i, _):
        at = pl.multiple_of(i * 256, 256)
        total[pl.ds(at, 256), :] = dot(cols[m, :, pl.ds(at, 256)], gpre[m], TN)
        return 0

    lax.fori_loop(0, conv_rows // 256, conv_step, 0)

    def proj_step(i, _):
        at = pl.multiple_of(i * 256, 256)
        total[pl.ds(conv_rows + at, 256), :] = dot(hid[m, :, pl.ds(at, 256)], gemb[m], TN)
        return 0

    lax.fori_loop(0, hid.shape[-1] // 256, proj_step, 0)


def hand_over(total, keep, send, m, half):
    width = total.shape[1] // 2
    for j in range(width // LANES):
        mine = pl.ds(pl.multiple_of(half * width + j * LANES, LANES), LANES)
        other = pl.ds(pl.multiple_of((1 - half) * width + j * LANES, LANES), LANES)
        at = (m * (width // LANES) + j) * total.shape[0]
        keep[at : at + total.shape[0], :] = total[:, mine]
        send[at : at + total.shape[0], :] = total[:, other].astype(BF16)


def kernel(
    frames, clips, halo, lengths, labels, own_a, own_v, got, wac_in, wap_in, wvc_in, wvp_in, keep, send,
    cols, slope, hid, gemb, gpre, total, emb_a, emb_v, inv_a, inv_v, gacc, giacc, feats, wac, wap, wvc, wvp, sems,
):
    me = lax.axis_index("tm")
    half = lax.rem(me, 2)
    rows_total = clips * frames
    start = me * (frames - 2 * halo) - halo if halo else 0
    first_clip = 0 if halo else me * clips
    block = 256 if frames % 256 == 0 else TILE
    per_clip = frames // block

    copies = []

    def fetch(source, target):
        copy = pltpu.make_async_copy(source, target, sems.at[len(copies)])
        copy.start()
        copies.append(copy)
        return copy

    def fetch_feats(m, own):
        if halo:
            return [fetch(own, feats.at[m])]
        seg = own.shape[1]
        mine = pl.ds(pl.multiple_of(me * seg, seg), seg)
        other = pl.ds(pl.multiple_of((1 - me) * seg, seg), seg)
        started = []
        for c in range(clips):
            started.append(fetch(own.at[first_clip + c], feats.at[m, c, mine, :]))
            started.append(fetch(got.at[m, c], feats.at[m, c, other, :]))
        return started

    feats_v = fetch_feats(1, own_v)
    weights_v = [fetch(wvc_in, wvc), fetch(wvp_in, wvp)]
    feats_a = fetch_feats(0, own_a)
    weights_a = [fetch(wac_in, wac), fetch(wap_in, wap)]
    gacc[...] = jnp.zeros(gacc.shape, F32)
    giacc[...] = jnp.zeros(giacc.shape, F32)

    for c in range(clips):
        for lo in (0, PAD + frames):
            emb_a[c, lo : lo + PAD, :] = jnp.zeros((PAD, emb_a.shape[2]), BF16)
            inv_a[c, lo : lo + PAD, :] = jnp.zeros((PAD, LANES), F32)

    def put_a(i, emb, inv):
        c = i // per_clip
        at = pl.multiple_of(PAD + lax.rem(i, per_clip) * block, PAD)
        emb_a[c, pl.ds(at, block), :] = emb
        inv_a[c, pl.ds(at, block), :] = inv

    def put_v(i, emb, inv):
        at = pl.multiple_of(i * block, block)
        emb_v[pl.ds(at, block), :] = emb
        inv_v[pl.ds(at, block), :] = inv

    forward(feats, 1, (feats_v, weights_v), wvc, wvp, cols, slope, hid, clips, frames, block, put_v)
    forward(feats, 0, (feats_a, weights_a), wac, wap, cols, slope, hid, clips, frames, block, put_a)

    tiles = frames // TILE
    row = lax.broadcasted_iota(jnp.int32, (TILE, WIN), 0)
    col = lax.broadcasted_iota(jnp.int32, (TILE, WIN), 1)
    shift = col - row - PAD
    in_band = (shift >= -SPAN) & (shift <= SPAN)
    row_1 = lax.broadcasted_iota(jnp.int32, (TILE, 1), 0)

    def tile_step(i, loss):
        c = i // tiles
        first = pl.multiple_of(lax.rem(i, tiles) * TILE, TILE)
        length = lengths[first_clip + c]
        label = labels[first_clip + c]
        here = pl.ds(pl.multiple_of(i * TILE, TILE), TILE)
        window = pl.ds(first, WIN)
        ev = emb_v[here, :]
        wa = emb_a[c, window, :]
        iv = inv_v[here, 0:1]
        ia = inv_a[c, window, :].T
        dots = dot(ev, wa, NT)
        scores = logit_sharpening_divisor * dots * iv * ia
        t = start + first + row_1
        u = start + first - PAD + col
        inside = t < length
        valid = in_band & inside & (u >= 0) & (u < length)
        target = t + label
        counted = inside & (target >= 0) & (target < length)
        hit = shift == label
        weights = jnp.where(valid, jnp.exp(scores), 0.0)
        sums = jnp.where(inside, jnp.sum(weights, axis=1, keepdims=True), 1.0)
        picked = jnp.sum(jnp.where(hit, scores, 0.0), axis=1, keepdims=True)
        own = (first + row_1 >= halo) & (first + row_1 < frames - halo)
        loss = loss + jnp.sum(jnp.where(counted & own, jnp.log(sums) - picked, 0.0))
        scale = jnp.where(counted, logit_sharpening_divisor * loss_scale, 0.0)
        grad = scale * (weights / sums - jnp.where(hit, 1.0, 0.0))
        gd = (grad * iv * ia).astype(BF16)
        by_dots = grad * dots
        giv = jnp.sum(by_dots * ia, axis=1, keepdims=True)
        gia = jnp.sum((by_dots * iv).T, axis=1, keepdims=True)
        glip = dot(gd, wa, NN) - (iv * iv * iv * giv) * ev.astype(F32)
        gemb[1, here, :] = jnp.where(own, glip, 0.0).astype(BF16)
        gacc[c, window, :] += dot(gd, ev, TN)
        giacc[c, window, :] += jnp.broadcast_to(gia, (WIN, LANES))
        return loss

    loss = lax.fori_loop(0, clips * tiles, tile_step, jnp.zeros((), F32), unroll=clips * tiles <= 8)

    def audio_step(i, _):
        c = i // per_clip
        at = pl.ds(pl.multiple_of(PAD + lax.rem(i, per_clip) * block, PAD), block)
        inv = inv_a[c, at, 0:1]
        grad = gacc[c, at, :] - (inv * inv * inv * giacc[c, at, 0:1]) * emb_a[c, at, :].astype(F32)
        if halo:
            at_row = lax.rem(i, per_clip) * block + lax.broadcasted_iota(jnp.int32, (block, 1), 0)
            grad = jnp.where((at_row >= halo) & (at_row < frames - halo), grad, 0.0)
        gemb[0, pl.ds(pl.multiple_of(i * block, block), block), :] = grad.astype(BF16)
        return 0

    lax.fori_loop(0, rows_total // block, audio_step, 0)

    count = jnp.zeros((), F32)
    for c in range(clips):
        count = count + (lengths[first_clip + c] - jnp.abs(labels[first_clip + c])).astype(F32)
    if halo:
        count = jnp.where(me == 0, count, 0.0)
    send_rows = send.shape[0] - 2 * PAD
    for at, value in ((send_rows, loss), (send_rows + PAD, count)):
        digits = jnp.broadcast_to(digits_of(value), (PAD, LANES))
        keep[at : at + PAD, :] = digits
        send[at : at + PAD, :] = digits.astype(BF16)

    backward(1, wvp, cols, slope, hid, gemb, gpre, total, block, rows_total)
    hand_over(total, keep, send, 1, half)
    backward(0, wap, cols, slope, hid, gemb, gpre, total, block, rows_total)
    hand_over(total, keep, send, 0, half)


def local_grads(halo, lengths, labels, own_a, own_v, got, wac, wap, wvc, wvp):
    clips, frames, chan = own_a.shape
    if not halo:
        clips, frames = clips // 2, frames * 2
    width = wap.shape[0]
    rows = clips * frames
    taps = wac.shape[0]
    grad_rows = taps * chan + width
    wac = wac.reshape(taps * chan, width)
    wvc = wvc.reshape(taps * chan, width)
    blocks = width // 2 // LANES
    smem = pl.BlockSpec(memory_space=pltpu.SMEM)
    vmem = pl.BlockSpec(memory_space=pltpu.VMEM)
    return pl.pallas_call(
        functools.partial(kernel, frames, clips, halo),
        out_shape=(
            pltpu.VMEM((2 * blocks * grad_rows + 2 * PAD, LANES), F32),
            pltpu.VMEM((2 * blocks * grad_rows + 2 * PAD, LANES), BF16),
        ),
        in_specs=[smem, smem] + [pl.BlockSpec(memory_space=pl.ANY)] * 7,
        out_specs=(vmem, vmem),
        scratch_shapes=[
            pltpu.VMEM((2, rows, taps * chan), BF16),
            pltpu.VMEM((2, rows, width), F32),
            pltpu.VMEM((2, rows, width), BF16),
            pltpu.VMEM((2, rows, width), BF16),
            pltpu.VMEM((2, rows, width), BF16),
            pltpu.VMEM((grad_rows, width), F32),
            pltpu.VMEM((clips, frames + 2 * PAD, width), BF16),
            pltpu.VMEM((rows, width), BF16),
            pltpu.VMEM((clips, frames + 2 * PAD, LANES), F32),
            pltpu.VMEM((rows, LANES), F32),
            pltpu.VMEM((clips, frames + 2 * PAD, width), F32),
            pltpu.VMEM((clips, frames + 2 * PAD, LANES), F32),
            pltpu.VMEM((2, clips, frames, chan), BF16),
            pltpu.VMEM((taps * chan, width), BF16),
            pltpu.VMEM((width, width), BF16),
            pltpu.VMEM((taps * chan, width), BF16),
            pltpu.VMEM((width, width), BF16),
            pltpu.SemaphoreType.DMA((4 * clips + 4,)),
        ],
        compiler_params=pltpu.CompilerParams(vmem_limit_bytes=56 * 1024 * 1024),
    )(lengths, labels, own_a, own_v, got, wac, wap, wvc, wvp)


def swap(value, axis, bit):
    return lax.ppermute(value, axis, [(i, i ^ bit) for i in range(lax.axis_size(axis))])


def swap_by_core(value, bits):
    peers = lax.axis_size("tm")
    pairs = []
    for clip in range(lax.axis_size("clip")):
        for tm in range(peers):
            pairs.append((clip * peers + tm, (clip ^ bits[tm % 2]) * peers + tm))
    return lax.ppermute(value, ("clip", "tm"), pairs)


def pick(value, index):
    return lax.dynamic_index_in_dim(value, index, 0, keepdims=False)


def halve(value, axis, bit, tile):
    me = (lax.axis_index(axis) // bit) % 2
    parts = value.reshape(2, -1, LANES)
    got = swap(jnp.concatenate([pick(parts, 1 - me).astype(BF16), tile]), axis, bit).astype(F32)
    rows = parts.shape[1]
    return pick(parts, me).astype(F32) + got[:rows], (tile.astype(F32) + got[rows:]).astype(BF16)


def double(value, axis, bit):
    me = (lax.axis_index(axis) // bit) % 2
    got = swap(value, axis, bit)
    return jnp.stack([jnp.where(me == 0, value, got), jnp.where(me == 0, got, value)]).reshape(-1, LANES)


def place_of(bits):
    clip, odd = lax.axis_index("clip"), lax.axis_index("tm") % 2
    return jnp.where(odd == 0, (clip // bits[0]) % 4, (clip // bits[1]) % 4)


def quarter(parts, bits, tile):
    me = place_of(bits)
    rows = parts.shape[1]
    mine = pick(parts, me).astype(F32)
    whole = tile.astype(F32)
    for k in (1, 2, 3):
        out = jnp.concatenate([pick(parts, me ^ k).astype(BF16), tile])
        got = swap_by_core(out, (k * bits[0], k * bits[1])).astype(F32)
        mine = mine + got[:rows]
        whole = whole + got[rows:]
    return mine, whole.astype(BF16)


def quadruple(value, bits):
    me = place_of(bits)
    got = [value] + [swap_by_core(value, (k * bits[0], k * bits[1])) for k in (1, 2, 3)]
    out = []
    for j in range(4):
        k = me ^ j
        out.append(jnp.where(k == 0, got[0], jnp.where(k == 1, got[1], jnp.where(k == 2, got[2], got[3]))))
    return jnp.stack(out).reshape(-1, LANES)


def bits_of(axis):
    size, bits = lax.axis_size(axis), []
    bit = 1
    while bit < size:
        bits.append(bit)
        bit *= 2
    return bits


def place_in_kernel(bits):
    clip, odd = lax.axis_index("clip"), lax.rem(lax.axis_index("tm"), 2)
    return jnp.where(odd == 0, lax.rem(clip // bits[0], 4), lax.rem(clip // bits[1], 4))


def sum_kernel(bits, count, base, *refs):
    got, mine, outs = refs[:count], refs[count], refs[count + 1 :]
    me = place_in_kernel(bits)
    part = mine.shape[0] - 2 * PAD

    def total(rows):
        value = base[rows, :]
        for ref in got:
            value = value + ref[rows, :].astype(F32)
        return value

    tile = total(pl.ds(4 * part, 2 * PAD))
    mine[part:, :] = tile
    for k, out in enumerate(outs):
        out[0:part, :] = total(pl.ds(pl.multiple_of((me ^ (k + 1)) * part, PAD), part)).astype(BF16)
        out[part:, :] = tile.astype(BF16)
    mine[0:part, :] = total(pl.ds(pl.multiple_of(me * part, PAD), part))


def sum_and_deal(base, got, bits):
    part = (base.shape[0] - 2 * PAD) // 4 + 2 * PAD
    vmem = pl.BlockSpec(memory_space=pltpu.VMEM)
    return pl.pallas_call(
        functools.partial(sum_kernel, bits, len(got)),
        out_shape=[pltpu.VMEM((part, LANES), F32)] + [pltpu.VMEM((part, LANES), BF16)] * 3,
        in_specs=[vmem] * (1 + len(got)),
        out_specs=[vmem] * 4,
        compiler_params=pltpu.CompilerParams(vmem_limit_bytes=16 * 1024 * 1024),
    )(base, *got)


def reduce_all(keep, send):
    got = swap(send, "tm", 1)
    rest = [("tm", bit) for bit in bits_of("tm")[1:]] + [("clip", bit) for bit in bits_of("clip")[4:]]
    rounds = ((1, 4), (4, 1))
    if rest:
        total = keep + got.astype(F32)
        total, tile = total[: -2 * PAD], total[-2 * PAD :].astype(BF16)
        for axis, bit in rest:
            total, tile = halve(total, axis, bit, tile)
        for bits in rounds:
            total, tile = quarter(total.reshape(4, -1, LANES), bits, tile)
    else:
        total, got = keep, [got]
        for bits in rounds:
            total, *outs = sum_and_deal(total, got, bits)
            got = [swap_by_core(out, ((k + 1) * bits[0], (k + 1) * bits[1])) for k, out in enumerate(outs)]
        for value in got:
            total = total + value.astype(F32)
        total, tile = total[: -2 * PAD], total[-2 * PAD :].astype(BF16)
    mine = total.astype(BF16)
    for bits in rounds[::-1]:
        mine = quadruple(mine, bits)
    for axis, bit in rest[::-1]:
        mine = double(mine, axis, bit)
    return mine, tile


def finish_kernel(own, *refs):
    if own:
        mine, tile, loss, scale_out, *outs = refs[:8]
        digits = tile[...].astype(F32)
        count = value_of(digits[PAD : PAD + 1])
        scale = 1.0 / count
        loss[0, 0] = value_of(digits[0:1]) / count
        scale_out[0, 0] = scale
    else:
        mine, scale_in, *outs = refs[:2] + refs[6:10]
        scale = scale_in[0, 0]
    staged, sems = refs[-2:]
    blocks, width = mine.shape[1], mine.shape[1] * LANES
    half = lax.rem(lax.axis_index("tm"), 2)
    half = half if own else 1 - half
    columns = pl.ds(pl.multiple_of(half * width, width), width)
    copies = []
    at = 0
    for n, out in enumerate(outs):
        m, rows = n // 2, out.shape[0]
        at = at if n % 2 else 0
        for j in range(blocks):
            staged[m, at : at + rows, j * LANES : (j + 1) * LANES] = mine[m, j, at : at + rows, :].astype(F32) * scale
        copy = pltpu.make_async_copy(staged.at[m, at : at + rows, :], out.at[:, columns], sems.at[n])
        copy.start()
        copies.append(copy)
        at += rows
    for copy in copies:
        copy.wait()


def finish(mine, tile, conv_rows, width):
    rows = conv_rows + width
    shape = (2, width // 2 // LANES, rows, LANES)
    got = swap(mine, "tm", 1)
    smem, vmem, hbm = (pl.BlockSpec(memory_space=space) for space in (pltpu.SMEM, pltpu.VMEM, pl.ANY))
    grads = [jax.ShapeDtypeStruct((n, width), F32) for n in (conv_rows, width) * 2]
    one = jax.ShapeDtypeStruct((1, 1), F32)
    scratch = [pltpu.VMEM((2, rows, width // 2), F32), pltpu.SemaphoreType.DMA((4,))]
    params = pltpu.CompilerParams(vmem_limit_bytes=16 * 1024 * 1024)
    cost = pl.CostEstimate(flops=rows * width, bytes_accessed=rows * width * 6, transcendentals=0)
    loss, scale, *outs = pl.pallas_call(
        functools.partial(finish_kernel, True),
        out_shape=[one, one] + grads,
        in_specs=[vmem, vmem],
        out_specs=[smem, smem] + [hbm] * 4,
        scratch_shapes=scratch,
        compiler_params=params,
        cost_estimate=cost,
    )(mine.reshape(shape), tile)
    outs = pl.pallas_call(
        functools.partial(finish_kernel, False),
        out_shape=grads,
        in_specs=[vmem, smem] + [hbm] * 4,
        out_specs=[hbm] * 4,
        scratch_shapes=scratch,
        input_output_aliases={n + 2: n for n in range(4)},
        compiler_params=params,
        cost_estimate=cost,
    )(got.reshape(shape), scale, *outs)
    return loss, outs


def shards(
    audio_feats, lip_feats, lengths, labels, w_audio_conv, w_audio_proj, w_lip_conv, w_lip_proj
):
    peers = lax.axis_size("tm")
    clips, frames, chan = audio_feats.shape
    halo = 0
    if peers == 2 and clips % 2 == 0:
        others = (1 - lax.axis_index("tm")) * (clips // 2)
        out = jnp.stack([lax.dynamic_slice_in_dim(x, others, clips // 2) for x in (audio_feats, lip_feats)])
        got = swap(out, "tm", 1)
    else:
        halo = HALO
        after = [(i, i + 1) for i in range(peers - 1)]
        before = [(i + 1, i) for i in range(peers - 1)]
        both = jnp.stack([audio_feats, lip_feats])
        audio_feats, lip_feats = jnp.concatenate(
            [
                lax.ppermute(both[:, :, -HALO:], "tm", after),
                both,
                lax.ppermute(both[:, :, :HALO], "tm", before),
            ],
            axis=2,
        )
        got = lengths.astype(BF16)
    keep, send = local_grads(
        halo, lengths, labels, audio_feats, lip_feats, got, w_audio_conv, w_audio_proj, w_lip_conv, w_lip_proj
    )
    mine, tile = reduce_all(keep, send)
    taps, chan, width = w_audio_conv.shape
    loss, (ac, ap, vc, vp) = finish(mine, tile, taps * chan, width)
    return (loss.reshape(()), ac.reshape(w_audio_conv.shape), ap, vc.reshape(w_lip_conv.shape), vp)


def solution(mesh):
    placed = (
        P("clip", "tm", None),
        P("clip", "tm", None),
        P("clip"),
        P("clip"),
        P(),
        P(),
        P(),
        P(),
    )
    return jax.shard_map(
        shards, mesh=mesh, in_specs=placed, out_specs=(P(), P(), P(), P(), P()), check_vma=False
    )
```

```python
import functools

import jax
import jax.numpy as jnp
from jax import lax
from jax.experimental import pallas as pl
from jax.experimental.pallas import tpu as pltpu
from jax.sharding import PartitionSpec as P

SPAN = 15
PAD = 16
TILE = 128
WIN = TILE + 2 * PAD
HALO = 64
TILES = 2 * PAD
LANES = 128
DIGITS = 48
FRACTION = 20

logit_sharpening_divisor = 10.0
loss_scale = 1024.0
epsilon = 1e-06

BF16 = jnp.bfloat16
F32 = jnp.float32


def dot(a, b, dims):
    return lax.dot_general(a, b, (dims, ((), ())), preferred_element_type=F32)


NN = ((1,), (0,))
NT = ((1,), (1,))
TN = ((0,), (0,))


def digit_weights(shape):
    lane = lax.broadcasted_iota(jnp.int32, shape, len(shape) - 1)
    return lane, jnp.exp2((lane - FRACTION).astype(F32))


def digits_of(value):
    lane, weight = digit_weights((1, LANES))
    size = jnp.abs(value)
    bits = jnp.floor(size / weight) - 2.0 * jnp.floor(size / (2.0 * weight))
    return jnp.where(lane < DIGITS, jnp.where(value < 0, -bits, bits), 0.0)


def value_of(digits):
    lane, weight = digit_weights(digits.shape)
    return jnp.sum(jnp.where(lane < DIGITS, digits * weight, 0.0))


def forward(feats, m, copies, w_conv, w_proj, cols, slope, hid, clips, frames, block, put):
    chan = feats.shape[-1]
    for copy in copies[0]:
        copy.wait()
    for c in range(clips):
        x = feats[m, c].astype(F32)
        row = lax.broadcasted_iota(jnp.int32, x.shape, 0)
        base = c * frames
        cols[base : base + frames, 0:chan] = jnp.where(row == 0, 0.0, pltpu.roll(x, 1, 0)).astype(BF16)
        cols[base : base + frames, chan : 2 * chan] = feats[m, c]
        cols[base : base + frames, 2 * chan : 3 * chan] = jnp.where(
            row == frames - 1, 0.0, pltpu.roll(x, frames - 1, 0)
        ).astype(BF16)
    for copy in copies[1]:
        copy.wait()

    def step(i, _):
        rows = pl.ds(pl.multiple_of(i * block, block), block)
        pre = dot(cols[rows, :], w_conv[...], NN)
        sigma = 0.5 * jnp.tanh(0.5 * pre) + 0.5
        hidden = (pre * sigma).astype(BF16)
        hid[rows, :] = hidden
        slope[rows, :] = sigma * (1.0 + pre * (1.0 - sigma))
        emb = dot(hidden, w_proj[...], NN).astype(BF16)
        values = emb.astype(F32)
        inv = lax.rsqrt(jnp.sum(values * values, axis=1, keepdims=True) + epsilon)
        put(i, emb, jnp.broadcast_to(inv, (block, LANES)))
        return 0

    lax.fori_loop(0, clips * frames // block, step, 0, unroll=True)


def backward(w_proj, cols, slope, hid, gemb, gpre, keep, send, block):
    def step(i, _):
        rows = pl.ds(pl.multiple_of(i * block, block), block)
        gpre[rows, :] = (dot(gemb[rows, :], w_proj[...], NT) * slope[rows, :]).astype(BF16)
        return 0

    lax.fori_loop(0, hid.shape[0] // block, step, 0, unroll=True)
    even = lax.rem(lax.axis_index("tm"), 2) == 0
    height = cols.shape[1] + hid.shape[1]
    start = 0
    for left, right in ((cols, gpre), (hid, gemb)):
        grad = dot(left[...], right[...], TN)
        rows, width = grad.shape[0], grad.shape[1] // 2
        mine = jnp.where(even, grad[:, :width], grad[:, width:])
        other = jnp.where(even, grad[:, width:], grad[:, :width])
        for j in range(width // LANES):
            at = j * height + start
            keep[at : at + rows, :] = mine[:, j * LANES : (j + 1) * LANES]
            send[at : at + rows, :] = other[:, j * LANES : (j + 1) * LANES].astype(BF16)
        start += rows


def kernel(
    frames, clips, halo, lengths, labels, own_a, own_v, got, wac_in, wap_in, wvc_in, wvp_in,
    keep, send, cols_a, slope_a, hid_a, gemb_a, cols_v, slope_v, hid_v, gemb_v, gpre, emb_a, emb_v, inv_a, inv_v, gacc, giacc, feats, wac, wap, wvc, wvp, sems,
):
    me = lax.axis_index("tm")
    rows_total = clips * frames
    start = me * (frames - 2 * halo) - halo if halo else 0
    first_clip = 0 if halo else me * clips
    block = block_of(frames)
    per_clip = frames // block

    copies = []

    def fetch(source, target):
        copy = pltpu.make_async_copy(source, target, sems.at[len(copies)])
        copy.start()
        copies.append(copy)
        return copy

    def fetch_feats(m, own):
        if halo:
            return [fetch(own, feats.at[m])]
        seg = own.shape[1]
        mine = pl.ds(pl.multiple_of(me * seg, seg), seg)
        other = pl.ds(pl.multiple_of((1 - me) * seg, seg), seg)
        started = []
        for c in range(clips):
            started.append(fetch(own.at[first_clip + c], feats.at[m, c, mine, :]))
            started.append(fetch(got.at[m, c], feats.at[m, c, other, :]))
        return started

    feats_v = fetch_feats(1, own_v)
    weights_v = [fetch(wvc_in, wvc), fetch(wvp_in, wvp)]
    feats_a = fetch_feats(0, own_a)
    weights_a = [fetch(wac_in, wac), fetch(wap_in, wap)]
    gacc[...] = jnp.zeros(gacc.shape, F32)
    giacc[...] = jnp.zeros(giacc.shape, F32)

    for c in range(clips):
        for lo in (0, PAD + frames):
            emb_a[c, lo : lo + PAD, :] = jnp.zeros((PAD, emb_a.shape[2]), BF16)
            inv_a[c, lo : lo + PAD, :] = jnp.zeros((PAD, LANES), F32)

    def put_a(i, emb, inv):
        c = i // per_clip
        at = pl.multiple_of(PAD + lax.rem(i, per_clip) * block, PAD)
        emb_a[c, pl.ds(at, block), :] = emb
        inv_a[c, pl.ds(at, block), :] = inv

    def put_v(i, emb, inv):
        at = pl.multiple_of(i * block, block)
        emb_v[pl.ds(at, block), :] = emb
        inv_v[pl.ds(at, block), :] = inv

    forward(feats, 1, (feats_v, weights_v), wvc, wvp, cols_v, slope_v, hid_v, clips, frames, block, put_v)
    forward(feats, 0, (feats_a, weights_a), wac, wap, cols_a, slope_a, hid_a, clips, frames, block, put_a)

    tiles = frames // TILE
    row = lax.broadcasted_iota(jnp.int32, (TILE, WIN), 0)
    col = lax.broadcasted_iota(jnp.int32, (TILE, WIN), 1)
    shift = col - row - PAD
    in_band = (shift >= -SPAN) & (shift <= SPAN)
    row_1 = lax.broadcasted_iota(jnp.int32, (TILE, 1), 0)

    def tile_step(i, loss):
        c = i // tiles
        first = pl.multiple_of(lax.rem(i, tiles) * TILE, TILE)
        length = lengths[first_clip + c]
        label = labels[first_clip + c]
        here = pl.ds(pl.multiple_of(i * TILE, TILE), TILE)
        window = pl.ds(first, WIN)
        ev = emb_v[here, :]
        wa = emb_a[c, window, :]
        iv = inv_v[here, 0:1]
        ia = inv_a[c, window, :].T
        dots = dot(ev, wa, NT)
        scores = logit_sharpening_divisor * dots * iv * ia
        t = start + first + row_1
        u = start + first - PAD + col
        inside = t < length
        valid = in_band & inside & (u >= 0) & (u < length)
        target = t + label
        counted = inside & (target >= 0) & (target < length)
        hit = shift == label
        weights = jnp.where(valid, jnp.exp(scores), 0.0)
        sums = jnp.where(inside, jnp.sum(weights, axis=1, keepdims=True), 1.0)
        picked = jnp.sum(jnp.where(hit, scores, 0.0), axis=1, keepdims=True)
        own = (first + row_1 >= halo) & (first + row_1 < frames - halo)
        loss = loss + jnp.sum(jnp.where(counted & own, jnp.log(sums) - picked, 0.0))
        scale = jnp.where(counted, logit_sharpening_divisor * loss_scale, 0.0)
        grad = scale * (weights / sums - jnp.where(hit, 1.0, 0.0))
        gd = (grad * iv * ia).astype(BF16)
        by_dots = grad * dots
        giv = jnp.sum(by_dots * ia, axis=1, keepdims=True)
        gia = jnp.sum((by_dots * iv).T, axis=1, keepdims=True)
        glip = dot(gd, wa, NN) - (iv * iv * iv * giv) * ev.astype(F32)
        gemb_v[here, :] = jnp.where(own, glip, 0.0).astype(BF16)
        gacc[c, window, :] += dot(gd, ev, TN)
        giacc[c, window, :] += jnp.broadcast_to(gia, (WIN, LANES))
        return loss

    loss = lax.fori_loop(0, clips * tiles, tile_step, jnp.zeros((), F32), unroll=clips * tiles <= 8)

    def audio_step(i, _):
        c = i // per_clip
        at = pl.ds(pl.multiple_of(PAD + lax.rem(i, per_clip) * block, PAD), block)
        inv = inv_a[c, at, 0:1]
        grad = gacc[c, at, :] - (inv * inv * inv * giacc[c, at, 0:1]) * emb_a[c, at, :].astype(F32)
        if halo:
            at_row = lax.rem(i, per_clip) * block + lax.broadcasted_iota(jnp.int32, (block, 1), 0)
            grad = jnp.where((at_row >= halo) & (at_row < frames - halo), grad, 0.0)
        gemb_a[pl.ds(pl.multiple_of(i * block, block), block), :] = grad.astype(BF16)
        return 0

    lax.fori_loop(0, rows_total // block, audio_step, 0)

    count = jnp.zeros((), F32)
    for c in range(clips):
        count = count + (lengths[first_clip + c] - jnp.abs(labels[first_clip + c])).astype(F32)
    if halo:
        count = jnp.where(me == 0, count, 0.0)
    send_rows = send.shape[0] - TILES
    for at, value in ((send_rows, loss), (send_rows + PAD, count)):
        digits = jnp.broadcast_to(digits_of(value), (PAD, LANES))
        keep[at : at + PAD, :] = digits
        send[at : at + PAD, :] = digits.astype(BF16)

    backward(wvp, cols_v, slope_v, hid_v, gemb_v, gpre, keep, send, block)


def block_of(frames):
    return next(n for n in (512, 256, TILE) if frames % n == 0)


def audio_kernel(block, w_proj, cols, slope, hid, gemb, keep, send, gpre):
    backward(w_proj, cols, slope, hid, gemb, gpre, keep, send, block)
    for ref in (keep, send):
        ref[ref.shape[0] - TILES :, :] = jnp.zeros((TILES, LANES), ref.dtype)


def local_grads(halo, lengths, labels, own_a, own_v, got, wac, wap, wvc, wvp):
    clips, frames, chan = own_a.shape
    if not halo:
        clips, frames = clips // 2, frames * 2
    width = wap.shape[0]
    rows = clips * frames
    taps = wac.shape[0]
    grad_rows = taps * chan + width
    wac = wac.reshape(taps * chan, width)
    wvc = wvc.reshape(taps * chan, width)
    blocks = width // 2 // LANES
    smem = pl.BlockSpec(memory_space=pltpu.SMEM)
    vmem = pl.BlockSpec(memory_space=pltpu.VMEM)
    hbm = pl.BlockSpec(memory_space=pl.ANY)
    sums = [pltpu.VMEM((blocks * grad_rows + TILES, LANES), dtype) for dtype in (F32, BF16)]
    saved = [
        pltpu.VMEM((rows, taps * chan), BF16),
        pltpu.VMEM((rows, width), F32),
        pltpu.VMEM((rows, width), BF16),
        pltpu.VMEM((rows, width), BF16),
    ]
    keep_v, send_v, *audio = pl.pallas_call(
        functools.partial(kernel, frames, clips, halo),
        out_shape=sums + saved,
        in_specs=[smem, smem, hbm, hbm, vmem] + [hbm] * 4,
        out_specs=[vmem] * 6,
        scratch_shapes=saved
        + [
            pltpu.VMEM((rows, width), BF16),
            pltpu.VMEM((clips, frames + 2 * PAD, width), BF16),
            pltpu.VMEM((rows, width), BF16),
            pltpu.VMEM((clips, frames + 2 * PAD, LANES), F32),
            pltpu.VMEM((rows, LANES), F32),
            pltpu.VMEM((clips, frames + 2 * PAD, width), F32),
            pltpu.VMEM((clips, frames + 2 * PAD, LANES), F32),
            pltpu.VMEM((2, clips, frames, chan), BF16),
            pltpu.VMEM((taps * chan, width), BF16),
            pltpu.VMEM((width, width), BF16),
            pltpu.VMEM((taps * chan, width), BF16),
            pltpu.VMEM((width, width), BF16),
            pltpu.SemaphoreType.DMA((4 * clips + 4,)),
        ],
        compiler_params=pltpu.CompilerParams(vmem_limit_bytes=48 * 1024 * 1024),
    )(lengths, labels, own_a, own_v, got, wac, wap, wvc, wvp)
    keep_a, send_a = pl.pallas_call(
        functools.partial(audio_kernel, block_of(frames)),
        out_shape=sums,
        in_specs=[vmem] * 5,
        out_specs=[vmem] * 2,
        scratch_shapes=[pltpu.VMEM((rows, width), BF16)],
        compiler_params=pltpu.CompilerParams(vmem_limit_bytes=32 * 1024 * 1024),
        cost_estimate=pl.CostEstimate(flops=2 * rows * width * (grad_rows + width), bytes_accessed=12 * rows * width, transcendentals=0),
    )(wap, *audio)
    return (keep_v, keep_a), (send_v, send_a)


def swap(value, axis, bit):
    return lax.ppermute(value, axis, [(i, i ^ bit) for i in range(lax.axis_size(axis))])


def swap_by_core(value, bits):
    peers = lax.axis_size("tm")
    pairs = []
    for clip in range(lax.axis_size("clip")):
        for tm in range(peers):
            pairs.append((clip * peers + tm, (clip ^ bits[tm % 2]) * peers + tm))
    return lax.ppermute(value, ("clip", "tm"), pairs)


def pick(value, index):
    return lax.dynamic_index_in_dim(value, index, 0, keepdims=False)


def halve(value, axis, bit, tile):
    me = (lax.axis_index(axis) // bit) % 2
    parts = value.reshape(2, -1, LANES)
    got = swap(jnp.concatenate([pick(parts, 1 - me).astype(BF16), tile]), axis, bit).astype(F32)
    rows = parts.shape[1]
    return pick(parts, me).astype(F32) + got[:rows], (tile.astype(F32) + got[rows:]).astype(BF16)


def double(value, axis, bit):
    me = (lax.axis_index(axis) // bit) % 2
    got = swap(value, axis, bit)
    return jnp.stack([jnp.where(me == 0, value, got), jnp.where(me == 0, got, value)]).reshape(-1, LANES)


def place_of(bits):
    clip, odd = lax.axis_index("clip"), lax.axis_index("tm") % 2
    return jnp.where(odd == 0, (clip // bits[0]) % 4, (clip // bits[1]) % 4)


def quarter(parts, bits, tile):
    me = place_of(bits)
    rows = parts.shape[1]
    mine = pick(parts, me).astype(F32)
    whole = tile.astype(F32)
    for k in (1, 2, 3):
        out = jnp.concatenate([pick(parts, me ^ k).astype(BF16), tile])
        got = swap_by_core(out, (k * bits[0], k * bits[1])).astype(F32)
        mine = mine + got[:rows]
        whole = whole + got[rows:]
    return mine, whole.astype(BF16)


def spread(value, bits):
    return [value] + [swap_by_core(value, (k * bits[0], k * bits[1])) for k in (1, 2, 3)]


def in_order(got, bits):
    me = place_of(bits)
    out = []
    for j in range(4):
        k = me ^ j
        out.append(jnp.where(k == 0, got[0], jnp.where(k == 1, got[1], jnp.where(k == 2, got[2], got[3]))))
    return jnp.stack(out).reshape(-1, LANES)


def bits_of(axis):
    size, bits = lax.axis_size(axis), []
    bit = 1
    while bit < size:
        bits.append(bit)
        bit *= 2
    return bits


def place_in_kernel(bits):
    clip, odd = lax.axis_index("clip"), lax.rem(lax.axis_index("tm"), 2)
    return jnp.where(odd == 0, lax.rem(clip // bits[0], 4), lax.rem(clip // bits[1], 4))


def place_kernel(bits, *refs):
    me = place_in_kernel(bits)
    out = refs[-1]
    part = out.shape[0] // 4
    for k in range(4):
        out[pl.ds(pl.multiple_of((me ^ k) * part, PAD), part), :] = refs[k][...]


def place(got, bits):
    vmem = pl.BlockSpec(memory_space=pltpu.VMEM)
    return pl.pallas_call(
        functools.partial(place_kernel, bits),
        out_shape=pltpu.VMEM((4 * got[0].shape[0], LANES), got[0].dtype),
        in_specs=[vmem] * 4,
        out_specs=vmem,
        compiler_params=pltpu.CompilerParams(vmem_limit_bytes=16 * 1024 * 1024),
    )(*got)


def sum_kernel(bits, counts, last, *refs):
    groups, at = [], 0
    for count in counts:
        groups.append(refs[at : at + 1 + count])
        at += 1 + count
    mine, *outs = refs[at:]

    def total(group, rows):
        value = group[0][rows, :]
        for ref in group[1:]:
            value = value + ref[rows, :].astype(F32)
        return value

    heights = [group[0].shape[0] - TILES for group in groups]
    tile = total(groups[0], pl.ds(heights[0], TILES))
    if last:
        mine[...] = total(groups[0], pl.ds(0, heights[0])).astype(BF16)
        outs[0][...] = tile.astype(BF16)
        return
    me = place_in_kernel(bits)
    for k, out in enumerate([mine] + outs):
        start = 0
        for group, height in zip(groups, heights):
            part = height // 4
            rows = pl.ds(pl.multiple_of((me ^ k) * part, PAD), part)
            out[start : start + part, :] = total(group, rows).astype(out.dtype)
            start += part
        out[start:, :] = tile.astype(out.dtype)


def sum_and_deal(groups, bits, last=False):
    heights = [group[0].shape[0] - TILES for group in groups]
    if last:
        shapes = [pltpu.VMEM((heights[0], LANES), BF16), pltpu.VMEM((TILES, LANES), BF16)]
    else:
        shapes = [pltpu.VMEM((sum(heights) // 4 + TILES, LANES), dtype) for dtype in (F32, BF16, BF16, BF16)]
    refs = [ref for group in groups for ref in group]
    vmem = pl.BlockSpec(memory_space=pltpu.VMEM)
    return pl.pallas_call(
        functools.partial(sum_kernel, bits, [len(group) - 1 for group in groups], last),
        out_shape=shapes,
        in_specs=[vmem] * len(refs),
        out_specs=[vmem] * len(shapes),
        compiler_params=pltpu.CompilerParams(vmem_limit_bytes=16 * 1024 * 1024),
    )(*refs)


def reduce_all(keep, send):
    gots = [swap(value, "tm", 1) for value in send]
    rest = [("tm", bit) for bit in bits_of("tm")[1:]] + [("clip", bit) for bit in bits_of("clip")[4:]]
    rounds = ((1, 4), (4, 1))
    if rest:
        mine, tiles = [], []
        for base, got in zip(keep, gots):
            total = base + got.astype(F32)
            total, tile = total[:-TILES], total[-TILES:].astype(BF16)
            for axis, bit in rest:
                total, tile = halve(total, axis, bit, tile)
            for bits in rounds:
                total, tile = quarter(total.reshape(4, -1, LANES), bits, tile)
            total = total.astype(BF16)
            for bits in rounds[::-1]:
                total = in_order(spread(total, bits), bits)
            for axis, bit in rest[::-1]:
                total = double(total, axis, bit)
            mine.append(total)
            tiles.append(tile)
        return mine, tiles[0]
    groups = []
    for base, got in zip(keep, gots):
        base, *outs = sum_and_deal([[base, got]], rounds[0])
        groups.append([base] + exchange(outs, rounds[0]))
    base, *outs = sum_and_deal(groups, rounds[1])
    mine, tile = sum_and_deal([[base] + exchange(outs, rounds[1])], None, last=True)
    mine = place(spread(mine, rounds[1]), rounds[1]).reshape(4, 2, -1, LANES)
    gots = [spread(mine[:, m].reshape(-1, LANES), rounds[0]) for m in (0, 1)]

    return [place(got, rounds[0]) for got in gots], tile


def exchange(outs, bits):
    return [swap_by_core(out, ((k + 1) * bits[0], (k + 1) * bits[1])) for k, out in enumerate(outs)]


def finish_kernel(own, rows, *refs):
    staged, sems = refs[-2:]
    if own:
        *halves, tile, loss = refs[:4]
    else:
        *halves, tile = refs[:3]
    outs = refs[-6:-2]
    digits = tile[...].astype(F32)
    count = value_of(digits[PAD : PAD + 1])
    scale = 1.0 / count
    if own:
        loss[0, 0] = value_of(digits[0:1]) / count
    blocks = halves[0].shape[0] // rows
    half = lax.rem(lax.axis_index("tm"), 2)
    half = half if own else 1 - half
    copies = []
    for m, mine in enumerate(halves):
        for j in range(blocks):
            at = j * rows
            column = pl.multiple_of((half * blocks + j) * LANES, LANES)
            for out in outs[2 * m : 2 * m + 2]:
                size = out.shape[0]
                staged[m, at : at + size, :] = mine[at : at + size, :].astype(F32) * scale
                copy = pltpu.make_async_copy(
                    staged.at[m, at : at + size, :], out.at[:, pl.ds(column, LANES)], sems.at[len(copies)]
                )
                copy.start()
                copies.append(copy)
                at += size
    for copy in copies:
        copy.wait()


def finish(halves, tile, conv_rows, width):
    gots = [swap(half, "tm", 1) for half in halves]
    smem, vmem, hbm = (pl.BlockSpec(memory_space=space) for space in (pltpu.SMEM, pltpu.VMEM, pl.ANY))
    grads = [jax.ShapeDtypeStruct((n, width), F32) for n in (conv_rows, width) * 2]
    rows = conv_rows + width
    scratch = [pltpu.VMEM((2, *halves[0].shape), F32), pltpu.SemaphoreType.DMA((4 * (halves[0].shape[0] // rows),))]
    params = pltpu.CompilerParams(vmem_limit_bytes=16 * 1024 * 1024)
    size = 2 * halves[0].size
    cost = pl.CostEstimate(flops=size, bytes_accessed=6 * size, transcendentals=0)
    loss, *outs = pl.pallas_call(
        functools.partial(finish_kernel, True, rows),
        out_shape=[jax.ShapeDtypeStruct((1, 1), F32)] + grads,
        in_specs=[vmem] * 3,
        out_specs=[smem] + [hbm] * 4,
        scratch_shapes=scratch,
        compiler_params=params,
        cost_estimate=cost,
    )(*halves, tile)
    outs = pl.pallas_call(
        functools.partial(finish_kernel, False, rows),
        out_shape=grads,
        in_specs=[vmem] * 3 + [hbm] * 4,
        out_specs=[hbm] * 4,
        scratch_shapes=scratch,
        input_output_aliases={n + 3: n for n in range(4)},
        compiler_params=params,
        cost_estimate=cost,
    )(*gots, tile, *outs)
    return loss, outs


def shards(
    audio_feats, lip_feats, lengths, labels, w_audio_conv, w_audio_proj, w_lip_conv, w_lip_proj
):
    peers = lax.axis_size("tm")
    clips, frames, chan = audio_feats.shape
    halo = 0
    if peers == 2 and clips % 2 == 0:
        others = (1 - lax.axis_index("tm")) * (clips // 2)
        out = jnp.stack([lax.dynamic_slice_in_dim(x, others, clips // 2) for x in (audio_feats, lip_feats)])
        got = swap(out, "tm", 1)
    else:
        halo = HALO
        after = [(i, i + 1) for i in range(peers - 1)]
        before = [(i + 1, i) for i in range(peers - 1)]
        both = jnp.stack([audio_feats, lip_feats])
        audio_feats, lip_feats = jnp.concatenate(
            [
                lax.ppermute(both[:, :, -HALO:], "tm", after),
                both,
                lax.ppermute(both[:, :, :HALO], "tm", before),
            ],
            axis=2,
        )
        got = lengths.astype(BF16)
    keep, send = local_grads(
        halo, lengths, labels, audio_feats, lip_feats, got, w_audio_conv, w_audio_proj, w_lip_conv, w_lip_proj
    )
    halves, tile = reduce_all(keep, send)
    taps, chan, width = w_audio_conv.shape
    loss, (vc, vp, ac, ap) = finish(halves, tile, taps * chan, width)
    return (loss.reshape(()), ac.reshape(w_audio_conv.shape), ap, vc.reshape(w_lip_conv.shape), vp)


def solution(mesh):
    placed = (
        P("clip", "tm", None),
        P("clip", "tm", None),
        P("clip"),
        P("clip"),
        P(),
        P(),
        P(),
        P(),
    )
    return jax.shard_map(
        shards, mesh=mesh, in_specs=placed, out_specs=(P(), P(), P(), P(), P()), check_vma=False
    )
```

```python
import functools

import jax
import jax.numpy as jnp
from jax import lax
from jax.experimental import pallas as pl
from jax.experimental.pallas import tpu as pltpu
from jax.sharding import PartitionSpec as P

SPAN = 15
PAD = 16
TILE = 128
WIN = TILE + 2 * PAD
HALO = 64
TILES = 2 * PAD
PLANS = (((1, 1), (4, 4)), ((1, 4), (4, 1)))
LANES = 128
DIGITS = 48
FRACTION = 20

logit_sharpening_divisor = 10.0
loss_scale = 1024.0
epsilon = 1e-06

BF16 = jnp.bfloat16
F32 = jnp.float32


def dot(a, b, dims):
    return lax.dot_general(a, b, (dims, ((), ())), preferred_element_type=F32)


NN = ((1,), (0,))
NT = ((1,), (1,))
TN = ((0,), (0,))


def digit_weights(shape):
    lane = lax.broadcasted_iota(jnp.int32, shape, len(shape) - 1)
    return lane, jnp.exp2((lane - FRACTION).astype(F32))


def digits_of(value):
    lane, weight = digit_weights((1, LANES))
    size = jnp.abs(value)
    bits = jnp.floor(size / weight) - 2.0 * jnp.floor(size / (2.0 * weight))
    return jnp.where(lane < DIGITS, jnp.where(value < 0, -bits, bits), 0.0)


def value_of(digits):
    lane, weight = digit_weights(digits.shape)
    return jnp.sum(jnp.where(lane < DIGITS, digits * weight, 0.0))


def forward(feats, m, copies, w_conv, w_proj, cols, slope, hid, clips, frames, block, put):
    chan = feats.shape[-1]
    for copy in copies[0]:
        copy.wait()
    for c in range(clips):
        x = feats[m, c].astype(F32)
        row = lax.broadcasted_iota(jnp.int32, x.shape, 0)
        base = c * frames
        cols[base : base + frames, 0:chan] = jnp.where(row == 0, 0.0, pltpu.roll(x, 1, 0)).astype(BF16)
        cols[base : base + frames, chan : 2 * chan] = feats[m, c]
        cols[base : base + frames, 2 * chan : 3 * chan] = jnp.where(
            row == frames - 1, 0.0, pltpu.roll(x, frames - 1, 0)
        ).astype(BF16)
    for copy in copies[1]:
        copy.wait()

    def step(i, _):
        rows = pl.ds(pl.multiple_of(i * block, block), block)
        pre = dot(cols[rows, :], w_conv[...], NN)
        sigma = 0.5 * jnp.tanh(0.5 * pre) + 0.5
        hidden = (pre * sigma).astype(BF16)
        hid[rows, :] = hidden
        slope[rows, :] = sigma * (1.0 + pre * (1.0 - sigma))
        emb = dot(hidden, w_proj[...], NN).astype(BF16)
        values = emb.astype(F32)
        inv = lax.rsqrt(jnp.sum(values * values, axis=1, keepdims=True) + epsilon)
        put(i, emb, jnp.broadcast_to(inv, (block, LANES)))
        return 0

    lax.fori_loop(0, clips * frames // block, step, 0, unroll=True)


def backward(w_proj, cols, slope, hid, gemb, gpre, keep, send, block):
    def step(i, _):
        rows = pl.ds(pl.multiple_of(i * block, block), block)
        gpre[rows, :] = (dot(gemb[rows, :], w_proj[...], NT) * slope[rows, :]).astype(BF16)
        return 0

    lax.fori_loop(0, hid.shape[0] // block, step, 0, unroll=True)
    even = lax.rem(lax.axis_index("tm"), 2) == 0
    height = cols.shape[1] + hid.shape[1]
    start = 0
    for left, right in ((cols, gpre), (hid, gemb)):
        grad = dot(left[...], right[...], TN)
        rows, width = grad.shape[0], grad.shape[1] // 2
        mine = jnp.where(even, grad[:, :width], grad[:, width:])
        other = jnp.where(even, grad[:, width:], grad[:, :width])
        for j in range(width // LANES):
            at = j * height + start
            keep[at : at + rows, :] = mine[:, j * LANES : (j + 1) * LANES]
            send[at : at + rows, :] = other[:, j * LANES : (j + 1) * LANES].astype(BF16)
        start += rows


def kernel(
    frames, clips, halo, lengths, labels, own_a, own_v, got, wac_in, wap_in, wvc_in, wvp_in,
    keep, send, cols_a, slope_a, hid_a, gemb_a, cols_v, slope_v, hid_v, gemb_v, gpre, emb_a, emb_v, inv_a, inv_v, gacc, giacc, feats, wac, wap, wvc, wvp, sems,
):
    me = lax.axis_index("tm")
    rows_total = clips * frames
    start = me * (frames - 2 * halo) - halo if halo else 0
    first_clip = 0 if halo else me * clips
    block = block_of(frames)
    per_clip = frames // block

    copies = []

    def fetch(source, target):
        copy = pltpu.make_async_copy(source, target, sems.at[len(copies)])
        copy.start()
        copies.append(copy)
        return copy

    def fetch_feats(m, own):
        if halo:
            return [fetch(own, feats.at[m])]
        seg = own.shape[1]
        mine = pl.ds(pl.multiple_of(me * seg, seg), seg)
        other = pl.ds(pl.multiple_of((1 - me) * seg, seg), seg)
        started = []
        for c in range(clips):
            started.append(fetch(own.at[first_clip + c], feats.at[m, c, mine, :]))
            started.append(fetch(got.at[m, c], feats.at[m, c, other, :]))
        return started

    feats_v = fetch_feats(1, own_v)
    weights_v = [fetch(wvc_in, wvc), fetch(wvp_in, wvp)]
    feats_a = fetch_feats(0, own_a)
    weights_a = [fetch(wac_in, wac), fetch(wap_in, wap)]
    gacc[...] = jnp.zeros(gacc.shape, F32)
    giacc[...] = jnp.zeros(giacc.shape, F32)

    for c in range(clips):
        for lo in (0, PAD + frames):
            emb_a[c, lo : lo + PAD, :] = jnp.zeros((PAD, emb_a.shape[2]), BF16)
            inv_a[c, lo : lo + PAD, :] = jnp.zeros((PAD, LANES), F32)

    def put_a(i, emb, inv):
        c = i // per_clip
        at = pl.multiple_of(PAD + lax.rem(i, per_clip) * block, PAD)
        emb_a[c, pl.ds(at, block), :] = emb
        inv_a[c, pl.ds(at, block), :] = inv

    def put_v(i, emb, inv):
        at = pl.multiple_of(i * block, block)
        emb_v[pl.ds(at, block), :] = emb
        inv_v[pl.ds(at, block), :] = inv

    forward(feats, 1, (feats_v, weights_v), wvc, wvp, cols_v, slope_v, hid_v, clips, frames, block, put_v)
    forward(feats, 0, (feats_a, weights_a), wac, wap, cols_a, slope_a, hid_a, clips, frames, block, put_a)

    tiles = frames // TILE
    row = lax.broadcasted_iota(jnp.int32, (TILE, WIN), 0)
    col = lax.broadcasted_iota(jnp.int32, (TILE, WIN), 1)
    shift = col - row - PAD
    in_band = (shift >= -SPAN) & (shift <= SPAN)
    row_1 = lax.broadcasted_iota(jnp.int32, (TILE, 1), 0)

    def tile_step(i, loss):
        c = i // tiles
        first = pl.multiple_of(lax.rem(i, tiles) * TILE, TILE)
        length = lengths[first_clip + c]
        label = labels[first_clip + c]
        here = pl.ds(pl.multiple_of(i * TILE, TILE), TILE)
        window = pl.ds(first, WIN)
        ev = emb_v[here, :]
        wa = emb_a[c, window, :]
        iv = inv_v[here, 0:1]
        ia = inv_a[c, window, :].T
        dots = dot(ev, wa, NT)
        scores = logit_sharpening_divisor * dots * iv * ia
        t = start + first + row_1
        u = start + first - PAD + col
        inside = t < length
        valid = in_band & inside & (u >= 0) & (u < length)
        target = t + label
        counted = inside & (target >= 0) & (target < length)
        hit = shift == label
        weights = jnp.where(valid, jnp.exp(scores), 0.0)
        sums = jnp.where(inside, jnp.sum(weights, axis=1, keepdims=True), 1.0)
        picked = jnp.sum(jnp.where(hit, scores, 0.0), axis=1, keepdims=True)
        own = (first + row_1 >= halo) & (first + row_1 < frames - halo)
        loss = loss + jnp.sum(jnp.where(counted & own, jnp.log(sums) - picked, 0.0))
        scale = jnp.where(counted, logit_sharpening_divisor * loss_scale, 0.0)
        grad = scale * (weights / sums - jnp.where(hit, 1.0, 0.0))
        gd = (grad * iv * ia).astype(BF16)
        by_dots = grad * dots
        giv = jnp.sum(by_dots * ia, axis=1, keepdims=True)
        gia = jnp.sum((by_dots * iv).T, axis=1, keepdims=True)
        glip = dot(gd, wa, NN) - (iv * iv * iv * giv) * ev.astype(F32)
        gemb_v[here, :] = jnp.where(own, glip, 0.0).astype(BF16)
        gacc[c, window, :] += dot(gd, ev, TN)
        giacc[c, window, :] += jnp.broadcast_to(gia, (WIN, LANES))
        return loss

    loss = lax.fori_loop(0, clips * tiles, tile_step, jnp.zeros((), F32), unroll=clips * tiles <= 8)

    def audio_step(i, _):
        c = i // per_clip
        at = pl.ds(pl.multiple_of(PAD + lax.rem(i, per_clip) * block, PAD), block)
        inv = inv_a[c, at, 0:1]
        grad = gacc[c, at, :] - (inv * inv * inv * giacc[c, at, 0:1]) * emb_a[c, at, :].astype(F32)
        if halo:
            at_row = lax.rem(i, per_clip) * block + lax.broadcasted_iota(jnp.int32, (block, 1), 0)
            grad = jnp.where((at_row >= halo) & (at_row < frames - halo), grad, 0.0)
        gemb_a[pl.ds(pl.multiple_of(i * block, block), block), :] = grad.astype(BF16)
        return 0

    lax.fori_loop(0, rows_total // block, audio_step, 0)

    count = jnp.zeros((), F32)
    for c in range(clips):
        count = count + (lengths[first_clip + c] - jnp.abs(labels[first_clip + c])).astype(F32)
    if halo:
        count = jnp.where(me == 0, count, 0.0)
    send_rows = send.shape[0] - TILES
    for at, value in ((send_rows, loss), (send_rows + PAD, count)):
        digits = jnp.broadcast_to(digits_of(value), (PAD, LANES))
        keep[at : at + PAD, :] = digits
        send[at : at + PAD, :] = digits.astype(BF16)

    backward(wvp, cols_v, slope_v, hid_v, gemb_v, gpre, keep, send, block)


def block_of(frames):
    return next(n for n in (512, 256, TILE) if frames % n == 0)


def audio_kernel(block, w_proj, cols, slope, hid, gemb, keep, send, gpre):
    backward(w_proj, cols, slope, hid, gemb, gpre, keep, send, block)
    for ref in (keep, send):
        ref[ref.shape[0] - TILES :, :] = jnp.zeros((TILES, LANES), ref.dtype)


def local_grads(halo, lengths, labels, own_a, own_v, got, wac, wap, wvc, wvp):
    clips, frames, chan = own_a.shape
    if not halo:
        clips, frames = clips // 2, frames * 2
    width = wap.shape[0]
    rows = clips * frames
    taps = wac.shape[0]
    grad_rows = taps * chan + width
    wac = wac.reshape(taps * chan, width)
    wvc = wvc.reshape(taps * chan, width)
    blocks = width // 2 // LANES
    smem = pl.BlockSpec(memory_space=pltpu.SMEM)
    vmem = pl.BlockSpec(memory_space=pltpu.VMEM)
    hbm = pl.BlockSpec(memory_space=pl.ANY)
    sums = [pltpu.VMEM((blocks * grad_rows + TILES, LANES), dtype) for dtype in (F32, BF16)]
    saved = [
        pltpu.VMEM((rows, taps * chan), BF16),
        pltpu.VMEM((rows, width), F32),
        pltpu.VMEM((rows, width), BF16),
        pltpu.VMEM((rows, width), BF16),
    ]
    keep_v, send_v, *audio = pl.pallas_call(
        functools.partial(kernel, frames, clips, halo),
        out_shape=sums + saved,
        in_specs=[smem, smem, hbm, hbm, vmem] + [hbm] * 4,
        out_specs=[vmem] * 6,
        scratch_shapes=saved
        + [
            pltpu.VMEM((rows, width), BF16),
            pltpu.VMEM((clips, frames + 2 * PAD, width), BF16),
            pltpu.VMEM((rows, width), BF16),
            pltpu.VMEM((clips, frames + 2 * PAD, LANES), F32),
            pltpu.VMEM((rows, LANES), F32),
            pltpu.VMEM((clips, frames + 2 * PAD, width), F32),
            pltpu.VMEM((clips, frames + 2 * PAD, LANES), F32),
            pltpu.VMEM((2, clips, frames, chan), BF16),
            pltpu.VMEM((taps * chan, width), BF16),
            pltpu.VMEM((width, width), BF16),
            pltpu.VMEM((taps * chan, width), BF16),
            pltpu.VMEM((width, width), BF16),
            pltpu.SemaphoreType.DMA((4 * clips + 4,)),
        ],
        compiler_params=pltpu.CompilerParams(vmem_limit_bytes=44 * 1024 * 1024),
    )(lengths, labels, own_a, own_v, got, wac, wap, wvc, wvp)
    keep_a, send_a = pl.pallas_call(
        functools.partial(audio_kernel, block_of(frames)),
        out_shape=sums,
        in_specs=[vmem] * 5,
        out_specs=[vmem] * 2,
        scratch_shapes=[pltpu.VMEM((rows, width), BF16)],
        compiler_params=pltpu.CompilerParams(vmem_limit_bytes=32 * 1024 * 1024),
        cost_estimate=pl.CostEstimate(flops=2 * rows * width * (grad_rows + width), bytes_accessed=12 * rows * width, transcendentals=0),
    )(wap, *audio)
    return (keep_v, keep_a), (send_v, send_a)


def swap(value, axis, bit):
    return lax.ppermute(value, axis, [(i, i ^ bit) for i in range(lax.axis_size(axis))])


def swap_by_core(value, bits):
    peers = lax.axis_size("tm")
    pairs = []
    for clip in range(lax.axis_size("clip")):
        for tm in range(peers):
            pairs.append((clip * peers + tm, (clip ^ bits[tm % 2]) * peers + tm))
    return lax.ppermute(value, ("clip", "tm"), pairs)


def pick(value, index):
    return lax.dynamic_index_in_dim(value, index, 0, keepdims=False)


def halve(value, axis, bit, tile):
    me = (lax.axis_index(axis) // bit) % 2
    parts = value.reshape(2, -1, LANES)
    got = swap(jnp.concatenate([pick(parts, 1 - me).astype(BF16), tile]), axis, bit).astype(F32)
    rows = parts.shape[1]
    return pick(parts, me).astype(F32) + got[:rows], (tile.astype(F32) + got[rows:]).astype(BF16)


def double(value, axis, bit):
    me = (lax.axis_index(axis) // bit) % 2
    got = swap(value, axis, bit)
    return jnp.stack([jnp.where(me == 0, value, got), jnp.where(me == 0, got, value)]).reshape(-1, LANES)


def place_of(bits):
    clip, odd = lax.axis_index("clip"), lax.axis_index("tm") % 2
    return jnp.where(odd == 0, (clip // bits[0]) % 4, (clip // bits[1]) % 4)


def quarter(parts, bits, tile):
    me = place_of(bits)
    rows = parts.shape[1]
    mine = pick(parts, me).astype(F32)
    whole = tile.astype(F32)
    for k in (1, 2, 3):
        out = jnp.concatenate([pick(parts, me ^ k).astype(BF16), tile])
        got = swap_by_core(out, (k * bits[0], k * bits[1])).astype(F32)
        mine = mine + got[:rows]
        whole = whole + got[rows:]
    return mine, whole.astype(BF16)


def spread(value, bits):
    return [value] + [swap_by_core(value, (k * bits[0], k * bits[1])) for k in (1, 2, 3)]


def in_order(got, bits):
    me = place_of(bits)
    out = []
    for j in range(4):
        k = me ^ j
        out.append(jnp.where(k == 0, got[0], jnp.where(k == 1, got[1], jnp.where(k == 2, got[2], got[3]))))
    return jnp.stack(out).reshape(-1, LANES)


def bits_of(axis):
    size, bits = lax.axis_size(axis), []
    bit = 1
    while bit < size:
        bits.append(bit)
        bit *= 2
    return bits


def place_in_kernel(bits):
    clip, odd = lax.axis_index("clip"), lax.rem(lax.axis_index("tm"), 2)
    return jnp.where(odd == 0, lax.rem(clip // bits[0], 4), lax.rem(clip // bits[1], 4))


def place_kernel(bits, *refs):
    me = place_in_kernel(bits)
    out = refs[-1]
    part = out.shape[0] // 4
    for k in range(4):
        out[pl.ds(pl.multiple_of((me ^ k) * part, PAD), part), :] = refs[k][...]


def place(got, bits):
    vmem = pl.BlockSpec(memory_space=pltpu.VMEM)
    return pl.pallas_call(
        functools.partial(place_kernel, bits),
        out_shape=pltpu.VMEM((4 * got[0].shape[0], LANES), got[0].dtype),
        in_specs=[vmem] * 4,
        out_specs=vmem,
        compiler_params=pltpu.CompilerParams(vmem_limit_bytes=16 * 1024 * 1024),
    )(*got)


def deal_kernel(bits, base, got, mine, *outs):
    me = place_in_kernel(bits)
    part = mine.shape[0] - TILES

    def total(rows):
        return base[rows, :] + got[rows, :].astype(F32)

    tile = total(pl.ds(4 * part, TILES))
    for k, out in enumerate((mine, *outs)):
        rows = pl.ds(pl.multiple_of((me ^ k) * part, PAD), part)
        out[0:part, :] = total(rows).astype(out.dtype)
        out[part:, :] = tile.astype(out.dtype)


def join_kernel(base, *refs):
    value = base[...]
    for ref in refs[:-1]:
        value = value + ref[...].astype(F32)
    refs[-1][...] = value.astype(BF16)


def split_kernel(one, other, *outs):
    start = 0
    for out in outs:
        rows = pl.ds(start, out.shape[0])
        out[...] = (one[rows, :].astype(F32) + other[rows, :].astype(F32)).astype(BF16)
        start += out.shape[0]


def on_chip(body, shapes, *args):
    vmem = pl.BlockSpec(memory_space=pltpu.VMEM)
    return pl.pallas_call(
        body,
        out_shape=[pltpu.VMEM((rows, LANES), dtype) for rows, dtype in shapes],
        in_specs=[vmem] * len(args),
        out_specs=[vmem] * len(shapes),
        compiler_params=pltpu.CompilerParams(vmem_limit_bytes=16 * 1024 * 1024),
    )(*args)


def reduce_all(keep, send):
    gots = [swap(value, "tm", 1) for value in send]
    rest = [("tm", bit) for bit in bits_of("tm")[1:]] + [("clip", bit) for bit in bits_of("clip")[4:]]
    rounds = ((1, 4), (4, 1))
    if rest:
        mine, tiles = [], []
        for base, got in zip(keep, gots):
            total = base + got.astype(F32)
            total, tile = total[:-TILES], total[-TILES:].astype(BF16)
            for axis, bit in rest:
                total, tile = halve(total, axis, bit, tile)
            for bits in rounds:
                total, tile = quarter(total.reshape(4, -1, LANES), bits, tile)
            total = total.astype(BF16)
            for bits in rounds[::-1]:
                total = in_order(spread(total, bits), bits)
            for axis, bit in rest[::-1]:
                total = double(total, axis, bit)
            mine.append(total)
            tiles.append(tile)
        return mine, tiles[0]
    mine, tiles = [], []
    for base, got, (groups, pairs) in zip(keep, gots, PLANS):
        part = (base.shape[0] - TILES) // 4 + TILES
        shapes = [(part, F32)] + [(part, BF16)] * 3
        base, *outs = on_chip(functools.partial(deal_kernel, groups), shapes, base, got)
        (value,) = on_chip(join_kernel, [(part, BF16)], base, *exchange(outs, groups))
        twice = tuple(2 * bit for bit in pairs)
        (value,) = on_chip(split_kernel, [(part, BF16)], value, swap_by_core(value, pairs))
        value, tile = on_chip(split_kernel, [(part - TILES, BF16), (TILES, BF16)], value, swap_by_core(value, twice))
        mine.append(value)
        tiles.append(tile)
    return [place(spread(value, plan[0]), plan[0]) for value, plan in zip(mine, PLANS)], tiles[0]


def exchange(outs, bits):
    return [swap_by_core(out, ((k + 1) * bits[0], (k + 1) * bits[1])) for k, out in enumerate(outs)]


def finish_kernel(own, rows, *refs):
    staged, sems = refs[-2:]
    if own:
        *halves, tile, loss = refs[:4]
    else:
        *halves, tile = refs[:3]
    outs = refs[-6:-2]
    digits = tile[...].astype(F32)
    count = value_of(digits[PAD : PAD + 1])
    scale = 1.0 / count
    if own:
        loss[0, 0] = value_of(digits[0:1]) / count
    blocks = halves[0].shape[0] // rows
    half = lax.rem(lax.axis_index("tm"), 2)
    half = half if own else 1 - half
    copies = []
    for m, mine in enumerate(halves):
        for j in range(blocks):
            at = j * rows
            column = pl.multiple_of((half * blocks + j) * LANES, LANES)
            for out in outs[2 * m : 2 * m + 2]:
                size = out.shape[0]
                staged[m, at : at + size, :] = mine[at : at + size, :].astype(F32) * scale
                copy = pltpu.make_async_copy(
                    staged.at[m, at : at + size, :], out.at[:, pl.ds(column, LANES)], sems.at[len(copies)]
                )
                copy.start()
                copies.append(copy)
                at += size
    for copy in copies:
        copy.wait()


def finish(halves, tile, conv_rows, width):
    gots = [swap(half, "tm", 1) for half in halves]
    smem, vmem, hbm = (pl.BlockSpec(memory_space=space) for space in (pltpu.SMEM, pltpu.VMEM, pl.ANY))
    grads = [jax.ShapeDtypeStruct((n, width), F32) for n in (conv_rows, width) * 2]
    rows = conv_rows + width
    scratch = [pltpu.VMEM((2, *halves[0].shape), F32), pltpu.SemaphoreType.DMA((4 * (halves[0].shape[0] // rows),))]
    params = pltpu.CompilerParams(vmem_limit_bytes=16 * 1024 * 1024)
    size = 2 * halves[0].size
    cost = pl.CostEstimate(flops=size, bytes_accessed=6 * size, transcendentals=0)
    loss, *outs = pl.pallas_call(
        functools.partial(finish_kernel, True, rows),
        out_shape=[jax.ShapeDtypeStruct((1, 1), F32)] + grads,
        in_specs=[vmem] * 3,
        out_specs=[smem] + [hbm] * 4,
        scratch_shapes=scratch,
        compiler_params=params,
        cost_estimate=cost,
    )(*halves, tile)
    outs = pl.pallas_call(
        functools.partial(finish_kernel, False, rows),
        out_shape=grads,
        in_specs=[vmem] * 3 + [hbm] * 4,
        out_specs=[hbm] * 4,
        scratch_shapes=scratch,
        input_output_aliases={n + 3: n for n in range(4)},
        compiler_params=params,
        cost_estimate=cost,
    )(*gots, tile, *outs)
    return loss, outs


def shards(
    audio_feats, lip_feats, lengths, labels, w_audio_conv, w_audio_proj, w_lip_conv, w_lip_proj
):
    peers = lax.axis_size("tm")
    clips, frames, chan = audio_feats.shape
    halo = 0
    if peers == 2 and clips % 2 == 0:
        others = (1 - lax.axis_index("tm")) * (clips // 2)
        out = jnp.stack([lax.dynamic_slice_in_dim(x, others, clips // 2) for x in (audio_feats, lip_feats)])
        got = swap(out, "tm", 1)
    else:
        halo = HALO
        after = [(i, i + 1) for i in range(peers - 1)]
        before = [(i + 1, i) for i in range(peers - 1)]
        both = jnp.stack([audio_feats, lip_feats])
        audio_feats, lip_feats = jnp.concatenate(
            [
                lax.ppermute(both[:, :, -HALO:], "tm", after),
                both,
                lax.ppermute(both[:, :, :HALO], "tm", before),
            ],
            axis=2,
        )
        got = lengths.astype(BF16)
    keep, send = local_grads(
        halo, lengths, labels, audio_feats, lip_feats, got, w_audio_conv, w_audio_proj, w_lip_conv, w_lip_proj
    )
    halves, tile = reduce_all(keep, send)
    taps, chan, width = w_audio_conv.shape
    loss, (vc, vp, ac, ap) = finish(halves, tile, taps * chan, width)
    return (loss.reshape(()), ac.reshape(w_audio_conv.shape), ap, vc.reshape(w_lip_conv.shape), vp)


def solution(mesh):
    placed = (
        P("clip", "tm", None),
        P("clip", "tm", None),
        P("clip"),
        P("clip"),
        P(),
        P(),
        P(),
        P(),
    )
    return jax.shard_map(
        shards, mesh=mesh, in_specs=placed, out_specs=(P(), P(), P(), P(), P()), check_vma=False
    )
```

```python
import functools

import jax
import jax.numpy as jnp
from jax import lax
from jax.experimental import pallas as pl
from jax.experimental.pallas import tpu as pltpu
from jax.sharding import PartitionSpec as P

SPAN = 15
PAD = 16
TILE = 128
WIN = TILE + 2 * PAD
HALO = 64
TILES = 2 * PAD
SLAB = 256
GROUPS = (((0, True), (1, True)), ((0, False), (1, False)))
PLANS = (((1, 1), (4, 8), (8, 4)), ((1, 4), (4, 1), (8, 2)))
LANES = 128
DIGITS = 48
FRACTION = 20

logit_sharpening_divisor = 10.0
loss_scale = 1024.0
epsilon = 1e-06

BF16 = jnp.bfloat16
F32 = jnp.float32


def dot(a, b, dims):
    return lax.dot_general(a, b, (dims, ((), ())), preferred_element_type=F32)


NN = ((1,), (0,))
NT = ((1,), (1,))
TN = ((0,), (0,))


def digit_weights(shape):
    lane = lax.broadcasted_iota(jnp.int32, shape, len(shape) - 1)
    return lane, jnp.exp2((lane - FRACTION).astype(F32))


def digits_of(value):
    lane, weight = digit_weights((1, LANES))
    size = jnp.abs(value)
    bits = jnp.floor(size / weight) - 2.0 * jnp.floor(size / (2.0 * weight))
    return jnp.where(lane < DIGITS, jnp.where(value < 0, -bits, bits), 0.0)


def value_of(digits):
    lane, weight = digit_weights(digits.shape)
    return jnp.sum(jnp.where(lane < DIGITS, digits * weight, 0.0))


def forward(feats, m, copies, w_conv, w_proj, cols, slope, hid, clips, frames, block, put):
    chan = feats.shape[-1]
    for copy in copies[0]:
        copy.wait()
    for c in range(clips):
        x = feats[m, c].astype(F32)
        row = lax.broadcasted_iota(jnp.int32, x.shape, 0)
        base = c * frames
        cols[base : base + frames, 0:chan] = jnp.where(row == 0, 0.0, pltpu.roll(x, 1, 0)).astype(BF16)
        cols[base : base + frames, chan : 2 * chan] = feats[m, c]
        cols[base : base + frames, 2 * chan : 3 * chan] = jnp.where(
            row == frames - 1, 0.0, pltpu.roll(x, frames - 1, 0)
        ).astype(BF16)
    for copy in copies[1]:
        copy.wait()

    def step(i, _):
        rows = pl.ds(pl.multiple_of(i * block, block), block)
        pre = dot(cols[rows, :], w_conv[...], NN)
        sigma = 0.5 * jnp.tanh(0.5 * pre) + 0.5
        hidden = (pre * sigma).astype(BF16)
        hid[rows, :] = hidden
        slope[rows, :] = sigma * (1.0 + pre * (1.0 - sigma))
        emb = dot(hidden, w_proj[...], NN).astype(BF16)
        values = emb.astype(F32)
        inv = lax.rsqrt(jnp.sum(values * values, axis=1, keepdims=True) + epsilon)
        put(i, emb, jnp.broadcast_to(inv, (block, LANES)))
        return 0

    lax.fori_loop(0, clips * frames // block, step, 0, unroll=True)


def backward(w_proj, cols, slope, hid, gemb, gpre, keep, send, block):
    def step(i, _):
        rows = pl.ds(pl.multiple_of(i * block, block), block)
        gpre[rows, :] = (dot(gemb[rows, :], w_proj[...], NT) * slope[rows, :]).astype(BF16)
        return 0

    lax.fori_loop(0, hid.shape[0] // block, step, 0, unroll=True)
    even = lax.rem(lax.axis_index("tm"), 2) == 0
    height = cols.shape[1] + hid.shape[1]
    start = 0
    for left, right in ((cols, gpre), (hid, gemb)):
        grad = dot(left[...], right[...], TN)
        rows, width = grad.shape[0], grad.shape[1] // 2
        mine = jnp.where(even, grad[:, :width], grad[:, width:])
        other = jnp.where(even, grad[:, width:], grad[:, :width])
        for j in range(width // LANES):
            at = j * height + start
            keep[at : at + rows, :] = mine[:, j * LANES : (j + 1) * LANES]
            send[at : at + rows, :] = other[:, j * LANES : (j + 1) * LANES].astype(BF16)
        start += rows


def kernel(
    frames, clips, halo, lengths, labels, own_a, own_v, got, wac_in, wap_in, wvc_in, wvp_in,
    keep, send, cols_a, slope_a, hid_a, gemb_a, cols_v, slope_v, hid_v, gemb_v, gpre, emb_a, emb_v, inv_a, inv_v, gacc, giacc, feats, wac, wap, wvc, wvp, sems,
):
    me = lax.axis_index("tm")
    rows_total = clips * frames
    start = me * (frames - 2 * halo) - halo if halo else 0
    first_clip = 0 if halo else me * clips
    block = block_of(frames)
    per_clip = frames // block

    copies = []

    def fetch(source, target):
        copy = pltpu.make_async_copy(source, target, sems.at[len(copies)])
        copy.start()
        copies.append(copy)
        return copy

    def fetch_feats(m, own):
        if halo:
            return [fetch(own, feats.at[m])]
        seg = own.shape[1]
        mine = pl.ds(pl.multiple_of(me * seg, seg), seg)
        other = pl.ds(pl.multiple_of((1 - me) * seg, seg), seg)
        started = []
        for c in range(clips):
            started.append(fetch(own.at[first_clip + c], feats.at[m, c, mine, :]))
            started.append(fetch(got.at[m, c], feats.at[m, c, other, :]))
        return started

    feats_v = fetch_feats(1, own_v)
    weights_v = [fetch(wvc_in, wvc), fetch(wvp_in, wvp)]
    feats_a = fetch_feats(0, own_a)
    weights_a = [fetch(wac_in, wac), fetch(wap_in, wap)]
    gacc[...] = jnp.zeros(gacc.shape, F32)
    giacc[...] = jnp.zeros(giacc.shape, F32)

    for c in range(clips):
        for lo in (0, PAD + frames):
            emb_a[c, lo : lo + PAD, :] = jnp.zeros((PAD, emb_a.shape[2]), BF16)
            inv_a[c, lo : lo + PAD, :] = jnp.zeros((PAD, LANES), F32)

    def put_a(i, emb, inv):
        c = i // per_clip
        at = pl.multiple_of(PAD + lax.rem(i, per_clip) * block, PAD)
        emb_a[c, pl.ds(at, block), :] = emb
        inv_a[c, pl.ds(at, block), :] = inv

    def put_v(i, emb, inv):
        at = pl.multiple_of(i * block, block)
        emb_v[pl.ds(at, block), :] = emb
        inv_v[pl.ds(at, block), :] = inv

    forward(feats, 1, (feats_v, weights_v), wvc, wvp, cols_v, slope_v, hid_v, clips, frames, block, put_v)
    forward(feats, 0, (feats_a, weights_a), wac, wap, cols_a, slope_a, hid_a, clips, frames, block, put_a)

    tiles = frames // TILE
    row = lax.broadcasted_iota(jnp.int32, (TILE, WIN), 0)
    col = lax.broadcasted_iota(jnp.int32, (TILE, WIN), 1)
    shift = col - row - PAD
    in_band = (shift >= -SPAN) & (shift <= SPAN)
    row_1 = lax.broadcasted_iota(jnp.int32, (TILE, 1), 0)

    def tile_step(i, loss):
        c = i // tiles
        first = pl.multiple_of(lax.rem(i, tiles) * TILE, TILE)
        length = lengths[first_clip + c]
        label = labels[first_clip + c]
        here = pl.ds(pl.multiple_of(i * TILE, TILE), TILE)
        window = pl.ds(first, WIN)
        ev = emb_v[here, :]
        wa = emb_a[c, window, :]
        iv = inv_v[here, 0:1]
        ia = inv_a[c, window, :].T
        dots = dot(ev, wa, NT)
        scores = logit_sharpening_divisor * dots * iv * ia
        t = start + first + row_1
        u = start + first - PAD + col
        inside = t < length
        valid = in_band & inside & (u >= 0) & (u < length)
        target = t + label
        counted = inside & (target >= 0) & (target < length)
        hit = shift == label
        weights = jnp.where(valid, jnp.exp(scores), 0.0)
        sums = jnp.where(inside, jnp.sum(weights, axis=1, keepdims=True), 1.0)
        picked = jnp.sum(jnp.where(hit, scores, 0.0), axis=1, keepdims=True)
        own = (first + row_1 >= halo) & (first + row_1 < frames - halo)
        loss = loss + jnp.sum(jnp.where(counted & own, jnp.log(sums) - picked, 0.0))
        scale = jnp.where(counted, logit_sharpening_divisor * loss_scale, 0.0)
        grad = scale * (weights / sums - jnp.where(hit, 1.0, 0.0))
        gd = (grad * iv * ia).astype(BF16)
        by_dots = grad * dots
        giv = jnp.sum(by_dots * ia, axis=1, keepdims=True)
        gia = jnp.sum((by_dots * iv).T, axis=1, keepdims=True)
        glip = dot(gd, wa, NN) - (iv * iv * iv * giv) * ev.astype(F32)
        gemb_v[here, :] = jnp.where(own, glip, 0.0).astype(BF16)
        gacc[c, window, :] += dot(gd, ev, TN)
        giacc[c, window, :] += jnp.broadcast_to(gia, (WIN, LANES))
        return loss

    loss = lax.fori_loop(0, clips * tiles, tile_step, jnp.zeros((), F32), unroll=clips * tiles <= 8)

    def audio_step(i, _):
        c = i // per_clip
        at = pl.ds(pl.multiple_of(PAD + lax.rem(i, per_clip) * block, PAD), block)
        inv = inv_a[c, at, 0:1]
        grad = gacc[c, at, :] - (inv * inv * inv * giacc[c, at, 0:1]) * emb_a[c, at, :].astype(F32)
        if halo:
            at_row = lax.rem(i, per_clip) * block + lax.broadcasted_iota(jnp.int32, (block, 1), 0)
            grad = jnp.where((at_row >= halo) & (at_row < frames - halo), grad, 0.0)
        gemb_a[pl.ds(pl.multiple_of(i * block, block), block), :] = grad.astype(BF16)
        return 0

    lax.fori_loop(0, rows_total // block, audio_step, 0)

    count = jnp.zeros((), F32)
    for c in range(clips):
        count = count + (lengths[first_clip + c] - jnp.abs(labels[first_clip + c])).astype(F32)
    if halo:
        count = jnp.where(me == 0, count, 0.0)
    send_rows = send.shape[0] - TILES
    for at, value in ((send_rows, loss), (send_rows + PAD, count)):
        digits = jnp.broadcast_to(digits_of(value), (PAD, LANES))
        keep[at : at + PAD, :] = digits
        send[at : at + PAD, :] = digits.astype(BF16)

    backward(wvp, cols_v, slope_v, hid_v, gemb_v, gpre, keep, send, block)


def block_of(frames):
    return next(n for n in (512, 256, TILE) if frames % n == 0)


def audio_kernel(block, w_proj, cols, slope, hid, gemb, keep, send, gpre):
    backward(w_proj, cols, slope, hid, gemb, gpre, keep, send, block)
    for ref in (keep, send):
        ref[ref.shape[0] - TILES :, :] = jnp.zeros((TILES, LANES), ref.dtype)


def local_grads(halo, lengths, labels, own_a, own_v, got, wac, wap, wvc, wvp):
    clips, frames, chan = own_a.shape
    if not halo:
        clips, frames = clips // 2, frames * 2
    width = wap.shape[0]
    rows = clips * frames
    taps = wac.shape[0]
    grad_rows = taps * chan + width
    wac = wac.reshape(taps * chan, width)
    wvc = wvc.reshape(taps * chan, width)
    blocks = width // 2 // LANES
    smem = pl.BlockSpec(memory_space=pltpu.SMEM)
    vmem = pl.BlockSpec(memory_space=pltpu.VMEM)
    hbm = pl.BlockSpec(memory_space=pl.ANY)
    sums = [pltpu.VMEM((blocks * grad_rows + TILES, LANES), dtype) for dtype in (F32, BF16)]
    saved = [
        pltpu.VMEM((rows, taps * chan), BF16),
        pltpu.VMEM((rows, width), F32),
        pltpu.VMEM((rows, width), BF16),
        pltpu.VMEM((rows, width), BF16),
    ]
    keep_v, send_v, *audio = pl.pallas_call(
        functools.partial(kernel, frames, clips, halo),
        out_shape=sums + saved,
        in_specs=[smem, smem, hbm, hbm, vmem] + [hbm] * 4,
        out_specs=[vmem] * 6,
        scratch_shapes=saved
        + [
            pltpu.VMEM((rows, width), BF16),
            pltpu.VMEM((clips, frames + 2 * PAD, width), BF16),
            pltpu.VMEM((rows, width), BF16),
            pltpu.VMEM((clips, frames + 2 * PAD, LANES), F32),
            pltpu.VMEM((rows, LANES), F32),
            pltpu.VMEM((clips, frames + 2 * PAD, width), F32),
            pltpu.VMEM((clips, frames + 2 * PAD, LANES), F32),
            pltpu.VMEM((2, clips, frames, chan), BF16),
            pltpu.VMEM((taps * chan, width), BF16),
            pltpu.VMEM((width, width), BF16),
            pltpu.VMEM((taps * chan, width), BF16),
            pltpu.VMEM((width, width), BF16),
            pltpu.SemaphoreType.DMA((4 * clips + 4,)),
        ],
        compiler_params=pltpu.CompilerParams(vmem_limit_bytes=44 * 1024 * 1024),
    )(lengths, labels, own_a, own_v, got, wac, wap, wvc, wvp)
    keep_a, send_a = pl.pallas_call(
        functools.partial(audio_kernel, block_of(frames)),
        out_shape=sums,
        in_specs=[vmem] * 5,
        out_specs=[vmem] * 2,
        scratch_shapes=[pltpu.VMEM((rows, width), BF16)],
        compiler_params=pltpu.CompilerParams(vmem_limit_bytes=32 * 1024 * 1024),
        cost_estimate=pl.CostEstimate(flops=2 * rows * width * (grad_rows + width), bytes_accessed=12 * rows * width, transcendentals=0),
    )(wap, *audio)
    return (keep_v, keep_a), (send_v, send_a)


def swap(value, axis, bit):
    return lax.ppermute(value, axis, [(i, i ^ bit) for i in range(lax.axis_size(axis))])


def swap_by_core(value, bits):
    peers = lax.axis_size("tm")
    pairs = []
    for clip in range(lax.axis_size("clip")):
        for tm in range(peers):
            pairs.append((clip * peers + tm, (clip ^ bits[tm % 2]) * peers + tm))
    return lax.ppermute(value, ("clip", "tm"), pairs)


def pick(value, index):
    return lax.dynamic_index_in_dim(value, index, 0, keepdims=False)


def halve(value, axis, bit, tile):
    me = (lax.axis_index(axis) // bit) % 2
    parts = value.reshape(2, -1, LANES)
    got = swap(jnp.concatenate([pick(parts, 1 - me).astype(BF16), tile]), axis, bit).astype(F32)
    rows = parts.shape[1]
    return pick(parts, me).astype(F32) + got[:rows], (tile.astype(F32) + got[rows:]).astype(BF16)


def double(value, axis, bit):
    me = (lax.axis_index(axis) // bit) % 2
    got = swap(value, axis, bit)
    return jnp.stack([jnp.where(me == 0, value, got), jnp.where(me == 0, got, value)]).reshape(-1, LANES)


def place_of(bits):
    clip, odd = lax.axis_index("clip"), lax.axis_index("tm") % 2
    return jnp.where(odd == 0, (clip // bits[0]) % 4, (clip // bits[1]) % 4)


def quarter(parts, bits, tile):
    me = place_of(bits)
    rows = parts.shape[1]
    mine = pick(parts, me).astype(F32)
    whole = tile.astype(F32)
    for k in (1, 2, 3):
        out = jnp.concatenate([pick(parts, me ^ k).astype(BF16), tile])
        got = swap_by_core(out, (k * bits[0], k * bits[1])).astype(F32)
        mine = mine + got[:rows]
        whole = whole + got[rows:]
    return mine, whole.astype(BF16)


def spread(value, bits):
    return [value] + [swap_by_core(value, (k * bits[0], k * bits[1])) for k in (1, 2, 3)]


def in_order(got, bits):
    me = place_of(bits)
    out = []
    for j in range(4):
        k = me ^ j
        out.append(jnp.where(k == 0, got[0], jnp.where(k == 1, got[1], jnp.where(k == 2, got[2], got[3]))))
    return jnp.stack(out).reshape(-1, LANES)


def bits_of(axis):
    size, bits = lax.axis_size(axis), []
    bit = 1
    while bit < size:
        bits.append(bit)
        bit *= 2
    return bits


def place_in_kernel(bits):
    clip, odd = lax.axis_index("clip"), lax.rem(lax.axis_index("tm"), 2)
    return jnp.where(odd == 0, lax.rem(clip // bits[0], 4), lax.rem(clip // bits[1], 4))


def place_kernel(bits, *refs):
    me = place_in_kernel(bits)
    out = refs[-1]
    part = out.shape[0] // 4
    for k in range(4):
        out[pl.ds(pl.multiple_of((me ^ k) * part, PAD), part), :] = refs[k][...]


def place(got, bits):
    vmem = pl.BlockSpec(memory_space=pltpu.VMEM)
    return pl.pallas_call(
        functools.partial(place_kernel, bits),
        out_shape=pltpu.VMEM((4 * got[0].shape[0], LANES), got[0].dtype),
        in_specs=[vmem] * 4,
        out_specs=vmem,
        compiler_params=pltpu.CompilerParams(vmem_limit_bytes=16 * 1024 * 1024),
    )(*got)


def deal_kernel(bits, base, got, mine, *outs):
    me = place_in_kernel(bits)
    part = mine.shape[0] - TILES

    def total(rows):
        return base[rows, :] + got[rows, :].astype(F32)

    tile = total(pl.ds(4 * part, TILES))
    for k, out in enumerate((mine, *outs)):
        rows = pl.ds(pl.multiple_of((me ^ k) * part, PAD), part)
        out[0:part, :] = total(rows).astype(out.dtype)
        out[part:, :] = tile.astype(out.dtype)


def join_kernel(base, *refs):
    value = base[...]
    for ref in refs[:-1]:
        value = value + ref[...].astype(F32)
    refs[-1][...] = value.astype(BF16)


def split_kernel(one, other, *outs):
    start = 0
    for out in outs:
        rows = pl.ds(start, out.shape[0])
        out[...] = (one[rows, :].astype(F32) + other[rows, :].astype(F32)).astype(BF16)
        start += out.shape[0]


def on_chip(body, shapes, *args):
    vmem = pl.BlockSpec(memory_space=pltpu.VMEM)
    return pl.pallas_call(
        body,
        out_shape=[pltpu.VMEM((rows, LANES), dtype) for rows, dtype in shapes],
        in_specs=[vmem] * len(args),
        out_specs=[vmem] * len(shapes),
        compiler_params=pltpu.CompilerParams(vmem_limit_bytes=16 * 1024 * 1024),
    )(*args)


def reduce_all(keep, send):
    gots = [swap(value, "tm", 1) for value in send]
    rest = [("tm", bit) for bit in bits_of("tm")[1:]] + [("clip", bit) for bit in bits_of("clip")[4:]]
    rounds = ((1, 4), (4, 1))
    if rest:
        mine, tiles = [], []
        for base, got in zip(keep, gots):
            total = base + got.astype(F32)
            total, tile = total[:-TILES], total[-TILES:].astype(BF16)
            for axis, bit in rest:
                total, tile = halve(total, axis, bit, tile)
            for bits in rounds:
                total, tile = quarter(total.reshape(4, -1, LANES), bits, tile)
            total = total.astype(BF16)
            for bits in rounds[::-1]:
                total = in_order(spread(total, bits), bits)
            for axis, bit in rest[::-1]:
                total = double(total, axis, bit)
            mine.append(total)
            tiles.append(tile)
        return mine, tiles[0]
    mine, tiles = [], []
    for base, got, (groups, pairs, last_pairs) in zip(keep, gots, PLANS):
        part = (base.shape[0] - TILES) // 4 + TILES
        shapes = [(part, F32)] + [(part, BF16)] * 3
        base, *outs = on_chip(functools.partial(deal_kernel, groups), shapes, base, got)
        (value,) = on_chip(join_kernel, [(part, BF16)], base, *exchange(outs, groups))
        (value,) = on_chip(split_kernel, [(part, BF16)], value, swap_by_core(value, pairs))
        shapes = [(part - TILES, BF16)] + [(TILES, BF16)] * (not tiles)
        value, *tile = on_chip(split_kernel, shapes, value, swap_by_core(value, last_pairs))
        mine.append(value)
        tiles += tile
    return [place(spread(value, plan[0]), plan[0]) for value, plan in zip(mine, PLANS)], tiles[0]


def exchange(outs, bits):
    return [swap_by_core(out, ((k + 1) * bits[0], (k + 1) * bits[1])) for k, out in enumerate(outs)]


def finish_kernel(parts, aliased, with_loss, rows, *refs):
    staged, sems = refs[-2:]
    sums, scalars = refs[: len(parts)], refs[len(parts)]
    outs = list(refs[len(parts) + 1 + aliased : -2])
    scale = scalars[0:1, :]
    if with_loss:
        outs.pop(0)[0, 0] = scalars[8, 0]
    encoders = sorted({m for m, _ in parts})
    blocks = sums[0].shape[0] // rows
    odd = lax.rem(lax.axis_index("tm"), 2)
    copies = []
    for n, (m, own) in enumerate(parts):
        half = odd if own else 1 - odd
        where = encoders.index(m) * 2
        at = 0
        columns = pl.ds(pl.multiple_of(half * blocks * LANES, LANES), blocks * LANES)
        for out in outs[where : where + 2]:
            for row in range(0, out.shape[0], SLAB):
                here, there = pl.ds(at + row, SLAB), pl.ds(row, SLAB)
                for j in range(blocks):
                    value = sums[n][pl.ds(j * rows + at + row, SLAB), :].astype(F32) * scale
                    staged[n, here, j * LANES : (j + 1) * LANES] = value
                copy = pltpu.make_async_copy(staged.at[n, here, :], out.at[there, columns], sems.at[len(copies)])
                copy.start()
                copies.append(copy)
            at += out.shape[0]
    for copy in copies:
        copy.wait()


def scalars_kernel(tile, out):
    digits = tile[...].astype(F32)
    count = value_of(digits[PAD : PAD + 1])
    out[0:8, :] = jnp.broadcast_to(1.0 / count, (8, LANES))
    out[8:16, :] = jnp.broadcast_to(value_of(digits[0:1]) / count, (8, LANES))


def finish_some(parts, sums, scalars, earlier, with_loss, conv_rows, width):
    smem, vmem, hbm = (pl.BlockSpec(memory_space=space) for space in (pltpu.SMEM, pltpu.VMEM, pl.ANY))
    encoders = sorted({m for m, _ in parts})
    grads = [jax.ShapeDtypeStruct((n, width), F32) for n in (conv_rows, width) * len(encoders)]
    known = [(m, array) for m in encoders if m in earlier for array in earlier[m]]
    places = {(m, n): i for i, (m, n) in enumerate((m, n) for m in encoders for n in (0, 1))}
    aliases = {
        len(parts) + 1 + i: with_loss + places[m, i % 2] for i, (m, _) in enumerate(known)
    }
    rows = conv_rows + width
    height = sums[0].shape[0]
    size = height * LANES * len(parts)
    outs = pl.pallas_call(
        functools.partial(finish_kernel, parts, len(known), with_loss, rows),
        out_shape=[jax.ShapeDtypeStruct((1, 1), F32)] * with_loss + grads,
        in_specs=[vmem] * (len(parts) + 1) + [hbm] * len(known),
        out_specs=[smem] * with_loss + [hbm] * len(grads),
        scratch_shapes=[
            pltpu.VMEM((len(parts), rows, width // 2), F32),
            pltpu.SemaphoreType.DMA((len(parts) * rows // SLAB,)),
        ],
        input_output_aliases=aliases,
        compiler_params=pltpu.CompilerParams(vmem_limit_bytes=20 * 1024 * 1024),
        cost_estimate=pl.CostEstimate(flops=size, bytes_accessed=6 * size, transcendentals=0),
    )(*sums, scalars, *[array for _, array in known])
    loss, outs = outs[:with_loss], outs[with_loss:]
    for i, m in enumerate(encoders):
        earlier = {**earlier, m: outs[2 * i : 2 * i + 2]}
    return loss, earlier


def finish(halves, tile, conv_rows, width):
    gots = [swap(half, "tm", 1) for half in halves]
    sums = {(m, own): (halves if own else gots)[m] for m in (0, 1) for own in (True, False)}
    (scalars,) = on_chip(scalars_kernel, [(16, F32)], tile)
    loss, done = [], {}
    for parts in GROUPS:
        value, done = finish_some(parts, [sums[part] for part in parts], scalars, done, not loss, conv_rows, width)
        loss = loss or value
    return loss[0], [*done[0], *done[1]]


def shards(
    audio_feats, lip_feats, lengths, labels, w_audio_conv, w_audio_proj, w_lip_conv, w_lip_proj
):
    peers = lax.axis_size("tm")
    clips, frames, chan = audio_feats.shape
    halo = 0
    if peers == 2 and clips % 2 == 0:
        others = (1 - lax.axis_index("tm")) * (clips // 2)
        out = jnp.stack([lax.dynamic_slice_in_dim(x, others, clips // 2) for x in (audio_feats, lip_feats)])
        got = swap(out, "tm", 1)
    else:
        halo = HALO
        after = [(i, i + 1) for i in range(peers - 1)]
        before = [(i + 1, i) for i in range(peers - 1)]
        both = jnp.stack([audio_feats, lip_feats])
        audio_feats, lip_feats = jnp.concatenate(
            [
                lax.ppermute(both[:, :, -HALO:], "tm", after),
                both,
                lax.ppermute(both[:, :, :HALO], "tm", before),
            ],
            axis=2,
        )
        got = lengths.astype(BF16)
    keep, send = local_grads(
        halo, lengths, labels, audio_feats, lip_feats, got, w_audio_conv, w_audio_proj, w_lip_conv, w_lip_proj
    )
    halves, tile = reduce_all(keep, send)
    taps, chan, width = w_audio_conv.shape
    loss, (vc, vp, ac, ap) = finish(halves, tile, taps * chan, width)
    return (loss.reshape(()), ac.reshape(w_audio_conv.shape), ap, vc.reshape(w_lip_conv.shape), vp)


def solution(mesh):
    placed = (
        P("clip", "tm", None),
        P("clip", "tm", None),
        P("clip"),
        P("clip"),
        P(),
        P(),
        P(),
        P(),
    )
    return jax.shard_map(
        shards, mesh=mesh, in_specs=placed, out_specs=(P(), P(), P(), P(), P()), check_vma=False
    )
```

```python
import functools

import jax
import jax.numpy as jnp
from jax import lax
from jax.experimental import pallas as pl
from jax.experimental.pallas import tpu as pltpu
from jax.sharding import PartitionSpec as P

SPAN = 15
PAD = 16
TILE = 128
WIN = TILE + 2 * PAD
HALO = 64
TILES = 2 * PAD
SLAB = 256
GROUPS = (((0, True), (1, True)), ((0, False), (1, False)))
PLANS = (((1, 1), (4, 8), (8, 4)), ((1, 4), (4, 1), (8, 2)))
LANES = 128
DIGITS = 48
FRACTION = 20

logit_sharpening_divisor = 10.0
loss_scale = 1024.0
epsilon = 1e-06

BF16 = jnp.bfloat16
F32 = jnp.float32


def dot(a, b, dims):
    return lax.dot_general(a, b, (dims, ((), ())), preferred_element_type=F32)


NN = ((1,), (0,))
NT = ((1,), (1,))
TN = ((0,), (0,))


def digit_weights(shape):
    lane = lax.broadcasted_iota(jnp.int32, shape, len(shape) - 1)
    return lane, jnp.exp2((lane - FRACTION).astype(F32))


def digits_of(value):
    lane, weight = digit_weights((1, LANES))
    size = jnp.abs(value)
    bits = jnp.floor(size / weight) - 2.0 * jnp.floor(size / (2.0 * weight))
    return jnp.where(lane < DIGITS, jnp.where(value < 0, -bits, bits), 0.0)


def value_of(digits):
    lane, weight = digit_weights(digits.shape)
    return jnp.sum(jnp.where(lane < DIGITS, digits * weight, 0.0))


def columns(feats, m, copies, cols, clips, frames):
    chan = feats.shape[-1]
    for copy in copies:
        copy.wait()
    for c in range(clips):
        x = feats[m, c].astype(F32)
        row = lax.broadcasted_iota(jnp.int32, x.shape, 0)
        base = c * frames
        cols[base : base + frames, 0:chan] = jnp.where(row == 0, 0.0, pltpu.roll(x, 1, 0)).astype(BF16)
        cols[base : base + frames, chan : 2 * chan] = feats[m, c]
        cols[base : base + frames, 2 * chan : 3 * chan] = jnp.where(
            row == frames - 1, 0.0, pltpu.roll(x, frames - 1, 0)
        ).astype(BF16)


def forward(i, w_conv, w_proj, cols, slope, hid, block, put):
    rows = pl.ds(i * block, block)
    pre = dot(cols[rows, :], w_conv[...], NN)
    yield
    sigma = 0.5 * jnp.tanh(0.5 * pre) + 0.5
    hidden = (pre * sigma).astype(BF16)
    hid[rows, :] = hidden
    slope[rows, :] = sigma * (1.0 + pre * (1.0 - sigma))
    yield
    emb = dot(hidden, w_proj[...], NN).astype(BF16)
    yield
    values = emb.astype(F32)
    inv = lax.rsqrt(jnp.sum(values * values, axis=1, keepdims=True) + epsilon)
    put(i, emb, jnp.broadcast_to(inv, (block, LANES)))
    yield


def staggered(works):
    running = []
    while works or running:
        running += works[:1]
        works = works[1:]
        running = [work for work in running if next(work, running) is not running]


def backward(w_proj, cols, slope, hid, gemb, gpre, keep, send, block):
    def step(i, _):
        rows = pl.ds(pl.multiple_of(i * block, block), block)
        gpre[rows, :] = (dot(gemb[rows, :], w_proj[...], NT) * slope[rows, :]).astype(BF16)
        return 0

    lax.fori_loop(0, hid.shape[0] // block, step, 0, unroll=True)
    even = lax.rem(lax.axis_index("tm"), 2) == 0
    height = cols.shape[1] + hid.shape[1]
    start = 0
    for left, right in ((cols, gpre), (hid, gemb)):
        grad = dot(left[...], right[...], TN)
        rows, width = grad.shape[0], grad.shape[1] // 2
        mine = jnp.where(even, grad[:, :width], grad[:, width:])
        other = jnp.where(even, grad[:, width:], grad[:, :width])
        for j in range(width // LANES):
            at = j * height + start
            keep[at : at + rows, :] = mine[:, j * LANES : (j + 1) * LANES]
            send[at : at + rows, :] = other[:, j * LANES : (j + 1) * LANES].astype(BF16)
        start += rows


def kernel(
    frames, clips, halo, lengths, labels, own_a, own_v, got, wac_in, wap_in, wvc_in, wvp_in,
    keep, send, cols_a, slope_a, hid_a, gemb_a, cols_v, slope_v, hid_v, gemb_v, gpre, emb_a, emb_v, inv_a, inv_v, gacc, giacc, feats, wac, wap, wvc, wvp, sems,
):
    me = lax.axis_index("tm")
    rows_total = clips * frames
    start = me * (frames - 2 * halo) - halo if halo else 0
    first_clip = 0 if halo else me * clips
    block = block_of(frames)
    per_clip = frames // block

    copies = []

    def fetch(source, target):
        copy = pltpu.make_async_copy(source, target, sems.at[len(copies)])
        copy.start()
        copies.append(copy)
        return copy

    def fetch_feats(m, own):
        if halo:
            return [fetch(own, feats.at[m])]
        seg = own.shape[1]
        mine = pl.ds(pl.multiple_of(me * seg, seg), seg)
        other = pl.ds(pl.multiple_of((1 - me) * seg, seg), seg)
        started = []
        for c in range(clips):
            started.append(fetch(own.at[first_clip + c], feats.at[m, c, mine, :]))
            started.append(fetch(got.at[m, c], feats.at[m, c, other, :]))
        return started

    feats_v = fetch_feats(1, own_v)
    weights_v = [fetch(wvc_in, wvc), fetch(wvp_in, wvp)]
    feats_a = fetch_feats(0, own_a)
    weights_a = [fetch(wac_in, wac), fetch(wap_in, wap)]
    gacc[...] = jnp.zeros(gacc.shape, F32)
    giacc[...] = jnp.zeros(giacc.shape, F32)

    for c in range(clips):
        for lo in (0, PAD + frames):
            emb_a[c, lo : lo + PAD, :] = jnp.zeros((PAD, emb_a.shape[2]), BF16)
            inv_a[c, lo : lo + PAD, :] = jnp.zeros((PAD, LANES), F32)

    def put_a(i, emb, inv):
        c = i // per_clip
        at = PAD + i % per_clip * block
        emb_a[c, pl.ds(at, block), :] = emb
        inv_a[c, pl.ds(at, block), :] = inv

    def put_v(i, emb, inv):
        at = i * block
        emb_v[pl.ds(at, block), :] = emb
        inv_v[pl.ds(at, block), :] = inv

    columns(feats, 1, feats_v, cols_v, clips, frames)
    for copy in weights_v:
        copy.wait()
    columns(feats, 0, feats_a, cols_a, clips, frames)
    for copy in weights_a:
        copy.wait()
    count = rows_total // block
    works_v = [forward(i, wvc, wvp, cols_v, slope_v, hid_v, block, put_v) for i in range(count)]
    works_a = [forward(i, wac, wap, cols_a, slope_a, hid_a, block, put_a) for i in range(count)]
    staggered(works_v + works_a)

    tiles = frames // TILE
    gang = next(n for n in (4, 2, 1) if clips * tiles % n == 0)
    row = lax.broadcasted_iota(jnp.int32, (TILE, WIN), 0)
    col = lax.broadcasted_iota(jnp.int32, (TILE, WIN), 1)
    shift = col - row - PAD
    in_band = (shift >= -SPAN) & (shift <= SPAN)
    row_1 = lax.broadcasted_iota(jnp.int32, (TILE, 1), 0)

    def tile_work(i):
        c = i // tiles
        first = pl.multiple_of(lax.rem(i, tiles) * TILE, TILE)
        length = lengths[first_clip + c]
        label = labels[first_clip + c]
        here = pl.ds(pl.multiple_of(i * TILE, TILE), TILE)
        window = pl.ds(first, WIN)
        ev = emb_v[here, :]
        wa = emb_a[c, window, :]
        dots = dot(ev, wa, NT)
        yield
        iv = inv_v[here, 0:1]
        both = iv * inv_a[c, window, :].T
        scores = (logit_sharpening_divisor * dots) * both
        yield
        t = start + first + row_1
        u = start + first - PAD + col[0:1]
        inside = t < length
        target = t + label
        counted = inside & (target >= 0) & (target < length)
        hit = shift == label
        weights = jnp.where(in_band & ((u >= 0) & (u < length)), jnp.exp(scores), 0.0)
        yield
        sums = jnp.where(counted, jnp.sum(weights, axis=1, keepdims=True), 1.0)
        picked = jnp.sum(jnp.where(hit, scores, 0.0), axis=1, keepdims=True)
        yield
        own = (first + row_1 >= halo) & (first + row_1 < frames - halo)
        loss = jnp.where(counted & own, jnp.log(sums) - picked, 0.0)
        scale = jnp.where(counted, logit_sharpening_divisor * loss_scale, 0.0)
        grad = (weights * (scale / sums) - jnp.where(hit, scale, 0.0)) * both
        gd = grad.astype(BF16)
        yield
        by_dots = grad * dots
        lip = dot(gd, wa, NN)
        yield
        audio = dot(gd, ev, TN)
        yield
        giv = jnp.sum(by_dots, axis=1, keepdims=True)
        gia = jnp.sum(by_dots.T, axis=1, keepdims=True)
        yield
        lip = lip - (iv * iv * giv) * ev.astype(F32)
        gemb_v[here, :] = jnp.where(own, lip, 0.0).astype(BF16)
        yield
        gacc[c, window, :] += audio
        giacc[c, window, :] += jnp.broadcast_to(gia, (WIN, LANES))
        yield loss

    def tile_step(i, loss):
        together = [tile_work(i + k * (clips * tiles // gang)) for k in range(gang)]
        last = [None]
        while last[0] is None:
            last = [next(work) for work in together]
        return loss + sum(last)

    loss = lax.fori_loop(0, clips * tiles // gang, tile_step, jnp.zeros((TILE, 1), F32), unroll=clips * tiles <= 8)
    loss = jnp.sum(loss)

    def audio_step(i, _):
        c = i // per_clip
        at = pl.ds(pl.multiple_of(PAD + lax.rem(i, per_clip) * block, PAD), block)
        inv = inv_a[c, at, 0:1]
        grad = gacc[c, at, :] - (inv * inv * giacc[c, at, 0:1]) * emb_a[c, at, :].astype(F32)
        if halo:
            at_row = lax.rem(i, per_clip) * block + lax.broadcasted_iota(jnp.int32, (block, 1), 0)
            grad = jnp.where((at_row >= halo) & (at_row < frames - halo), grad, 0.0)
        gemb_a[pl.ds(pl.multiple_of(i * block, block), block), :] = grad.astype(BF16)
        return 0

    lax.fori_loop(0, rows_total // block, audio_step, 0)

    count = jnp.zeros((), F32)
    for c in range(clips):
        count = count + (lengths[first_clip + c] - jnp.abs(labels[first_clip + c])).astype(F32)
    if halo:
        count = jnp.where(me == 0, count, 0.0)
    send_rows = send.shape[0] - TILES
    for at, value in ((send_rows, loss), (send_rows + PAD, count)):
        digits = jnp.broadcast_to(digits_of(value), (PAD, LANES))
        keep[at : at + PAD, :] = digits
        send[at : at + PAD, :] = digits.astype(BF16)

    backward(wvp, cols_v, slope_v, hid_v, gemb_v, gpre, keep, send, block)


def block_of(frames):
    return next(n for n in (512, 256, TILE) if frames % n == 0)


def audio_kernel(block, w_proj, cols, slope, hid, gemb, keep, send, gpre):
    backward(w_proj, cols, slope, hid, gemb, gpre, keep, send, block)
    for ref in (keep, send):
        ref[ref.shape[0] - TILES :, :] = jnp.zeros((TILES, LANES), ref.dtype)


def local_grads(halo, lengths, labels, own_a, own_v, got, wac, wap, wvc, wvp):
    clips, frames, chan = own_a.shape
    if not halo:
        clips, frames = clips // 2, frames * 2
    width = wap.shape[0]
    rows = clips * frames
    taps = wac.shape[0]
    grad_rows = taps * chan + width
    wac = wac.reshape(taps * chan, width)
    wvc = wvc.reshape(taps * chan, width)
    blocks = width // 2 // LANES
    smem = pl.BlockSpec(memory_space=pltpu.SMEM)
    vmem = pl.BlockSpec(memory_space=pltpu.VMEM)
    hbm = pl.BlockSpec(memory_space=pl.ANY)
    sums = [pltpu.VMEM((blocks * grad_rows + TILES, LANES), dtype) for dtype in (F32, BF16)]
    saved = [
        pltpu.VMEM((rows, taps * chan), BF16),
        pltpu.VMEM((rows, width), F32),
        pltpu.VMEM((rows, width), BF16),
        pltpu.VMEM((rows, width), BF16),
    ]
    keep_v, send_v, *audio = pl.pallas_call(
        functools.partial(kernel, frames, clips, halo),
        out_shape=sums + saved,
        in_specs=[smem, smem, hbm, hbm, vmem] + [hbm] * 4,
        out_specs=[vmem] * 6,
        scratch_shapes=saved
        + [
            pltpu.VMEM((rows, width), BF16),
            pltpu.VMEM((clips, frames + 2 * PAD, width), BF16),
            pltpu.VMEM((rows, width), BF16),
            pltpu.VMEM((clips, frames + 2 * PAD, LANES), F32),
            pltpu.VMEM((rows, LANES), F32),
            pltpu.VMEM((clips, frames + 2 * PAD, width), F32),
            pltpu.VMEM((clips, frames + 2 * PAD, LANES), F32),
            pltpu.VMEM((2, clips, frames, chan), BF16),
            pltpu.VMEM((taps * chan, width), BF16),
            pltpu.VMEM((width, width), BF16),
            pltpu.VMEM((taps * chan, width), BF16),
            pltpu.VMEM((width, width), BF16),
            pltpu.SemaphoreType.DMA((4 * clips + 4,)),
        ],
        compiler_params=pltpu.CompilerParams(vmem_limit_bytes=44 * 1024 * 1024),
    )(lengths, labels, own_a, own_v, got, wac, wap, wvc, wvp)
    keep_a, send_a = pl.pallas_call(
        functools.partial(audio_kernel, block_of(frames)),
        out_shape=sums,
        in_specs=[vmem] * 5,
        out_specs=[vmem] * 2,
        scratch_shapes=[pltpu.VMEM((rows, width), BF16)],
        compiler_params=pltpu.CompilerParams(vmem_limit_bytes=32 * 1024 * 1024),
        cost_estimate=pl.CostEstimate(flops=2 * rows * width * (grad_rows + width), bytes_accessed=12 * rows * width, transcendentals=0),
    )(wap, *audio)
    return (keep_v, keep_a), (send_v, send_a)


def swap(value, axis, bit):
    return lax.ppermute(value, axis, [(i, i ^ bit) for i in range(lax.axis_size(axis))])


def swap_by_core(value, bits):
    peers = lax.axis_size("tm")
    pairs = []
    for clip in range(lax.axis_size("clip")):
        for tm in range(peers):
            pairs.append((clip * peers + tm, (clip ^ bits[tm % 2]) * peers + tm))
    return lax.ppermute(value, ("clip", "tm"), pairs)


def pick(value, index):
    return lax.dynamic_index_in_dim(value, index, 0, keepdims=False)


def halve(value, axis, bit, tile):
    me = (lax.axis_index(axis) // bit) % 2
    parts = value.reshape(2, -1, LANES)
    got = swap(jnp.concatenate([pick(parts, 1 - me).astype(BF16), tile]), axis, bit).astype(F32)
    rows = parts.shape[1]
    return pick(parts, me).astype(F32) + got[:rows], (tile.astype(F32) + got[rows:]).astype(BF16)


def double(value, axis, bit):
    me = (lax.axis_index(axis) // bit) % 2
    got = swap(value, axis, bit)
    return jnp.stack([jnp.where(me == 0, value, got), jnp.where(me == 0, got, value)]).reshape(-1, LANES)


def place_of(bits):
    clip, odd = lax.axis_index("clip"), lax.axis_index("tm") % 2
    return jnp.where(odd == 0, (clip // bits[0]) % 4, (clip // bits[1]) % 4)


def quarter(parts, bits, tile):
    me = place_of(bits)
    rows = parts.shape[1]
    mine = pick(parts, me).astype(F32)
    whole = tile.astype(F32)
    for k in (1, 2, 3):
        out = jnp.concatenate([pick(parts, me ^ k).astype(BF16), tile])
        got = swap_by_core(out, (k * bits[0], k * bits[1])).astype(F32)
        mine = mine + got[:rows]
        whole = whole + got[rows:]
    return mine, whole.astype(BF16)


def spread(value, bits):
    return [value] + [swap_by_core(value, (k * bits[0], k * bits[1])) for k in (1, 2, 3)]


def in_order(got, bits):
    me = place_of(bits)
    out = []
    for j in range(4):
        k = me ^ j
        out.append(jnp.where(k == 0, got[0], jnp.where(k == 1, got[1], jnp.where(k == 2, got[2], got[3]))))
    return jnp.stack(out).reshape(-1, LANES)


def bits_of(axis):
    size, bits = lax.axis_size(axis), []
    bit = 1
    while bit < size:
        bits.append(bit)
        bit *= 2
    return bits


def place_in_kernel(bits):
    clip, odd = lax.axis_index("clip"), lax.rem(lax.axis_index("tm"), 2)
    return jnp.where(odd == 0, lax.rem(clip // bits[0], 4), lax.rem(clip // bits[1], 4))


def place_kernel(bits, *refs):
    me = place_in_kernel(bits)
    out = refs[-1]
    part = out.shape[0] // 4
    for k in range(4):
        out[pl.ds(pl.multiple_of((me ^ k) * part, PAD), part), :] = refs[k][...]


def place(got, bits):
    vmem = pl.BlockSpec(memory_space=pltpu.VMEM)
    return pl.pallas_call(
        functools.partial(place_kernel, bits),
        out_shape=pltpu.VMEM((4 * got[0].shape[0], LANES), got[0].dtype),
        in_specs=[vmem] * 4,
        out_specs=vmem,
        compiler_params=pltpu.CompilerParams(vmem_limit_bytes=16 * 1024 * 1024),
    )(*got)


def deal_kernel(bits, base, got, mine, *outs):
    me = place_in_kernel(bits)
    part = mine.shape[0] - TILES

    def total(rows):
        return base[rows, :] + got[rows, :].astype(F32)

    tile = total(pl.ds(4 * part, TILES))
    for k, out in enumerate((mine, *outs)):
        rows = pl.ds(pl.multiple_of((me ^ k) * part, PAD), part)
        out[0:part, :] = total(rows).astype(out.dtype)
        out[part:, :] = tile.astype(out.dtype)


def join_kernel(base, *refs):
    value = base[...]
    for ref in refs[:-1]:
        value = value + ref[...].astype(F32)
    refs[-1][...] = value.astype(BF16)


def split_kernel(one, other, *outs):
    start = 0
    for out in outs:
        rows = pl.ds(start, out.shape[0])
        out[...] = (one[rows, :].astype(F32) + other[rows, :].astype(F32)).astype(BF16)
        start += out.shape[0]


def on_chip(body, shapes, *args):
    vmem = pl.BlockSpec(memory_space=pltpu.VMEM)
    return pl.pallas_call(
        body,
        out_shape=[pltpu.VMEM((rows, LANES), dtype) for rows, dtype in shapes],
        in_specs=[vmem] * len(args),
        out_specs=[vmem] * len(shapes),
        compiler_params=pltpu.CompilerParams(vmem_limit_bytes=16 * 1024 * 1024),
    )(*args)


def reduce_all(keep, send):
    gots = [swap(value, "tm", 1) for value in send]
    rest = [("tm", bit) for bit in bits_of("tm")[1:]] + [("clip", bit) for bit in bits_of("clip")[4:]]
    rounds = ((1, 4), (4, 1))
    if rest:
        mine, tiles = [], []
        for base, got in zip(keep, gots):
            total = base + got.astype(F32)
            total, tile = total[:-TILES], total[-TILES:].astype(BF16)
            for axis, bit in rest:
                total, tile = halve(total, axis, bit, tile)
            for bits in rounds:
                total, tile = quarter(total.reshape(4, -1, LANES), bits, tile)
            total = total.astype(BF16)
            for bits in rounds[::-1]:
                total = in_order(spread(total, bits), bits)
            for axis, bit in rest[::-1]:
                total = double(total, axis, bit)
            mine.append(total)
            tiles.append(tile)
        return mine, tiles[0]
    mine, tiles = [], []
    for base, got, (groups, pairs, last_pairs) in zip(keep, gots, PLANS):
        part = (base.shape[0] - TILES) // 4 + TILES
        shapes = [(part, F32)] + [(part, BF16)] * 3
        base, *outs = on_chip(functools.partial(deal_kernel, groups), shapes, base, got)
        (value,) = on_chip(join_kernel, [(part, BF16)], base, *exchange(outs, groups))
        (value,) = on_chip(split_kernel, [(part, BF16)], value, swap_by_core(value, pairs))
        shapes = [(part - TILES, BF16)] + [(TILES, BF16)] * (not tiles)
        value, *tile = on_chip(split_kernel, shapes, value, swap_by_core(value, last_pairs))
        mine.append(value)
        tiles += tile
    return [place(spread(value, plan[0]), plan[0]) for value, plan in zip(mine, PLANS)], tiles[0]


def exchange(outs, bits):
    return [swap_by_core(out, ((k + 1) * bits[0], (k + 1) * bits[1])) for k, out in enumerate(outs)]


def finish_kernel(parts, aliased, with_loss, rows, *refs):
    staged, sems = refs[-2:]
    sums, scalars = refs[: len(parts)], refs[len(parts)]
    outs = list(refs[len(parts) + 1 + aliased : -2])
    scale = scalars[0:1, :]
    if with_loss:
        outs.pop(0)[0, 0] = scalars[8, 0]
    encoders = sorted({m for m, _ in parts})
    blocks = sums[0].shape[0] // rows
    odd = lax.rem(lax.axis_index("tm"), 2)
    copies = []
    for n, (m, own) in enumerate(parts):
        half = odd if own else 1 - odd
        where = encoders.index(m) * 2
        at = 0
        columns = pl.ds(pl.multiple_of(half * blocks * LANES, LANES), blocks * LANES)
        for out in outs[where : where + 2]:
            for row in range(0, out.shape[0], SLAB):
                here, there = pl.ds(at + row, SLAB), pl.ds(row, SLAB)
                for j in range(blocks):
                    value = sums[n][pl.ds(j * rows + at + row, SLAB), :].astype(F32) * scale
                    staged[n, here, j * LANES : (j + 1) * LANES] = value
                copy = pltpu.make_async_copy(staged.at[n, here, :], out.at[there, columns], sems.at[len(copies)])
                copy.start()
                copies.append(copy)
            at += out.shape[0]
    for copy in copies:
        copy.wait()


def scalars_kernel(tile, out):
    digits = tile[...].astype(F32)
    count = value_of(digits[PAD : PAD + 1])
    out[0:8, :] = jnp.broadcast_to(1.0 / count, (8, LANES))
    out[8:16, :] = jnp.broadcast_to(value_of(digits[0:1]) / count, (8, LANES))


def finish_some(parts, sums, scalars, earlier, with_loss, conv_rows, width):
    smem, vmem, hbm = (pl.BlockSpec(memory_space=space) for space in (pltpu.SMEM, pltpu.VMEM, pl.ANY))
    encoders = sorted({m for m, _ in parts})
    grads = [jax.ShapeDtypeStruct((n, width), F32) for n in (conv_rows, width) * len(encoders)]
    known = [(m, array) for m in encoders if m in earlier for array in earlier[m]]
    places = {(m, n): i for i, (m, n) in enumerate((m, n) for m in encoders for n in (0, 1))}
    aliases = {
        len(parts) + 1 + i: with_loss + places[m, i % 2] for i, (m, _) in enumerate(known)
    }
    rows = conv_rows + width
    height = sums[0].shape[0]
    size = height * LANES * len(parts)
    outs = pl.pallas_call(
        functools.partial(finish_kernel, parts, len(known), with_loss, rows),
        out_shape=[jax.ShapeDtypeStruct((1, 1), F32)] * with_loss + grads,
        in_specs=[vmem] * (len(parts) + 1) + [hbm] * len(known),
        out_specs=[smem] * with_loss + [hbm] * len(grads),
        scratch_shapes=[
            pltpu.VMEM((len(parts), rows, width // 2), F32),
            pltpu.SemaphoreType.DMA((len(parts) * rows // SLAB,)),
        ],
        input_output_aliases=aliases,
        compiler_params=pltpu.CompilerParams(vmem_limit_bytes=20 * 1024 * 1024),
        cost_estimate=pl.CostEstimate(flops=size, bytes_accessed=6 * size, transcendentals=0),
    )(*sums, scalars, *[array for _, array in known])
    loss, outs = outs[:with_loss], outs[with_loss:]
    for i, m in enumerate(encoders):
        earlier = {**earlier, m: outs[2 * i : 2 * i + 2]}
    return loss, earlier


def finish(halves, tile, conv_rows, width):
    gots = [swap(half, "tm", 1) for half in halves]
    sums = {(m, own): (halves if own else gots)[m] for m in (0, 1) for own in (True, False)}
    (scalars,) = on_chip(scalars_kernel, [(16, F32)], tile)
    loss, done = [], {}
    for parts in GROUPS:
        value, done = finish_some(parts, [sums[part] for part in parts], scalars, done, not loss, conv_rows, width)
        loss = loss or value
    return loss[0], [*done[0], *done[1]]


def shards(
    audio_feats, lip_feats, lengths, labels, w_audio_conv, w_audio_proj, w_lip_conv, w_lip_proj
):
    peers = lax.axis_size("tm")
    clips, frames, chan = audio_feats.shape
    halo = 0
    if peers == 2 and clips % 2 == 0:
        others = (1 - lax.axis_index("tm")) * (clips // 2)
        out = jnp.stack([lax.dynamic_slice_in_dim(x, others, clips // 2) for x in (audio_feats, lip_feats)])
        got = swap(out, "tm", 1)
    else:
        halo = HALO
        after = [(i, i + 1) for i in range(peers - 1)]
        before = [(i + 1, i) for i in range(peers - 1)]
        both = jnp.stack([audio_feats, lip_feats])
        audio_feats, lip_feats = jnp.concatenate(
            [
                lax.ppermute(both[:, :, -HALO:], "tm", after),
                both,
                lax.ppermute(both[:, :, :HALO], "tm", before),
            ],
            axis=2,
        )
        got = lengths.astype(BF16)
    keep, send = local_grads(
        halo, lengths, labels, audio_feats, lip_feats, got, w_audio_conv, w_audio_proj, w_lip_conv, w_lip_proj
    )
    halves, tile = reduce_all(keep, send)
    taps, chan, width = w_audio_conv.shape
    loss, (vc, vp, ac, ap) = finish(halves, tile, taps * chan, width)
    return (loss.reshape(()), ac.reshape(w_audio_conv.shape), ap, vc.reshape(w_lip_conv.shape), vp)


def solution(mesh):
    placed = (
        P("clip", "tm", None),
        P("clip", "tm", None),
        P("clip"),
        P("clip"),
        P(),
        P(),
        P(),
        P(),
    )
    return jax.shard_map(
        shards, mesh=mesh, in_specs=placed, out_specs=(P(), P(), P(), P(), P()), check_vma=False
    )
```

```python
import functools

import jax
import jax.numpy as jnp
from jax import lax
from jax.experimental import pallas as pl
from jax.experimental.pallas import tpu as pltpu
from jax.sharding import PartitionSpec as P

SPAN = 15
PAD = 16
TILE = 128
WIN = TILE + 2 * PAD
HALO = 64
TILES = 2 * PAD
SLAB = 256
GROUPS = (((0, True), (1, True)), ((0, False), (1, False)))
PLANS = (((1, 1), (4, 8), (8, 4)), ((1, 4), (4, 1), (8, 2)))
LANES = 128
DIGITS = 48
FRACTION = 20

logit_sharpening_divisor = 10.0
loss_scale = 1024.0
epsilon = 1e-06

BF16 = jnp.bfloat16
F32 = jnp.float32


def dot(a, b, dims):
    return lax.dot_general(a, b, (dims, ((), ())), preferred_element_type=F32)


NN = ((1,), (0,))
NT = ((1,), (1,))
TN = ((0,), (0,))


def digit_weights(shape):
    lane = lax.broadcasted_iota(jnp.int32, shape, len(shape) - 1)
    return lane, jnp.exp2((lane - FRACTION).astype(F32))


def digits_of(value):
    lane, weight = digit_weights((1, LANES))
    size = jnp.abs(value)
    bits = jnp.floor(size / weight) - 2.0 * jnp.floor(size / (2.0 * weight))
    return jnp.where(lane < DIGITS, jnp.where(value < 0, -bits, bits), 0.0)


def value_of(digits):
    lane, weight = digit_weights(digits.shape)
    return jnp.sum(jnp.where(lane < DIGITS, digits * weight, 0.0))


def columns(feats, m, copies, cols, clips, frames):
    chan = feats.shape[-1]
    for copy in copies:
        copy.wait()
    for c in range(clips):
        x = feats[m, c].astype(F32)
        row = lax.broadcasted_iota(jnp.int32, x.shape, 0)
        base = c * frames
        cols[base : base + frames, 0:chan] = jnp.where(row == 0, 0.0, pltpu.roll(x, 1, 0)).astype(BF16)
        cols[base : base + frames, chan : 2 * chan] = feats[m, c]
        cols[base : base + frames, 2 * chan : 3 * chan] = jnp.where(
            row == frames - 1, 0.0, pltpu.roll(x, frames - 1, 0)
        ).astype(BF16)


def forward(i, w_conv, w_proj, cols, slope, hid, block, put):
    rows = pl.ds(i * block, block)
    pre = dot(cols[rows, :], w_conv[...], NN)
    yield
    sigma = 0.5 * jnp.tanh(0.5 * pre) + 0.5
    hidden = (pre * sigma).astype(BF16)
    hid[rows, :] = hidden
    slope[rows, :] = sigma * (1.0 + pre * (1.0 - sigma))
    yield
    emb = dot(hidden, w_proj[...], NN).astype(BF16)
    yield
    values = emb.astype(F32)
    inv = lax.rsqrt(jnp.sum(values * values, axis=1, keepdims=True) + epsilon)
    put(i, emb, jnp.broadcast_to(inv, (block, LANES)))
    yield


def staggered(works):
    running = []
    while works or running:
        running += works[:1]
        works = works[1:]
        running = [work for work in running if next(work, running) is not running]


def backward(w_proj, cols, slope, hid, gemb, gpre, keep, send, block):
    def step(i, _):
        rows = pl.ds(pl.multiple_of(i * block, block), block)
        gpre[rows, :] = (dot(gemb[rows, :], w_proj[...], NT) * slope[rows, :]).astype(BF16)
        return 0

    lax.fori_loop(0, hid.shape[0] // block, step, 0, unroll=True)
    even = lax.rem(lax.axis_index("tm"), 2) == 0
    height = cols.shape[1] + hid.shape[1]
    start = 0
    for left, right in ((cols, gpre), (hid, gemb)):
        grad = dot(left[...], right[...], TN)
        rows, width = grad.shape[0], grad.shape[1] // 2
        mine = jnp.where(even, grad[:, :width], grad[:, width:])
        other = jnp.where(even, grad[:, width:], grad[:, :width])
        for j in range(width // LANES):
            at = j * height + start
            keep[at : at + rows, :] = mine[:, j * LANES : (j + 1) * LANES]
            send[at : at + rows, :] = other[:, j * LANES : (j + 1) * LANES].astype(BF16)
        start += rows


def kernel(
    frames, clips, halo, lengths, labels, own_a, own_v, got, wac_in, wap_in, wvc_in, wvp_in,
    keep, send, cols_a, slope_a, hid_a, gemb_a, cols_v, slope_v, hid_v, gemb_v, gpre, emb_a, emb_v, inv_a, inv_v, gacc, giacc, feats, wac, wap, wvc, wvp, sems,
):
    me = lax.axis_index("tm")
    rows_total = clips * frames
    start = me * (frames - 2 * halo) - halo if halo else 0
    first_clip = 0 if halo else me * clips
    block = block_of(frames)
    per_clip = frames // block

    copies = []

    def fetch(source, target):
        copy = pltpu.make_async_copy(source, target, sems.at[len(copies)])
        copy.start()
        copies.append(copy)
        return copy

    def fetch_feats(m, own):
        if halo:
            return [fetch(own, feats.at[m])]
        seg = own.shape[1]
        mine = pl.ds(pl.multiple_of(me * seg, seg), seg)
        other = pl.ds(pl.multiple_of((1 - me) * seg, seg), seg)
        started = []
        for c in range(clips):
            started.append(fetch(own.at[first_clip + c], feats.at[m, c, mine, :]))
            started.append(fetch(got.at[m, c], feats.at[m, c, other, :]))
        return started

    feats_v = fetch_feats(1, own_v)
    weights_v = [fetch(wvc_in, wvc), fetch(wvp_in, wvp)]
    feats_a = fetch_feats(0, own_a)
    weights_a = [fetch(wac_in, wac), fetch(wap_in, wap)]
    gacc[...] = jnp.zeros(gacc.shape, F32)
    giacc[...] = jnp.zeros(giacc.shape, F32)

    for c in range(clips):
        for lo in (0, PAD + frames):
            emb_a[c, lo : lo + PAD, :] = jnp.zeros((PAD, emb_a.shape[2]), BF16)
            inv_a[c, lo : lo + PAD, :] = jnp.zeros((PAD, LANES), F32)

    def put_a(i, emb, inv):
        c = i // per_clip
        at = PAD + i % per_clip * block
        emb_a[c, pl.ds(at, block), :] = emb
        inv_a[c, pl.ds(at, block), :] = inv

    def put_v(i, emb, inv):
        at = i * block
        emb_v[pl.ds(at, block), :] = emb
        inv_v[pl.ds(at, block), :] = inv

    columns(feats, 1, feats_v, cols_v, clips, frames)
    for copy in weights_v:
        copy.wait()
    columns(feats, 0, feats_a, cols_a, clips, frames)
    for copy in weights_a:
        copy.wait()
    count = rows_total // block
    works_v = [forward(i, wvc, wvp, cols_v, slope_v, hid_v, block, put_v) for i in range(count)]
    works_a = [forward(i, wac, wap, cols_a, slope_a, hid_a, block, put_a) for i in range(count)]
    staggered(works_v + works_a)

    tiles = frames // TILE
    gang = next(n for n in (4, 2, 1) if clips * tiles % n == 0)
    row = lax.broadcasted_iota(jnp.int32, (TILE, WIN), 0)
    col = lax.broadcasted_iota(jnp.int32, (TILE, WIN), 1)
    shift = col - row - PAD
    in_band = (shift >= -SPAN) & (shift <= SPAN)
    row_1 = lax.broadcasted_iota(jnp.int32, (TILE, 1), 0)

    def tile_work(i):
        c = i // tiles
        first = pl.multiple_of(lax.rem(i, tiles) * TILE, TILE)
        length = lengths[first_clip + c]
        label = labels[first_clip + c]
        here = pl.ds(pl.multiple_of(i * TILE, TILE), TILE)
        window = pl.ds(first, WIN)
        ev = emb_v[here, :]
        wa = emb_a[c, window, :]
        dots = dot(ev, wa, NT)
        yield
        iv = inv_v[here, 0:1]
        both = iv * inv_a[c, window, :].T
        scores = (logit_sharpening_divisor * dots) * both
        yield
        t = start + first + row_1
        u = start + first - PAD + col[0:1]
        inside = (t >= 0) & (t < length)
        target = t + label
        counted = inside & (target >= 0) & (target < length)
        hit = shift == label
        weights = jnp.where(in_band & ((u >= 0) & (u < length)), jnp.exp(scores), 0.0)
        yield
        sums = jnp.where(counted, jnp.sum(weights, axis=1, keepdims=True), 1.0)
        picked = jnp.sum(jnp.where(hit, scores, 0.0), axis=1, keepdims=True)
        yield
        own = (first + row_1 >= halo) & (first + row_1 < frames - halo)
        loss = jnp.where(counted & own, jnp.log(sums) - picked, 0.0)
        scale = jnp.where(counted, logit_sharpening_divisor * loss_scale, 0.0)
        grad = (weights * (scale / sums) - jnp.where(hit, scale, 0.0)) * both
        gd = grad.astype(BF16)
        yield
        by_dots = grad * dots
        lip = dot(gd, wa, NN)
        yield
        audio = dot(gd, ev, TN)
        yield
        giv = jnp.sum(by_dots, axis=1, keepdims=True)
        gia = jnp.sum(by_dots.T, axis=1, keepdims=True)
        yield
        lip = lip - (iv * iv * giv) * ev.astype(F32)
        gemb_v[here, :] = jnp.where(own, lip, 0.0).astype(BF16)
        yield
        gacc[c, window, :] += audio
        giacc[c, window, :] += jnp.broadcast_to(gia, (WIN, LANES))
        yield loss

    def tile_step(i, loss):
        together = [tile_work(i + k * (clips * tiles // gang)) for k in range(gang)]
        last = [None]
        while last[0] is None:
            last = [next(work) for work in together]
        return loss + sum(last)

    loss = lax.fori_loop(0, clips * tiles // gang, tile_step, jnp.zeros((TILE, 1), F32), unroll=clips * tiles <= 8)
    loss = jnp.sum(loss)

    def audio_step(i, _):
        c = i // per_clip
        at = pl.ds(pl.multiple_of(PAD + lax.rem(i, per_clip) * block, PAD), block)
        inv = inv_a[c, at, 0:1]
        grad = gacc[c, at, :] - (inv * inv * giacc[c, at, 0:1]) * emb_a[c, at, :].astype(F32)
        if halo:
            at_row = lax.rem(i, per_clip) * block + lax.broadcasted_iota(jnp.int32, (block, 1), 0)
            grad = jnp.where((at_row >= halo) & (at_row < frames - halo), grad, 0.0)
        gemb_a[pl.ds(pl.multiple_of(i * block, block), block), :] = grad.astype(BF16)
        return 0

    lax.fori_loop(0, rows_total // block, audio_step, 0)

    count = jnp.zeros((), F32)
    for c in range(clips):
        count = count + (lengths[first_clip + c] - jnp.abs(labels[first_clip + c])).astype(F32)
    if halo:
        count = jnp.where(me == 0, count, 0.0)
    send_rows = send.shape[0] - TILES
    for at, value in ((send_rows, loss), (send_rows + PAD, count)):
        digits = jnp.broadcast_to(digits_of(value), (PAD, LANES))
        keep[at : at + PAD, :] = digits
        send[at : at + PAD, :] = digits.astype(BF16)

    backward(wvp, cols_v, slope_v, hid_v, gemb_v, gpre, keep, send, block)


def block_of(frames):
    return next(n for n in (512, 256, TILE) if frames % n == 0)


def audio_kernel(block, w_proj, cols, slope, hid, gemb, keep, send, gpre):
    backward(w_proj, cols, slope, hid, gemb, gpre, keep, send, block)
    for ref in (keep, send):
        ref[ref.shape[0] - TILES :, :] = jnp.zeros((TILES, LANES), ref.dtype)


def local_grads(halo, lengths, labels, own_a, own_v, got, wac, wap, wvc, wvp):
    clips, frames, chan = own_a.shape
    if not halo:
        clips, frames = clips // 2, frames * 2
    width = wap.shape[0]
    rows = clips * frames
    taps = wac.shape[0]
    grad_rows = taps * chan + width
    wac = wac.reshape(taps * chan, width)
    wvc = wvc.reshape(taps * chan, width)
    blocks = width // 2 // LANES
    smem = pl.BlockSpec(memory_space=pltpu.SMEM)
    vmem = pl.BlockSpec(memory_space=pltpu.VMEM)
    hbm = pl.BlockSpec(memory_space=pl.ANY)
    sums = [pltpu.VMEM((blocks * grad_rows + TILES, LANES), dtype) for dtype in (F32, BF16)]
    saved = [
        pltpu.VMEM((rows, taps * chan), BF16),
        pltpu.VMEM((rows, width), F32),
        pltpu.VMEM((rows, width), BF16),
        pltpu.VMEM((rows, width), BF16),
    ]
    keep_v, send_v, *audio = pl.pallas_call(
        functools.partial(kernel, frames, clips, halo),
        out_shape=sums + saved,
        in_specs=[smem, smem, hbm, hbm, vmem] + [hbm] * 4,
        out_specs=[vmem] * 6,
        scratch_shapes=saved
        + [
            pltpu.VMEM((rows, width), BF16),
            pltpu.VMEM((clips, frames + 2 * PAD, width), BF16),
            pltpu.VMEM((rows, width), BF16),
            pltpu.VMEM((clips, frames + 2 * PAD, LANES), F32),
            pltpu.VMEM((rows, LANES), F32),
            pltpu.VMEM((clips, frames + 2 * PAD, width), F32),
            pltpu.VMEM((clips, frames + 2 * PAD, LANES), F32),
            pltpu.VMEM((2, clips, frames, chan), BF16),
            pltpu.VMEM((taps * chan, width), BF16),
            pltpu.VMEM((width, width), BF16),
            pltpu.VMEM((taps * chan, width), BF16),
            pltpu.VMEM((width, width), BF16),
            pltpu.SemaphoreType.DMA((4 * clips + 4,)),
        ],
        compiler_params=pltpu.CompilerParams(vmem_limit_bytes=44 * 1024 * 1024),
    )(lengths, labels, own_a, own_v, got, wac, wap, wvc, wvp)
    keep_a, send_a = pl.pallas_call(
        functools.partial(audio_kernel, block_of(frames)),
        out_shape=sums,
        in_specs=[vmem] * 5,
        out_specs=[vmem] * 2,
        scratch_shapes=[pltpu.VMEM((rows, width), BF16)],
        compiler_params=pltpu.CompilerParams(vmem_limit_bytes=32 * 1024 * 1024),
        cost_estimate=pl.CostEstimate(flops=2 * rows * width * (grad_rows + width), bytes_accessed=12 * rows * width, transcendentals=0),
    )(wap, *audio)
    return (keep_v, keep_a), (send_v, send_a)


def swap(value, axis, bit):
    return lax.ppermute(value, axis, [(i, i ^ bit) for i in range(lax.axis_size(axis))])


def swap_by_core(value, bits):
    peers = lax.axis_size("tm")
    pairs = []
    for clip in range(lax.axis_size("clip")):
        for tm in range(peers):
            pairs.append((clip * peers + tm, (clip ^ bits[tm % 2]) * peers + tm))
    return lax.ppermute(value, ("clip", "tm"), pairs)


def pick(value, index):
    return lax.dynamic_index_in_dim(value, index, 0, keepdims=False)


def halve(value, axis, bit, tile):
    me = (lax.axis_index(axis) // bit) % 2
    parts = value.reshape(2, -1, LANES)
    got = swap(jnp.concatenate([pick(parts, 1 - me).astype(BF16), tile]), axis, bit).astype(F32)
    rows = parts.shape[1]
    return pick(parts, me).astype(F32) + got[:rows], (tile.astype(F32) + got[rows:]).astype(BF16)


def double(value, axis, bit):
    me = (lax.axis_index(axis) // bit) % 2
    got = swap(value, axis, bit)
    return jnp.stack([jnp.where(me == 0, value, got), jnp.where(me == 0, got, value)]).reshape(-1, LANES)


def place_of(bits):
    clip, odd = lax.axis_index("clip"), lax.axis_index("tm") % 2
    return jnp.where(odd == 0, (clip // bits[0]) % 4, (clip // bits[1]) % 4)


def quarter(parts, bits, tile):
    me = place_of(bits)
    rows = parts.shape[1]
    mine = pick(parts, me).astype(F32)
    whole = tile.astype(F32)
    for k in (1, 2, 3):
        out = jnp.concatenate([pick(parts, me ^ k).astype(BF16), tile])
        got = swap_by_core(out, (k * bits[0], k * bits[1])).astype(F32)
        mine = mine + got[:rows]
        whole = whole + got[rows:]
    return mine, whole.astype(BF16)


def spread(value, bits):
    return [value] + [swap_by_core(value, (k * bits[0], k * bits[1])) for k in (1, 2, 3)]


def in_order(got, bits):
    me = place_of(bits)
    out = []
    for j in range(4):
        k = me ^ j
        out.append(jnp.where(k == 0, got[0], jnp.where(k == 1, got[1], jnp.where(k == 2, got[2], got[3]))))
    return jnp.stack(out).reshape(-1, LANES)


def bits_of(axis):
    size, bits = lax.axis_size(axis), []
    bit = 1
    while bit < size:
        bits.append(bit)
        bit *= 2
    return bits


def place_in_kernel(bits):
    clip, odd = lax.axis_index("clip"), lax.rem(lax.axis_index("tm"), 2)
    return jnp.where(odd == 0, lax.rem(clip // bits[0], 4), lax.rem(clip // bits[1], 4))


def place_kernel(bits, *refs):
    me = place_in_kernel(bits)
    out = refs[-1]
    part = out.shape[0] // 4
    for k in range(4):
        out[pl.ds(pl.multiple_of((me ^ k) * part, PAD), part), :] = refs[k][...]


def place(got, bits):
    vmem = pl.BlockSpec(memory_space=pltpu.VMEM)
    return pl.pallas_call(
        functools.partial(place_kernel, bits),
        out_shape=pltpu.VMEM((4 * got[0].shape[0], LANES), got[0].dtype),
        in_specs=[vmem] * 4,
        out_specs=vmem,
        compiler_params=pltpu.CompilerParams(vmem_limit_bytes=16 * 1024 * 1024),
    )(*got)


def deal_kernel(bits, base, got, mine, *outs):
    me = place_in_kernel(bits)
    part = mine.shape[0] - TILES

    def total(rows):
        return base[rows, :] + got[rows, :].astype(F32)

    tile = total(pl.ds(4 * part, TILES))
    for k, out in enumerate((mine, *outs)):
        rows = pl.ds(pl.multiple_of((me ^ k) * part, PAD), part)
        out[0:part, :] = total(rows).astype(out.dtype)
        out[part:, :] = tile.astype(out.dtype)


def join_kernel(base, *refs):
    value = base[...]
    for ref in refs[:-1]:
        value = value + ref[...].astype(F32)
    refs[-1][...] = value.astype(BF16)


def split_kernel(one, other, *outs):
    start = 0
    for out in outs:
        rows = pl.ds(start, out.shape[0])
        out[...] = (one[rows, :].astype(F32) + other[rows, :].astype(F32)).astype(BF16)
        start += out.shape[0]


def on_chip(body, shapes, *args):
    vmem = pl.BlockSpec(memory_space=pltpu.VMEM)
    return pl.pallas_call(
        body,
        out_shape=[pltpu.VMEM((rows, LANES), dtype) for rows, dtype in shapes],
        in_specs=[vmem] * len(args),
        out_specs=[vmem] * len(shapes),
        compiler_params=pltpu.CompilerParams(vmem_limit_bytes=16 * 1024 * 1024),
    )(*args)


def reduce_all(keep, send):
    gots = [swap(value, "tm", 1) for value in send]
    rest = [("tm", bit) for bit in bits_of("tm")[1:]] + [("clip", bit) for bit in bits_of("clip")[4:]]
    rounds = ((1, 4), (4, 1))
    if rest:
        mine, tiles = [], []
        for base, got in zip(keep, gots):
            total = base + got.astype(F32)
            total, tile = total[:-TILES], total[-TILES:].astype(BF16)
            for axis, bit in rest:
                total, tile = halve(total, axis, bit, tile)
            for bits in rounds:
                total, tile = quarter(total.reshape(4, -1, LANES), bits, tile)
            total = total.astype(BF16)
            for bits in rounds[::-1]:
                total = in_order(spread(total, bits), bits)
            for axis, bit in rest[::-1]:
                total = double(total, axis, bit)
            mine.append(total)
            tiles.append(tile)
        return mine, tiles[0]
    mine, tiles = [], []
    for base, got, (groups, pairs, last_pairs) in zip(keep, gots, PLANS):
        part = (base.shape[0] - TILES) // 4 + TILES
        shapes = [(part, F32)] + [(part, BF16)] * 3
        base, *outs = on_chip(functools.partial(deal_kernel, groups), shapes, base, got)
        (value,) = on_chip(join_kernel, [(part, BF16)], base, *exchange(outs, groups))
        (value,) = on_chip(split_kernel, [(part, BF16)], value, swap_by_core(value, pairs))
        shapes = [(part - TILES, BF16)] + [(TILES, BF16)] * (not tiles)
        value, *tile = on_chip(split_kernel, shapes, value, swap_by_core(value, last_pairs))
        mine.append(value)
        tiles += tile
    return [place(spread(value, plan[0]), plan[0]) for value, plan in zip(mine, PLANS)], tiles[0]


def exchange(outs, bits):
    return [swap_by_core(out, ((k + 1) * bits[0], (k + 1) * bits[1])) for k, out in enumerate(outs)]


def finish_kernel(parts, aliased, with_loss, rows, *refs):
    staged, sems = refs[-2:]
    sums, scalars = refs[: len(parts)], refs[len(parts)]
    outs = list(refs[len(parts) + 1 + aliased : -2])
    scale = scalars[0:1, :]
    if with_loss:
        outs.pop(0)[0, 0] = scalars[8, 0]
    encoders = sorted({m for m, _ in parts})
    blocks = sums[0].shape[0] // rows
    odd = lax.rem(lax.axis_index("tm"), 2)
    copies = []
    for n, (m, own) in enumerate(parts):
        half = odd if own else 1 - odd
        where = encoders.index(m) * 2
        at = 0
        columns = pl.ds(pl.multiple_of(half * blocks * LANES, LANES), blocks * LANES)
        for out in outs[where : where + 2]:
            for row in range(0, out.shape[0], SLAB):
                here, there = pl.ds(at + row, SLAB), pl.ds(row, SLAB)
                for j in range(blocks):
                    value = sums[n][pl.ds(j * rows + at + row, SLAB), :].astype(F32) * scale
                    staged[n, here, j * LANES : (j + 1) * LANES] = value
                copy = pltpu.make_async_copy(staged.at[n, here, :], out.at[there, columns], sems.at[len(copies)])
                copy.start()
                copies.append(copy)
            at += out.shape[0]
    for copy in copies:
        copy.wait()


def scalars_kernel(tile, out):
    digits = tile[...].astype(F32)
    count = value_of(digits[PAD : PAD + 1])
    out[0:8, :] = jnp.broadcast_to(1.0 / count, (8, LANES))
    out[8:16, :] = jnp.broadcast_to(value_of(digits[0:1]) / count, (8, LANES))


def finish_some(parts, sums, scalars, earlier, with_loss, conv_rows, width):
    smem, vmem, hbm = (pl.BlockSpec(memory_space=space) for space in (pltpu.SMEM, pltpu.VMEM, pl.ANY))
    encoders = sorted({m for m, _ in parts})
    grads = [jax.ShapeDtypeStruct((n, width), F32) for n in (conv_rows, width) * len(encoders)]
    known = [(m, array) for m in encoders if m in earlier for array in earlier[m]]
    places = {(m, n): i for i, (m, n) in enumerate((m, n) for m in encoders for n in (0, 1))}
    aliases = {
        len(parts) + 1 + i: with_loss + places[m, i % 2] for i, (m, _) in enumerate(known)
    }
    rows = conv_rows + width
    height = sums[0].shape[0]
    size = height * LANES * len(parts)
    outs = pl.pallas_call(
        functools.partial(finish_kernel, parts, len(known), with_loss, rows),
        out_shape=[jax.ShapeDtypeStruct((1, 1), F32)] * with_loss + grads,
        in_specs=[vmem] * (len(parts) + 1) + [hbm] * len(known),
        out_specs=[smem] * with_loss + [hbm] * len(grads),
        scratch_shapes=[
            pltpu.VMEM((len(parts), rows, width // 2), F32),
            pltpu.SemaphoreType.DMA((len(parts) * rows // SLAB,)),
        ],
        input_output_aliases=aliases,
        compiler_params=pltpu.CompilerParams(vmem_limit_bytes=20 * 1024 * 1024),
        cost_estimate=pl.CostEstimate(flops=size, bytes_accessed=6 * size, transcendentals=0),
    )(*sums, scalars, *[array for _, array in known])
    loss, outs = outs[:with_loss], outs[with_loss:]
    for i, m in enumerate(encoders):
        earlier = {**earlier, m: outs[2 * i : 2 * i + 2]}
    return loss, earlier


def finish(halves, tile, conv_rows, width):
    gots = [swap(half, "tm", 1) for half in halves]
    sums = {(m, own): (halves if own else gots)[m] for m in (0, 1) for own in (True, False)}
    (scalars,) = on_chip(scalars_kernel, [(16, F32)], tile)
    loss, done = [], {}
    for parts in GROUPS:
        value, done = finish_some(parts, [sums[part] for part in parts], scalars, done, not loss, conv_rows, width)
        loss = loss or value
    return loss[0], [*done[0], *done[1]]


def shards(
    audio_feats, lip_feats, lengths, labels, w_audio_conv, w_audio_proj, w_lip_conv, w_lip_proj
):
    peers = lax.axis_size("tm")
    clips, frames, chan = audio_feats.shape
    halo = 0
    if peers == 2 and clips % 2 == 0:
        others = (1 - lax.axis_index("tm")) * (clips // 2)
        out = jnp.stack([lax.dynamic_slice_in_dim(x, others, clips // 2) for x in (audio_feats, lip_feats)])
        got = swap(out, "tm", 1)
    else:
        halo = HALO
        after = [(i, i + 1) for i in range(peers - 1)]
        before = [(i + 1, i) for i in range(peers - 1)]
        both = jnp.stack([audio_feats, lip_feats])
        audio_feats, lip_feats = jnp.concatenate(
            [
                lax.ppermute(both[:, :, -HALO:], "tm", after),
                both,
                lax.ppermute(both[:, :, :HALO], "tm", before),
            ],
            axis=2,
        )
        got = lengths.astype(BF16)
    keep, send = local_grads(
        halo, lengths, labels, audio_feats, lip_feats, got, w_audio_conv, w_audio_proj, w_lip_conv, w_lip_proj
    )
    halves, tile = reduce_all(keep, send)
    taps, chan, width = w_audio_conv.shape
    loss, (vc, vp, ac, ap) = finish(halves, tile, taps * chan, width)
    return (loss.reshape(()), ac.reshape(w_audio_conv.shape), ap, vc.reshape(w_lip_conv.shape), vp)


def solution(mesh):
    placed = (
        P("clip", "tm", None),
        P("clip", "tm", None),
        P("clip"),
        P("clip"),
        P(),
        P(),
        P(),
        P(),
    )
    return jax.shard_map(
        shards, mesh=mesh, in_specs=placed, out_specs=(P(), P(), P(), P(), P()), check_vma=False
    )
```

```python
import functools

import jax
import jax.numpy as jnp
from jax import lax
from jax.experimental import pallas as pl
from jax.experimental.pallas import tpu as pltpu
from jax.sharding import PartitionSpec as P

SPAN = 15
PAD = 16
TILE = 128
WIN = TILE + 2 * PAD
HALO = 64
TILES = 2 * PAD
SLAB = 256
GROUPS = (((0, True), (1, True)), ((0, False), (1, False)))
PLANS = (((1, 1), (4, 8), (8, 4)), ((1, 4), (4, 1), (8, 2)))
LANES = 128
DIGITS = 48
FRACTION = 20

logit_sharpening_divisor = 10.0
loss_scale = 1024.0
epsilon = 1e-06

BF16 = jnp.bfloat16
F32 = jnp.float32


def dot(a, b, dims):
    return lax.dot_general(a, b, (dims, ((), ())), preferred_element_type=F32)


NN = ((1,), (0,))
NT = ((1,), (1,))
TN = ((0,), (0,))


def digit_weights(shape):
    lane = lax.broadcasted_iota(jnp.int32, shape, len(shape) - 1)
    return lane, jnp.exp2((lane - FRACTION).astype(F32))


def digits_of(value):
    lane, weight = digit_weights((1, LANES))
    size = jnp.abs(value)
    bits = jnp.floor(size / weight) - 2.0 * jnp.floor(size / (2.0 * weight))
    return jnp.where(lane < DIGITS, jnp.where(value < 0, -bits, bits), 0.0)


def value_of(digits):
    lane, weight = digit_weights(digits.shape)
    return jnp.sum(jnp.where(lane < DIGITS, digits * weight, 0.0))


def columns(feats, m, copies, cols, clips, frames):
    chan = feats.shape[-1]
    for copy in copies:
        copy.wait()
    for c in range(clips):
        x = feats[m, c].astype(F32)
        row = lax.broadcasted_iota(jnp.int32, x.shape, 0)
        base = c * frames
        cols[base : base + frames, 0:chan] = jnp.where(row == 0, 0.0, pltpu.roll(x, 1, 0)).astype(BF16)
        cols[base : base + frames, chan : 2 * chan] = feats[m, c]
        cols[base : base + frames, 2 * chan : 3 * chan] = jnp.where(
            row == frames - 1, 0.0, pltpu.roll(x, frames - 1, 0)
        ).astype(BF16)


def forward(i, w_conv, w_proj, cols, slope, hid, block, put):
    rows = pl.ds(i * block, block)
    pre = dot(cols[rows, :], w_conv[...], NN)
    yield
    sigma = 0.5 * jnp.tanh(0.5 * pre) + 0.5
    hidden = (pre * sigma).astype(BF16)
    hid[rows, :] = hidden
    slope[rows, :] = sigma * (1.0 + pre * (1.0 - sigma))
    yield
    emb = dot(hidden, w_proj[...], NN).astype(BF16)
    yield
    values = emb.astype(F32)
    inv = lax.rsqrt(jnp.sum(values * values, axis=1, keepdims=True) + epsilon)
    put(i, emb, jnp.broadcast_to(inv, (block, LANES)))
    yield


def staggered(works):
    running = []
    while works or running:
        running += works[:1]
        works = works[1:]
        running = [work for work in running if next(work, running) is not running]


def backward(w_proj, cols, slope, hid, gemb, gpre, keep, send, block):
    def step(i, _):
        rows = pl.ds(pl.multiple_of(i * block, block), block)
        gpre[rows, :] = (dot(gemb[rows, :], w_proj[...], NT) * slope[rows, :]).astype(BF16)
        return 0

    lax.fori_loop(0, hid.shape[0] // block, step, 0, unroll=True)
    even = lax.rem(lax.axis_index("tm"), 2) == 0
    height = cols.shape[1] + hid.shape[1]
    start = 0
    for left, right in ((cols, gpre), (hid, gemb)):
        grad = dot(left[...], right[...], TN)
        rows, width = grad.shape[0], grad.shape[1] // 2
        mine = jnp.where(even, grad[:, :width], grad[:, width:])
        other = jnp.where(even, grad[:, width:], grad[:, :width])
        for j in range(width // LANES):
            at = j * height + start
            keep[at : at + rows, :] = mine[:, j * LANES : (j + 1) * LANES]
            send[at : at + rows, :] = other[:, j * LANES : (j + 1) * LANES].astype(BF16)
        start += rows


def kernel(
    frames, clips, halo, lengths, labels, own_a, own_v, got, wac_in, wap_in, wvc_in, wvp_in,
    keep, send, cols_a, slope_a, hid_a, gemb_a, cols_v, slope_v, hid_v, gemb_v, gpre, emb_a, emb_v, inv_a, inv_v, gacc, giacc, feats, wac, wap, wvc, wvp, sems,
):
    me = lax.axis_index("tm")
    rows_total = clips * frames
    start = me * (frames - 2 * halo) - halo if halo else 0
    first_clip = 0 if halo else me * clips
    block = block_of(frames)
    per_clip = frames // block

    copies = []

    def fetch(source, target):
        copy = pltpu.make_async_copy(source, target, sems.at[len(copies)])
        copy.start()
        copies.append(copy)
        return copy

    def fetch_feats(m, own):
        if halo:
            return [fetch(own, feats.at[m])]
        seg = own.shape[1]
        mine = pl.ds(pl.multiple_of(me * seg, seg), seg)
        other = pl.ds(pl.multiple_of((1 - me) * seg, seg), seg)
        started = []
        for c in range(clips):
            started.append(fetch(own.at[first_clip + c], feats.at[m, c, mine, :]))
            started.append(fetch(got.at[m, c], feats.at[m, c, other, :]))
        return started

    feats_v = fetch_feats(1, own_v)
    weights_v = [fetch(wvc_in, wvc), fetch(wvp_in, wvp)]
    feats_a = fetch_feats(0, own_a)
    weights_a = [fetch(wac_in, wac), fetch(wap_in, wap)]
    gacc[...] = jnp.zeros(gacc.shape, F32)
    giacc[...] = jnp.zeros(giacc.shape, F32)

    for c in range(clips):
        for lo in (0, PAD + frames):
            emb_a[c, lo : lo + PAD, :] = jnp.zeros((PAD, emb_a.shape[2]), BF16)
            inv_a[c, lo : lo + PAD, :] = jnp.zeros((PAD, LANES), F32)

    def put_a(i, emb, inv):
        c = i // per_clip
        at = PAD + i % per_clip * block
        emb_a[c, pl.ds(at, block), :] = emb
        inv_a[c, pl.ds(at, block), :] = inv

    def put_v(i, emb, inv):
        at = i * block
        emb_v[pl.ds(at, block), :] = emb
        inv_v[pl.ds(at, block), :] = inv

    columns(feats, 1, feats_v, cols_v, clips, frames)
    for copy in weights_v:
        copy.wait()
    columns(feats, 0, feats_a, cols_a, clips, frames)
    for copy in weights_a:
        copy.wait()
    count = rows_total // block
    works_v = [forward(i, wvc, wvp, cols_v, slope_v, hid_v, block, put_v) for i in range(count)]
    works_a = [forward(i, wac, wap, cols_a, slope_a, hid_a, block, put_a) for i in range(count)]
    staggered(works_v + works_a)

    tiles = frames // TILE
    gang = next(n for n in (4, 2, 1) if clips * tiles % n == 0)
    row = lax.broadcasted_iota(jnp.int32, (TILE, WIN), 0)
    col = lax.broadcasted_iota(jnp.int32, (TILE, WIN), 1)
    shift = col - row - PAD
    in_band = (shift >= -SPAN) & (shift <= SPAN)
    row_1 = lax.broadcasted_iota(jnp.int32, (TILE, 1), 0)

    def tile_work(i):
        c = i // tiles
        first = pl.multiple_of(lax.rem(i, tiles) * TILE, TILE)
        length = lengths[first_clip + c]
        label = labels[first_clip + c]
        here = pl.ds(pl.multiple_of(i * TILE, TILE), TILE)
        window = pl.ds(first, WIN)
        ev = emb_v[here, :]
        wa = emb_a[c, window, :]
        dots = dot(ev, wa, NT)
        yield
        iv = inv_v[here, 0:1]
        both = iv * inv_a[c, window, :].T
        scores = (logit_sharpening_divisor * dots) * both
        yield
        t = start + first + row_1
        u = start + first - PAD + col[0:1]
        inside = (t >= 0) & (t < length)
        target = t + label
        counted = inside & (target >= 0) & (target < length)
        hit = shift == label
        weights = jnp.where(in_band & ((u >= 0) & (u < length)), jnp.exp(scores), 0.0)
        yield
        sums = jnp.where(counted, jnp.sum(weights, axis=1, keepdims=True), 1.0)
        picked = jnp.sum(jnp.where(hit, scores, 0.0), axis=1, keepdims=True)
        yield
        own = (first + row_1 >= halo) & (first + row_1 < frames - halo)
        loss = jnp.where(counted & own, jnp.log(sums) - picked, 0.0)
        scale = jnp.where(counted, logit_sharpening_divisor * loss_scale, 0.0)
        grad = (weights * (scale / sums) - jnp.where(hit, scale, 0.0)) * both
        gd = grad.astype(BF16)
        yield
        by_dots = grad * dots
        lip = dot(gd, wa, NN)
        yield
        audio = dot(gd, ev, TN)
        yield
        giv = jnp.sum(by_dots, axis=1, keepdims=True)
        gia = jnp.sum(by_dots.T, axis=1, keepdims=True)
        yield
        lip = lip - (iv * iv * giv) * ev.astype(F32)
        gemb_v[here, :] = jnp.where(own, lip, 0.0).astype(BF16)
        yield
        gacc[c, window, :] += audio
        giacc[c, window, :] += jnp.broadcast_to(gia, (WIN, LANES))
        yield loss

    def tile_step(i, loss):
        together = [tile_work(i + k * (clips * tiles // gang)) for k in range(gang)]
        last = [None]
        while last[0] is None:
            last = [next(work) for work in together]
        return loss + sum(last)

    loss = lax.fori_loop(0, clips * tiles // gang, tile_step, jnp.zeros((TILE, 1), F32), unroll=clips * tiles <= 8)
    loss = jnp.sum(loss)

    def audio_step(i, _):
        c = i // per_clip
        at = pl.ds(pl.multiple_of(PAD + lax.rem(i, per_clip) * block, PAD), block)
        inv = inv_a[c, at, 0:1]
        grad = gacc[c, at, :] - (inv * inv * giacc[c, at, 0:1]) * emb_a[c, at, :].astype(F32)
        if halo:
            at_row = lax.rem(i, per_clip) * block + lax.broadcasted_iota(jnp.int32, (block, 1), 0)
            grad = jnp.where((at_row >= halo) & (at_row < frames - halo), grad, 0.0)
        gemb_a[pl.ds(pl.multiple_of(i * block, block), block), :] = grad.astype(BF16)
        return 0


    count = jnp.zeros((), F32)
    for c in range(clips):
        count = count + (lengths[first_clip + c] - jnp.abs(labels[first_clip + c])).astype(F32)
    if halo:
        count = jnp.where(me == 0, count, 0.0)
    send_rows = send.shape[0] - TILES
    for at, value in ((send_rows, loss), (send_rows + PAD, count)):
        digits = jnp.broadcast_to(digits_of(value), (PAD, LANES))
        keep[at : at + PAD, :] = digits
        send[at : at + PAD, :] = digits.astype(BF16)

    backward(wvp, cols_v, slope_v, hid_v, gemb_v, gpre, keep, send, block)
    lax.fori_loop(0, rows_total // block, audio_step, 0, unroll=True)


def block_of(frames):
    return next(n for n in (512, 256, TILE) if frames % n == 0)


def audio_kernel(block, w_proj, cols, slope, hid, gemb, keep, send, gpre):
    backward(w_proj, cols, slope, hid, gemb, gpre, keep, send, block)
    for ref in (keep, send):
        ref[ref.shape[0] - TILES :, :] = jnp.zeros((TILES, LANES), ref.dtype)


def local_grads(halo, lengths, labels, own_a, own_v, got, wac, wap, wvc, wvp):
    clips, frames, chan = own_a.shape
    if not halo:
        clips, frames = clips // 2, frames * 2
    width = wap.shape[0]
    rows = clips * frames
    taps = wac.shape[0]
    grad_rows = taps * chan + width
    wac = wac.reshape(taps * chan, width)
    wvc = wvc.reshape(taps * chan, width)
    blocks = width // 2 // LANES
    smem = pl.BlockSpec(memory_space=pltpu.SMEM)
    vmem = pl.BlockSpec(memory_space=pltpu.VMEM)
    hbm = pl.BlockSpec(memory_space=pl.ANY)
    sums = [pltpu.VMEM((blocks * grad_rows + TILES, LANES), dtype) for dtype in (F32, BF16)]
    saved = [
        pltpu.VMEM((rows, taps * chan), BF16),
        pltpu.VMEM((rows, width), F32),
        pltpu.VMEM((rows, width), BF16),
        pltpu.VMEM((rows, width), BF16),
    ]
    keep_v, send_v, *audio = pl.pallas_call(
        functools.partial(kernel, frames, clips, halo),
        out_shape=sums + saved,
        in_specs=[smem, smem, hbm, hbm, vmem] + [hbm] * 4,
        out_specs=[vmem] * 6,
        scratch_shapes=saved
        + [
            pltpu.VMEM((rows, width), BF16),
            pltpu.VMEM((clips, frames + 2 * PAD, width), BF16),
            pltpu.VMEM((rows, width), BF16),
            pltpu.VMEM((clips, frames + 2 * PAD, LANES), F32),
            pltpu.VMEM((rows, LANES), F32),
            pltpu.VMEM((clips, frames + 2 * PAD, width), F32),
            pltpu.VMEM((clips, frames + 2 * PAD, LANES), F32),
            pltpu.VMEM((2, clips, frames, chan), BF16),
            pltpu.VMEM((taps * chan, width), BF16),
            pltpu.VMEM((width, width), BF16),
            pltpu.VMEM((taps * chan, width), BF16),
            pltpu.VMEM((width, width), BF16),
            pltpu.SemaphoreType.DMA((4 * clips + 4,)),
        ],
        compiler_params=pltpu.CompilerParams(vmem_limit_bytes=44 * 1024 * 1024),
    )(lengths, labels, own_a, own_v, got, wac, wap, wvc, wvp)
    keep_a, send_a = pl.pallas_call(
        functools.partial(audio_kernel, block_of(frames)),
        out_shape=sums,
        in_specs=[vmem] * 5,
        out_specs=[vmem] * 2,
        scratch_shapes=[pltpu.VMEM((rows, width), BF16)],
        compiler_params=pltpu.CompilerParams(vmem_limit_bytes=32 * 1024 * 1024),
        cost_estimate=pl.CostEstimate(flops=2 * rows * width * (grad_rows + width), bytes_accessed=12 * rows * width, transcendentals=0),
    )(wap, *audio)
    return (keep_v, keep_a), (send_v, send_a)


def swap(value, axis, bit):
    return lax.ppermute(value, axis, [(i, i ^ bit) for i in range(lax.axis_size(axis))])


def swap_by_core(value, bits):
    peers = lax.axis_size("tm")
    pairs = []
    for clip in range(lax.axis_size("clip")):
        for tm in range(peers):
            pairs.append((clip * peers + tm, (clip ^ bits[tm % 2]) * peers + tm))
    return lax.ppermute(value, ("clip", "tm"), pairs)


def pick(value, index):
    return lax.dynamic_index_in_dim(value, index, 0, keepdims=False)


def halve(value, axis, bit, tile):
    me = (lax.axis_index(axis) // bit) % 2
    parts = value.reshape(2, -1, LANES)
    got = swap(jnp.concatenate([pick(parts, 1 - me).astype(BF16), tile]), axis, bit).astype(F32)
    rows = parts.shape[1]
    return pick(parts, me).astype(F32) + got[:rows], (tile.astype(F32) + got[rows:]).astype(BF16)


def double(value, axis, bit):
    me = (lax.axis_index(axis) // bit) % 2
    got = swap(value, axis, bit)
    return jnp.stack([jnp.where(me == 0, value, got), jnp.where(me == 0, got, value)]).reshape(-1, LANES)


def place_of(bits):
    clip, odd = lax.axis_index("clip"), lax.axis_index("tm") % 2
    return jnp.where(odd == 0, (clip // bits[0]) % 4, (clip // bits[1]) % 4)


def quarter(parts, bits, tile):
    me = place_of(bits)
    rows = parts.shape[1]
    mine = pick(parts, me).astype(F32)
    whole = tile.astype(F32)
    for k in (1, 2, 3):
        out = jnp.concatenate([pick(parts, me ^ k).astype(BF16), tile])
        got = swap_by_core(out, (k * bits[0], k * bits[1])).astype(F32)
        mine = mine + got[:rows]
        whole = whole + got[rows:]
    return mine, whole.astype(BF16)


def spread(value, bits):
    return [value] + [swap_by_core(value, (k * bits[0], k * bits[1])) for k in (1, 2, 3)]


def in_order(got, bits):
    me = place_of(bits)
    out = []
    for j in range(4):
        k = me ^ j
        out.append(jnp.where(k == 0, got[0], jnp.where(k == 1, got[1], jnp.where(k == 2, got[2], got[3]))))
    return jnp.stack(out).reshape(-1, LANES)


def bits_of(axis):
    size, bits = lax.axis_size(axis), []
    bit = 1
    while bit < size:
        bits.append(bit)
        bit *= 2
    return bits


def place_in_kernel(bits):
    clip, odd = lax.axis_index("clip"), lax.rem(lax.axis_index("tm"), 2)
    return jnp.where(odd == 0, lax.rem(clip // bits[0], 4), lax.rem(clip // bits[1], 4))


def place_kernel(bits, *refs):
    me = place_in_kernel(bits)
    out = refs[-1]
    part = out.shape[0] // 4
    for k in range(4):
        out[pl.ds(pl.multiple_of((me ^ k) * part, PAD), part), :] = refs[k][...]


def place(got, bits):
    vmem = pl.BlockSpec(memory_space=pltpu.VMEM)
    return pl.pallas_call(
        functools.partial(place_kernel, bits),
        out_shape=pltpu.VMEM((4 * got[0].shape[0], LANES), got[0].dtype),
        in_specs=[vmem] * 4,
        out_specs=vmem,
        compiler_params=pltpu.CompilerParams(vmem_limit_bytes=16 * 1024 * 1024),
    )(*got)


def deal_kernel(bits, base, got, mine, *outs):
    me = place_in_kernel(bits)
    part = mine.shape[0] - TILES

    def total(rows):
        return base[rows, :] + got[rows, :].astype(F32)

    tile = total(pl.ds(4 * part, TILES))
    for k, out in enumerate((mine, *outs)):
        rows = pl.ds(pl.multiple_of((me ^ k) * part, PAD), part)
        out[0:part, :] = total(rows).astype(out.dtype)
        out[part:, :] = tile.astype(out.dtype)


def join_kernel(base, *refs):
    value = base[...]
    for ref in refs[:-1]:
        value = value + ref[...].astype(F32)
    refs[-1][...] = value.astype(BF16)


def split_kernel(one, other, *outs):
    start = 0
    for out in outs:
        rows = pl.ds(start, out.shape[0])
        out[...] = (one[rows, :].astype(F32) + other[rows, :].astype(F32)).astype(BF16)
        start += out.shape[0]


def on_chip(body, shapes, *args):
    vmem = pl.BlockSpec(memory_space=pltpu.VMEM)
    return pl.pallas_call(
        body,
        out_shape=[pltpu.VMEM((rows, LANES), dtype) for rows, dtype in shapes],
        in_specs=[vmem] * len(args),
        out_specs=[vmem] * len(shapes),
        compiler_params=pltpu.CompilerParams(vmem_limit_bytes=16 * 1024 * 1024),
    )(*args)


def reduce_all(keep, send):
    gots = [swap(value, "tm", 1) for value in send]
    rest = [("tm", bit) for bit in bits_of("tm")[1:]] + [("clip", bit) for bit in bits_of("clip")[4:]]
    rounds = ((1, 4), (4, 1))
    if rest:
        mine, tiles = [], []
        for base, got in zip(keep, gots):
            total = base + got.astype(F32)
            total, tile = total[:-TILES], total[-TILES:].astype(BF16)
            for axis, bit in rest:
                total, tile = halve(total, axis, bit, tile)
            for bits in rounds:
                total, tile = quarter(total.reshape(4, -1, LANES), bits, tile)
            total = total.astype(BF16)
            for bits in rounds[::-1]:
                total = in_order(spread(total, bits), bits)
            for axis, bit in rest[::-1]:
                total = double(total, axis, bit)
            mine.append(total)
            tiles.append(tile)
        return mine, tiles[0]
    mine, tiles = [], []
    for base, got, (groups, pairs, last_pairs) in zip(keep, gots, PLANS):
        part = (base.shape[0] - TILES) // 4 + TILES
        shapes = [(part, F32)] + [(part, BF16)] * 3
        base, *outs = on_chip(functools.partial(deal_kernel, groups), shapes, base, got)
        (value,) = on_chip(join_kernel, [(part, BF16)], base, *exchange(outs, groups))
        (value,) = on_chip(split_kernel, [(part, BF16)], value, swap_by_core(value, pairs))
        shapes = [(part - TILES, BF16)] + [(TILES, BF16)] * (not tiles)
        value, *tile = on_chip(split_kernel, shapes, value, swap_by_core(value, last_pairs))
        mine.append(value)
        tiles += tile
    return [place(spread(value, plan[0]), plan[0]) for value, plan in zip(mine, PLANS)], tiles[0]


def exchange(outs, bits):
    return [swap_by_core(out, ((k + 1) * bits[0], (k + 1) * bits[1])) for k, out in enumerate(outs)]


def finish_kernel(parts, aliased, with_loss, rows, *refs):
    staged, sems = refs[-2:]
    sums, scalars = refs[: len(parts)], refs[len(parts)]
    outs = list(refs[len(parts) + 1 + aliased : -2])
    scale = scalars[0:1, :]
    if with_loss:
        outs.pop(0)[0, 0] = scalars[8, 0]
    encoders = sorted({m for m, _ in parts})
    blocks = sums[0].shape[0] // rows
    odd = lax.rem(lax.axis_index("tm"), 2)
    copies = []
    for n, (m, own) in enumerate(parts):
        half = odd if own else 1 - odd
        where = encoders.index(m) * 2
        at = 0
        columns = pl.ds(pl.multiple_of(half * blocks * LANES, LANES), blocks * LANES)
        for out in outs[where : where + 2]:
            for row in range(0, out.shape[0], SLAB):
                here, there = pl.ds(at + row, SLAB), pl.ds(row, SLAB)
                for j in range(blocks):
                    value = sums[n][pl.ds(j * rows + at + row, SLAB), :].astype(F32) * scale
                    staged[n, here, j * LANES : (j + 1) * LANES] = value
                copy = pltpu.make_async_copy(staged.at[n, here, :], out.at[there, columns], sems.at[len(copies)])
                copy.start()
                copies.append(copy)
            at += out.shape[0]
    for copy in copies:
        copy.wait()


def scalars_kernel(tile, out):
    digits = tile[...].astype(F32)
    count = value_of(digits[PAD : PAD + 1])
    out[0:8, :] = jnp.broadcast_to(1.0 / count, (8, LANES))
    out[8:16, :] = jnp.broadcast_to(value_of(digits[0:1]) / count, (8, LANES))


def finish_some(parts, sums, scalars, earlier, with_loss, conv_rows, width):
    smem, vmem, hbm = (pl.BlockSpec(memory_space=space) for space in (pltpu.SMEM, pltpu.VMEM, pl.ANY))
    encoders = sorted({m for m, _ in parts})
    grads = [jax.ShapeDtypeStruct((n, width), F32) for n in (conv_rows, width) * len(encoders)]
    known = [(m, array) for m in encoders if m in earlier for array in earlier[m]]
    places = {(m, n): i for i, (m, n) in enumerate((m, n) for m in encoders for n in (0, 1))}
    aliases = {
        len(parts) + 1 + i: with_loss + places[m, i % 2] for i, (m, _) in enumerate(known)
    }
    rows = conv_rows + width
    height = sums[0].shape[0]
    size = height * LANES * len(parts)
    outs = pl.pallas_call(
        functools.partial(finish_kernel, parts, len(known), with_loss, rows),
        out_shape=[jax.ShapeDtypeStruct((1, 1), F32)] * with_loss + grads,
        in_specs=[vmem] * (len(parts) + 1) + [hbm] * len(known),
        out_specs=[smem] * with_loss + [hbm] * len(grads),
        scratch_shapes=[
            pltpu.VMEM((len(parts), rows, width // 2), F32),
            pltpu.SemaphoreType.DMA((len(parts) * rows // SLAB,)),
        ],
        input_output_aliases=aliases,
        compiler_params=pltpu.CompilerParams(vmem_limit_bytes=20 * 1024 * 1024),
        cost_estimate=pl.CostEstimate(flops=size, bytes_accessed=6 * size, transcendentals=0),
    )(*sums, scalars, *[array for _, array in known])
    loss, outs = outs[:with_loss], outs[with_loss:]
    for i, m in enumerate(encoders):
        earlier = {**earlier, m: outs[2 * i : 2 * i + 2]}
    return loss, earlier


def finish(halves, tile, conv_rows, width):
    gots = [swap(half, "tm", 1) for half in halves]
    sums = {(m, own): (halves if own else gots)[m] for m in (0, 1) for own in (True, False)}
    (scalars,) = on_chip(scalars_kernel, [(16, F32)], tile)
    loss, done = [], {}
    for parts in GROUPS:
        value, done = finish_some(parts, [sums[part] for part in parts], scalars, done, not loss, conv_rows, width)
        loss = loss or value
    return loss[0], [*done[0], *done[1]]


def shards(
    audio_feats, lip_feats, lengths, labels, w_audio_conv, w_audio_proj, w_lip_conv, w_lip_proj
):
    peers = lax.axis_size("tm")
    clips, frames, chan = audio_feats.shape
    halo = 0
    if peers == 2 and clips % 2 == 0:
        others = (1 - lax.axis_index("tm")) * (clips // 2)
        out = jnp.stack([lax.dynamic_slice_in_dim(x, others, clips // 2) for x in (audio_feats, lip_feats)])
        got = swap(out, "tm", 1)
    else:
        halo = HALO
        after = [(i, i + 1) for i in range(peers - 1)]
        before = [(i + 1, i) for i in range(peers - 1)]
        both = jnp.stack([audio_feats, lip_feats])
        audio_feats, lip_feats = jnp.concatenate(
            [
                lax.ppermute(both[:, :, -HALO:], "tm", after),
                both,
                lax.ppermute(both[:, :, :HALO], "tm", before),
            ],
            axis=2,
        )
        got = lengths.astype(BF16)
    keep, send = local_grads(
        halo, lengths, labels, audio_feats, lip_feats, got, w_audio_conv, w_audio_proj, w_lip_conv, w_lip_proj
    )
    halves, tile = reduce_all(keep, send)
    taps, chan, width = w_audio_conv.shape
    loss, (vc, vp, ac, ap) = finish(halves, tile, taps * chan, width)
    return (loss.reshape(()), ac.reshape(w_audio_conv.shape), ap, vc.reshape(w_lip_conv.shape), vp)


def solution(mesh):
    placed = (
        P("clip", "tm", None),
        P("clip", "tm", None),
        P("clip"),
        P("clip"),
        P(),
        P(),
        P(),
        P(),
    )
    return jax.shard_map(
        shards, mesh=mesh, in_specs=placed, out_specs=(P(), P(), P(), P(), P()), check_vma=False
    )
```
